32 devices in a mesh: wide: 8 (over z, x), rep: 4 (over y, core).
Axes of the slice: x: 2, y: 2, z: 4, core: 2. Of those that a mesh axis runs over, the one named last changes fastest.
Arguments:
- tokens: bfloat16 [64, 64, 64, 512], P('rep', 'wide'), may hold values from -8 to 8
- cotangent: float32 [64, 64, 64, 512], P('rep', 'wide'), may hold values from -6 to 6
- norm_gain: float32 [2, 2, 512], replicated, may hold values from 0.5 to 1.5
- norm_shift: float32 [2, 2, 512], replicated, may hold values from -1.75 to 1.75
- mix_in: bfloat16 [2, 512, 128], replicated, may hold values from -0.5 to 0.5
- mix_in_bias: float32 [2, 8, 128], replicated, may hold values from -1.75 to 1.75
- mix_out: bfloat16 [2, 512, 128], replicated, may hold values from -0.5 to 0.5
- mix_out_bias: float32 [2, 8, 128], replicated, may hold values from -1.75 to 1.75
- w_in: bfloat16 [2, 512, 2048], replicated, may hold values from -0.25 to 0.25
- b_in: float32 [2, 2048], replicated, may hold values from -1.75 to 1.75
- w_out: bfloat16 [2, 2048, 512], replicated, may hold values from -0.125 to 0.125
- b_out: float32 [2, 512], replicated, may hold values from -1.75 to 1.75
Outputs:
- output_field: float32 [64, 64, 64, 512], P('rep', 'wide')
- input_grad: float32 [64, 64, 64, 512], P('rep', 'wide')
- gain_grad: float32 [2, 2, 512], replicated
- shift_grad: float32 [2, 2, 512], replicated
- mix_in_grad: float32 [2, 512, 128], P(None, 'wide')
- mix_in_bias_grad: float32 [2, 8, 128], replicated
- mix_out_grad: float32 [2, 512, 128], P(None, 'wide')
- mix_out_bias_grad: float32 [2, 8, 128], replicated
- w_in_grad: float32 [2, 512, 2048], P(None, 'wide')
- b_in_grad: float32 [2, 2048], replicated
- w_out_grad: float32 [2, 2048, 512], P(None, None, 'wide')
- b_out_grad: float32 [2, 512], replicated
The draws below stay inside these ranges and needn't reach their ends.
All inputs are finite; a program needn't handle non-finite values.
Results may differ from the reference program's by a relative error of at most 0.035.
Values may be sent and summed in bfloat16 or wider, within the bound.
No kernel may reach another device: no remote copies, remote signals or barrier semaphores. Data moves between devices by JAX's collectives and lax.ppermute only.
A program may use at most 704 MiB of HBM per device.

```python
import math
import jax
import jax.numpy as jnp
from jax import lax

D = 512
NB = 8
BS = 64
FF = 2048
KW = 32
KH = 32
H = 64
W = 64
LAYERS = 2
ITEMS = 64


def spiked(entries, own_key, source, target, parts, factor):
    def block_of(axis_at):
        return (jnp.arange(entries.shape[axis_at]) // (entries.shape[axis_at] // parts)).reshape((-1,) + (1,) * (entries.ndim - 1 - axis_at))

    near = jax.random.permutation(own_key, parts)[block_of(target)]
    far = (block_of(target) + parts // 2) % parts
    return jnp.where((block_of(source) == near) | (block_of(source) == far), factor * entries, entries)


def levels(rng, dims, split, least, top_value):
    level, own = 1.0, jax.random.fold_in(rng, 6)
    for position, shards_of in split:
        heights = jnp.exp(jax.random.uniform(jax.random.fold_in(own, position), (shards_of,), jnp.float32, least / len(split), top_value / len(split)))
        level = level * jnp.repeat(heights, dims[position] // shards_of).reshape([-1 if axis == position else 1 for axis in range(len(dims))])
    return level


def bell_draw(rng, dims, scale, limit, cuts=(), kind=jnp.bfloat16):
    array = jax.random.normal(rng, dims, jnp.float32) * scale
    if len(cuts) > 0:
        array = levels(rng, dims, cuts, -0.22, 0.18) * array
    return jnp.clip(array, min=-limit, max=limit).astype(kind)


def gaussian_with(key, shape, scale, bound, shards, heavy, held_as=jnp.bfloat16):
    drawn = scale * jax.random.normal(key, shape, jnp.float32)
    if shards:
        drawn = drawn * levels(key, shape, shards, -0.22, 0.18)
    return jnp.clip(spiked(drawn, jax.random.fold_in(key, 3), *heavy), -bound, bound).astype(held_as)


def setup_inputs(seed: int = 0) -> dict:
    seeds = jax.random.split(jax.random.key(seed), 13)
    tokens = bell_draw(seeds[0], (ITEMS, H, W, D), 1.0, 8.0, ((0, 4), (1, 8)))
    cotangent = gaussian_with(seeds[1], (ITEMS, H, W, D), 1.0, 6.0, ((0, 4), (1, 8)), (1, 3, 8, 2.0), jnp.float32)
    norm_gain = jnp.clip(1.0 + 0.1 * jax.random.normal(seeds[2], (LAYERS, 2, D), jnp.float32), 0.5, 1.5)
    norm_shift = bell_draw(seeds[3], (LAYERS, 2, D), 0.3, 1.75, (), jnp.float32)
    mix_in = bell_draw(seeds[4], (LAYERS, D, 2 * BS), (2 * BS) ** -0.5, 0.5)
    mix_in_bias = bell_draw(seeds[5], (LAYERS, NB, 2 * BS), 0.3, 1.75, (), jnp.float32)
    mix_out = bell_draw(seeds[6], (LAYERS, D, 2 * BS), (2 * BS) ** -0.5, 0.5)
    mix_out_bias = bell_draw(seeds[7], (LAYERS, NB, 2 * BS), 0.3, 1.75, (), jnp.float32)
    w_in = bell_draw(seeds[8], (LAYERS, D, FF), D ** -0.5, 0.25)
    b_in = bell_draw(seeds[9], (LAYERS, FF), 0.3, 1.75, (), jnp.float32)
    w_out = bell_draw(seeds[10], (LAYERS, FF, D), FF ** -0.5, 0.125)
    b_out = bell_draw(seeds[11], (LAYERS, D), 0.3, 1.75, (), jnp.float32)
    return {"tokens": tokens, "cotangent": cotangent, "norm_gain": norm_gain, "norm_shift": norm_shift, "mix_in": mix_in, "mix_in_bias": mix_in_bias, "mix_out": mix_out, "mix_out_bias": mix_out_bias, "w_in": w_in, "b_in": b_in, "w_out": w_out, "b_out": b_out}


EPSILON = 1e-05
THRESHOLD = 0.1
HIGHEST = lax.Precision.HIGHEST

@jax.custom_vjp
def low(v):
    return lax.optimization_barrier(v.astype(jnp.bfloat16)).astype(jnp.float32)

@jax.custom_vjp
def low_back(v):
    return v

def low_keep(v):
    return (low(v), None)

def low_pass(kept, grad):
    return (grad,)

def back_keep(v):
    return (v, None)

def back_low(kept, grad):
    return (low(grad),)
low.defvjp(low_keep, low_pass)
low_back.defvjp(back_keep, back_low)

def dft_tables():
    col_index = jnp.arange(W, dtype=jnp.int32)
    col_freq = jnp.arange(KW, dtype=jnp.int32)
    col_phase = (col_index[:, None] * col_freq[None, :] % W).astype(jnp.float32) * (2.0 * math.pi / W)
    col_scale = 1.0 / math.sqrt(W)
    forward_cols = jnp.stack([jnp.cos(col_phase), -jnp.sin(col_phase)], axis=1) * col_scale
    doubling = jnp.where(col_freq == 0, 1.0, 2.0).astype(jnp.float32)
    inverse_cols = jnp.stack([jnp.cos(col_phase).T * doubling[:, None], -jnp.sin(col_phase).T * doubling[:, None]], axis=0) * col_scale
    row_index = jnp.arange(H, dtype=jnp.int32)
    mode_index = jnp.arange(KH, dtype=jnp.int32)
    row_freq = jnp.where(mode_index < KH // 2, mode_index, H - KH + mode_index)
    row_phase = (row_freq[:, None] * row_index[None, :] % H).astype(jnp.float32) * (2.0 * math.pi / H)
    cosine = jnp.cos(row_phase) / math.sqrt(H)
    sine = jnp.sin(row_phase) / math.sqrt(H)
    forward_rows = jnp.stack([jnp.stack([cosine, sine], -1), jnp.stack([-sine, cosine], -1)], 1)
    inverse_rows = jnp.stack([jnp.stack([cosine.T, -sine.T], -1), jnp.stack([sine.T, cosine.T], -1)], 1)
    return (forward_cols, inverse_cols, forward_rows, inverse_rows)

def layer_norm(values, gain_row, shift_row):
    center = values - lax.optimization_barrier(jnp.mean(values, axis=-1, keepdims=True))
    spread = lax.optimization_barrier(jnp.mean(center * center, axis=-1, keepdims=True))
    return center * lax.rsqrt(spread + EPSILON) * gain_row + shift_row

def mix_layer(spectra, weight, bias):
    weight_four = weight.reshape(NB, BS, 2, BS)
    real_weight = weight_four[:, :, 0]
    imag_weight = weight_four[:, :, 1]
    bias_three = bias.reshape(NB, 2, BS)
    real_in = spectra[:, :, :, 0]
    imag_in = spectra[:, :, :, 1]
    real_out = jnp.einsum('njkcb,cbe->njkce', real_in, real_weight, precision=HIGHEST) - jnp.einsum('njkcb,cbe->njkce', imag_in, imag_weight, precision=HIGHEST) + bias_three[:, 0]
    imag_out = jnp.einsum('njkcb,cbe->njkce', real_in, imag_weight, precision=HIGHEST) + jnp.einsum('njkcb,cbe->njkce', imag_in, real_weight, precision=HIGHEST) + bias_three[:, 1]
    return jnp.stack([real_out, imag_out], axis=3)

def one_layer(current, tables, params):
    forward_cols, inverse_cols, forward_rows, inverse_rows = tables
    gains, shifts, mixing_in, mixing_in_bias, mixing_out, mixing_out_bias, proj_in, bias_in, proj_out, bias_out = params
    batch_count = current.shape[0]
    normed = layer_norm(current, gains[0], shifts[0])
    spectra = low_back(low(jnp.einsum('nhwd,wpk->nhkpd', low(normed), forward_cols, precision=HIGHEST)))
    spectra = spectra.reshape(batch_count, H, KW, 2, NB, BS)
    row_spec = low_back(low(jnp.einsum('jphq,nhkqcb->njkpcb', forward_rows, spectra, precision=HIGHEST)))
    first_pre = low_back(mix_layer(row_spec, mixing_in, mixing_in_bias))
    active = low(jax.nn.gelu(first_pre, approximate=True))
    second = low_back(mix_layer(active, mixing_out, mixing_out_bias))
    shrunk = low(second - THRESHOLD * jnp.tanh(second / THRESHOLD))
    back_rows = low_back(low(jnp.einsum('hpjq,njkqcb->nhkpcb', inverse_rows, shrunk, precision=HIGHEST)))
    filtered = jnp.einsum('pkw,nhkpcb->nhwcb', inverse_cols, back_rows, precision=HIGHEST)
    filtered = low_back(filtered.reshape(batch_count, H, W, D))
    middle = current + filtered + normed
    lowered = low(layer_norm(middle, gains[1], shifts[1]))
    hidden_pre = low_back(jnp.einsum('nhwd,df->nhwf', lowered, proj_in, precision=HIGHEST) + bias_in)
    hidden_act = low(jax.nn.gelu(hidden_pre, approximate=True))
    branch = low_back(jnp.einsum('nhwf,fd->nhwd', hidden_act, proj_out, precision=HIGHEST) + bias_out)
    return middle + branch

def reference(tokens, cotangent, norm_gain, norm_shift, mix_in, mix_in_bias, mix_out, mix_out_bias, w_in, b_in, w_out, b_out):
    tables = tuple((low(table_item) for table_item in dft_tables()))
    params = tuple((p_array.astype(jnp.float32) for p_array in (norm_gain, norm_shift, mix_in, mix_in_bias, mix_out, mix_out_bias, w_in, b_in, w_out, b_out)))

    def forward(weights, inputs):

        def per_item(one_item):
            current = one_item[None]
            for depth_index in range(LAYERS):
                current = one_layer(current, tables, tuple((p_array[depth_index] for p_array in weights)))
            return current[0]
        return lax.map(jax.checkpoint(per_item), inputs)
    outputs, pullback = jax.vjp(forward, params, tokens.astype(jnp.float32))
    grads, grad_in = pullback(cotangent)
    return (outputs, grad_in, grads[0], grads[1], grads[2], grads[3], grads[4], grads[5], grads[6], grads[7], grads[8], grads[9])
```

```python
import functools
import math

import jax
import jax.numpy as jnp
import ml_dtypes
import numpy as np
from jax import lax
from jax.experimental import pallas as pl
from jax.experimental.pallas import tpu as pltpu
from jax.sharding import PartitionSpec as P

D = 512
NB = 8
BS = 64
KW = 32
KH = 32
H = 64
W = 64
LAYERS = 2


EPSILON = 1e-05
THRESHOLD = 0.1
HIGHEST = lax.Precision.HIGHEST


def dft_tables():
    col_index = jnp.arange(W, dtype=jnp.int32)
    col_freq = jnp.arange(KW, dtype=jnp.int32)
    col_phase = (col_index[:, None] * col_freq[None, :] % W).astype(jnp.float32) * (
        2.0 * math.pi / W
    )
    col_scale = 1.0 / math.sqrt(W)
    forward_cols = jnp.stack([jnp.cos(col_phase), -jnp.sin(col_phase)], axis=1) * col_scale
    doubling = jnp.where(col_freq == 0, 1.0, 2.0).astype(jnp.float32)
    inverse_cols = (
        jnp.stack(
            [jnp.cos(col_phase).T * doubling[:, None], -jnp.sin(col_phase).T * doubling[:, None]],
            axis=0,
        )
        * col_scale
    )
    row_index = jnp.arange(H, dtype=jnp.int32)
    mode_index = jnp.arange(KH, dtype=jnp.int32)
    row_freq = jnp.where(mode_index < KH // 2, mode_index, H - KH + mode_index)
    row_phase = (row_freq[:, None] * row_index[None, :] % H).astype(jnp.float32) * (
        2.0 * math.pi / H
    )
    cosine = jnp.cos(row_phase) / math.sqrt(H)
    sine = jnp.sin(row_phase) / math.sqrt(H)
    forward_rows = jnp.stack([jnp.stack([cosine, sine], -1), jnp.stack([-sine, cosine], -1)], 1)
    inverse_rows = jnp.stack(
        [jnp.stack([cosine.T, -sine.T], -1), jnp.stack([sine.T, cosine.T], -1)], 1
    )
    return (forward_cols, inverse_cols, forward_rows, inverse_rows)


def layer_norm(values, gain_row, shift_row):
    center = values - jnp.mean(values, axis=-1, keepdims=True)
    spread = jnp.mean(center * center, axis=-1, keepdims=True)
    return center * lax.rsqrt(spread + EPSILON) * gain_row + shift_row


def gelu_tanh(values):
    return jax.nn.gelu(values, approximate=True)


def shrink(values):
    return values - THRESHOLD * jnp.tanh(values / THRESHOLD)


def block_matrix(weights, onehot_low):
    picked = jnp.einsum(
        "ac,cbd->abd",
        onehot_low,
        weights.reshape(NB, BS, 2 * BS),
        preferred_element_type=jnp.float32,
    ).astype(jnp.bfloat16)
    real_part = picked[:, :, :BS]
    imag_part = picked[:, :, BS:]
    upper = jnp.concatenate([real_part, imag_part], -1)
    lower = jnp.concatenate([-imag_part, real_part], -1)
    return jnp.concatenate([upper, lower], 1)


def mode_forward(arriving, forward_rows, mixing):
    first_big, first_bias, second_big, second_bias = mixing
    item_count, pair_count = (arriving.shape[0], arriving.shape[1])
    halves = arriving.reshape(item_count, pair_count, H, 2, BS)
    mode_data = jnp.einsum(
        "jphq,iahqb->iajpb", forward_rows, halves, preferred_element_type=jnp.float32
    )
    mode_data = mode_data.reshape(item_count, pair_count, KH, 2 * BS).astype(jnp.bfloat16)
    first_pre = (
        jnp.einsum("iakc,acd->iakd", mode_data, first_big, preferred_element_type=jnp.float32)
        + first_bias[None, :, None, :]
    )
    active = gelu_tanh(first_pre).astype(jnp.bfloat16)
    second = (
        jnp.einsum("iakc,acd->iakd", active, second_big, preferred_element_type=jnp.float32)
        + second_bias[None, :, None, :]
    )
    return (mode_data, first_pre, active, second)


def mode_inverse(second, inverse_rows):
    item_count, pair_count = (second.shape[0], second.shape[1])
    shrunk = shrink(second).astype(jnp.bfloat16).reshape(item_count, pair_count, KH, 2, BS)
    rows_out = jnp.einsum(
        "hpjq,iajqb->iahpb", inverse_rows, shrunk, preferred_element_type=jnp.float32
    )
    return rows_out.reshape(item_count, pair_count, H, 2 * BS).astype(jnp.bfloat16)


def mode_backward(first_pre, second, arrived, forward_rows, inverse_rows, mixing):
    first_big, first_bias, second_big, second_bias = mixing
    item_count, pair_count = (arrived.shape[0], arrived.shape[1])
    halves = arrived.reshape(item_count, pair_count, H, 2, BS)
    d_shrunk = jnp.einsum(
        "hpjq,iahpb->iajqb", inverse_rows, halves, preferred_element_type=jnp.float32
    )
    d_shrunk = d_shrunk.reshape(item_count, pair_count, KH, 2 * BS)
    unused, shrink_pull = jax.vjp(shrink, second)
    d_second = shrink_pull(d_shrunk)[0].astype(jnp.bfloat16)
    d_active = jnp.einsum(
        "iakd,acd->iakc", d_second, second_big, preferred_element_type=jnp.float32
    )
    unused, gelu_pull = jax.vjp(gelu_tanh, first_pre)
    d_first = gelu_pull(d_active)[0].astype(jnp.bfloat16)
    d_modes = jnp.einsum(
        "iakd,acd->iakc", d_first, first_big, preferred_element_type=jnp.float32
    ).astype(jnp.bfloat16)
    d_halves = d_modes.reshape(item_count, pair_count, KH, 2, BS)
    d_rows = jnp.einsum(
        "jphq,iajpb->iahqb", forward_rows, d_halves, preferred_element_type=jnp.float32
    )
    return (
        d_rows.reshape(item_count, pair_count, H, 2 * BS).astype(jnp.bfloat16),
        d_first,
        d_second,
    )


def block_grads(inputs, grads, onehot_full):
    product = jnp.einsum("iakc,iakd->acd", inputs, grads, preferred_element_type=jnp.float32)
    real_grad = product[:, :BS, :BS] + product[:, BS:, BS:]
    imag_grad = product[:, :BS, BS:] - product[:, BS:, :BS]
    pair_grad = jnp.concatenate([real_grad, imag_grad], -1)
    weight_grad = jnp.einsum("ac,abd->cbd", onehot_full, pair_grad, precision=HIGHEST).reshape(
        D, 2 * BS
    )
    bias_terms = jnp.sum(grads.astype(jnp.float32), axis=(0, 2))
    bias_grad = jnp.dot(onehot_full.T, bias_terms, precision=HIGHEST)
    return (weight_grad, bias_grad)


def body(
    tokens,
    cotangent,
    norm_gain,
    norm_shift,
    mix_in,
    mix_in_bias,
    mix_out,
    mix_out_bias,
    w_in,
    b_in,
    w_out,
    b_out,
):
    forward_cols, inverse_cols, forward_rows, inverse_rows = [
        table_item.astype(jnp.bfloat16) for table_item in dft_tables()
    ]
    devices = lax.axis_size("wide")
    per_device = NB * KW // devices
    global_pair = lax.axis_index("wide") * per_device + jnp.arange(per_device, dtype=jnp.int32)
    onehot_full = (global_pair[:, None] // KW == jnp.arange(NB, dtype=jnp.int32)[None, :]).astype(
        jnp.float32
    )
    onehot_low = onehot_full.astype(jnp.bfloat16)
    item_count, rows_dev = (tokens.shape[0], tokens.shape[1])
    current = tokens.astype(jnp.float32)
    stored = []
    for depth_index in range(LAYERS):
        mixing = (
            block_matrix(mix_in[depth_index], onehot_low),
            jnp.dot(onehot_full, mix_in_bias[depth_index], precision=HIGHEST),
            block_matrix(mix_out[depth_index], onehot_low),
            jnp.dot(onehot_full, mix_out_bias[depth_index], precision=HIGHEST),
        )
        normed = layer_norm(current, norm_gain[depth_index, 0], norm_shift[depth_index, 0])
        spectra = jnp.einsum(
            "irwcb,wpk->ickrpb",
            normed.astype(jnp.bfloat16).reshape(item_count, rows_dev, W, NB, BS),
            forward_cols,
            preferred_element_type=jnp.float32,
        )
        spectra = spectra.reshape(item_count, NB * KW, rows_dev, 2 * BS).astype(jnp.bfloat16)
        forward_mode_data, first_pre, forward_active, second = mode_forward(
            lax.all_to_all(spectra, "wide", split_axis=1, concat_axis=2, tiled=True),
            forward_rows,
            mixing,
        )
        returning = lax.all_to_all(
            mode_inverse(second, inverse_rows), "wide", split_axis=2, concat_axis=1, tiled=True
        )
        returned = (returning,)
        back_rows = returned[0].reshape(item_count, NB, KW, rows_dev, 2, BS)
        filtered = jnp.einsum(
            "pkw,ickrpb->irwcb", inverse_cols, back_rows, preferred_element_type=jnp.float32
        )
        middle = current + filtered.reshape(item_count, rows_dev, W, D) + normed
        lowered = layer_norm(middle, norm_gain[depth_index, 1], norm_shift[depth_index, 1]).astype(
            jnp.bfloat16
        )
        hidden_pre = (
            jnp.einsum(
                "irwd,df->irwf", lowered, w_in[depth_index], preferred_element_type=jnp.float32
            )
            + b_in[depth_index]
        )
        hidden_act = gelu_tanh(hidden_pre).astype(jnp.bfloat16)
        branch = (
            jnp.einsum(
                "irwf,fd->irwd", hidden_act, w_out[depth_index], preferred_element_type=jnp.float32
            )
            + b_out[depth_index]
        )
        stored.append(
            (
                current,
                normed,
                spectra,
                middle,
                lowered,
                hidden_pre,
                hidden_act,
                mixing,
                returned[1:],
            )
        )
        current = middle + branch
    upstream = cotangent
    collected = [None] * LAYERS
    for depth_index in reversed(range(LAYERS)):
        (
            layer_input,
            normed,
            spectra,
            middle,
            lowered,
            hidden_pre,
            hidden_act,
            mixing,
            kept_modes,
        ) = stored[depth_index]
        branch_grad = upstream.astype(jnp.bfloat16)
        w_out_part = jnp.einsum(
            "irwf,irwd->fd", hidden_act, branch_grad, preferred_element_type=jnp.float32
        )
        b_out_part = jnp.sum(branch_grad.astype(jnp.float32), axis=(0, 1, 2))
        act_grad = jnp.einsum(
            "irwd,fd->irwf", branch_grad, w_out[depth_index], preferred_element_type=jnp.float32
        )
        unused, gelu_pull = jax.vjp(gelu_tanh, hidden_pre)
        pre_grad = gelu_pull(act_grad)[0].astype(jnp.bfloat16)
        w_in_part = jnp.einsum(
            "irwd,irwf->df", lowered, pre_grad, preferred_element_type=jnp.float32
        )
        b_in_part = jnp.sum(pre_grad.astype(jnp.float32), axis=(0, 1, 2))
        low_grad = jnp.einsum(
            "irwf,df->irwd", pre_grad, w_in[depth_index], preferred_element_type=jnp.float32
        )
        unused, second_norm_pull = jax.vjp(
            layer_norm, middle, norm_gain[depth_index, 1], norm_shift[depth_index, 1]
        )
        mid_norm_grad, gain_second, shift_second = second_norm_pull(low_grad)
        mid_grad = upstream + mid_norm_grad
        filt_grad = mid_grad.astype(jnp.bfloat16).reshape(item_count, rows_dev, W, NB, BS)
        back_grad = jnp.einsum(
            "pkw,irwcb->ickrpb", inverse_cols, filt_grad, preferred_element_type=jnp.float32
        )
        back_grad = back_grad.reshape(item_count, NB * KW, rows_dev, 2 * BS).astype(jnp.bfloat16)
        backward_arriving = lax.all_to_all(spectra, "wide", split_axis=1, concat_axis=2, tiled=True)
        arrived = lax.all_to_all(back_grad, "wide", split_axis=1, concat_axis=2, tiled=True)
        backward_mode_data, backward_first_pre, backward_active, backward_second = mode_forward(
            backward_arriving, forward_rows, mixing
        )
        d_rows, d_first, d_second = mode_backward(
            backward_first_pre, backward_second, arrived, forward_rows, inverse_rows, mixing
        )
        sent_back = lax.all_to_all(d_rows, "wide", split_axis=2, concat_axis=1, tiled=True)
        col_grad, mode_data, active, d_first, d_second = (
            sent_back,
            backward_mode_data,
            backward_active,
            d_first,
            d_second,
        )
        mix_in_part, mix_in_bias_part = block_grads(mode_data, d_first, onehot_full)
        mix_out_part, mix_out_bias_part = block_grads(active, d_second, onehot_full)
        col_grad = col_grad.reshape(item_count, NB, KW, rows_dev, 2, BS)
        normed_grad = jnp.einsum(
            "wpk,ickrpb->irwcb", forward_cols, col_grad, preferred_element_type=jnp.float32
        )
        normed_grad = normed_grad.reshape(item_count, rows_dev, W, D) + mid_grad
        unused, first_norm_pull = jax.vjp(
            layer_norm, layer_input, norm_gain[depth_index, 0], norm_shift[depth_index, 0]
        )
        input_part, gain_first, shift_first = first_norm_pull(normed_grad)
        upstream = mid_grad + input_part
        collected[depth_index] = (
            jnp.stack([gain_first, gain_second]),
            jnp.stack([shift_first, shift_second]),
            mix_in_part,
            mix_in_bias_part,
            mix_out_part,
            mix_out_bias_part,
            w_in_part,
            b_in_part,
            w_out_part,
            b_out_part,
        )
    stacked = [
        jnp.stack([collected[depth_index][slot] for depth_index in range(LAYERS)])
        for slot in range(10)
    ]
    small_grads = lax.psum(
        (stacked[0], stacked[1], stacked[3], stacked[5], stacked[7], stacked[9]), ("wide", "rep")
    )
    large_grads = (stacked[2], stacked[4], stacked[6], stacked[8])
    pieces = (
        lax.psum_scatter(large_grads[0], "wide", scatter_dimension=1, tiled=True),
        lax.psum_scatter(large_grads[1], "wide", scatter_dimension=1, tiled=True),
        lax.psum_scatter(large_grads[2], "wide", scatter_dimension=1, tiled=True),
        lax.psum_scatter(large_grads[3], "wide", scatter_dimension=2, tiled=True),
    )
    pieces = (
        lax.psum(pieces[0].astype(jnp.bfloat16), "rep").astype(jnp.float32),
        lax.psum(pieces[1].astype(jnp.bfloat16), "rep").astype(jnp.float32),
        lax.psum(pieces[2].astype(jnp.bfloat16), "rep").astype(jnp.float32),
        lax.psum(pieces[3].astype(jnp.bfloat16), "rep").astype(jnp.float32),
    )
    return (
        current,
        upstream,
        small_grads[0],
        small_grads[1],
        pieces[0],
        small_grads[2],
        pieces[1],
        small_grads[3],
        pieces[2],
        small_grads[4],
        pieces[3],
        small_grads[5],
    )


BF = jnp.bfloat16
F32 = jnp.float32
FF = 2048
GROUPS = 4
GELU_A = math.sqrt(2.0 / math.pi)
GELU_B = GELU_A * 0.044715
HB = 16
KB = 8
TT = 512
FC = 512
VMEM = 58 * 1024 * 1024


def plain_tables():
    def low(table):
        return table.astype(np.float32).astype(ml_dtypes.bfloat16).astype(np.float64)

    index = np.arange(64)
    col_phase = 2.0 * np.pi * ((index[:, None] * np.arange(KW)[None, :]) % W) / W
    forward_cols = np.stack([np.cos(col_phase), -np.sin(col_phase)], axis=1) / math.sqrt(W)
    doubling = np.where(np.arange(KW) == 0, 1.0, 2.0)[:, None]
    inverse_cols = (
        np.stack([np.cos(col_phase).T * doubling, -np.sin(col_phase).T * doubling], axis=0)
        / math.sqrt(W)
    )
    modes = np.arange(KH)
    row_freq = np.where(modes < KH // 2, modes, H - KH + modes)
    row_phase = 2.0 * np.pi * ((row_freq[:, None] * index[None, :]) % H) / H
    cosine = np.cos(row_phase) / math.sqrt(H)
    sine = np.sin(row_phase) / math.sqrt(H)
    forward_rows = np.stack([np.stack([cosine, sine], -1), np.stack([-sine, cosine], -1)], 1)
    inverse_rows = np.stack(
        [np.stack([cosine.T, -sine.T], -1), np.stack([sine.T, cosine.T], -1)], 1
    )
    return [low(table) for table in (forward_cols, inverse_cols, forward_rows, inverse_rows)]


def matrix_tables():
    forward_cols, inverse_cols, forward_rows, inverse_rows = plain_tables()
    eye = np.eye(8)
    into = np.einsum("wpk,gh->kpghw", forward_cols, eye).reshape(512, 512)
    outof = np.einsum("pkw,gh->gwkph", inverse_cols, eye).reshape(512, 512)
    pair = np.eye(2)
    rows_in = np.einsum("jphq,ab->apjbqh", forward_rows, pair).reshape(128, 256)
    rows_out = np.einsum("hpjq,ab->aphbqj", inverse_rows, pair).reshape(256, 128)
    return [
        jnp.asarray(np.ascontiguousarray(table).astype(ml_dtypes.bfloat16))
        for table in (into, outof, rows_in, rows_out, outof.T, into.T, rows_out.T, rows_in.T)
    ]


def big_matrices(weight):
    four = weight.reshape(GROUPS, 2, BS, 2, BS)
    eye = jnp.eye(2, dtype=weight.dtype)
    real = (four[:, :, :, 0][:, :, :, None, :] * eye[None, :, None, :, None]).reshape(
        GROUPS, 128, 128
    )
    imag = (four[:, :, :, 1][:, :, :, None, :] * eye[None, :, None, :, None]).reshape(
        GROUPS, 128, 128
    )
    upper = jnp.concatenate([real, imag], -1)
    lower = jnp.concatenate([-imag, real], -1)
    return jnp.concatenate([upper, lower], 1)


def big_bias(bias):
    return bias.reshape(GROUPS, 2, 2, BS).transpose(0, 2, 1, 3).reshape(GROUPS, 1, 256)


def small_matrix(big):
    parts = big.reshape(GROUPS, 2, 2, BS, 2, 2, BS)
    kept = jnp.stack([parts[:, :, c, :, :, c] for c in range(2)], 1)
    real = kept[:, :, 0, :, 0] + kept[:, :, 1, :, 1]
    imag = kept[:, :, 0, :, 1] - kept[:, :, 1, :, 0]
    return jnp.concatenate([real, imag], -1).reshape(D, 2 * BS)


def small_bias(big):
    summed = jnp.sum(big, axis=1)
    return summed.reshape(GROUPS, 2, 2, BS).transpose(0, 2, 1, 3).reshape(NB, 2 * BS)


def mm(left, right):
    return jnp.dot(left, right, preferred_element_type=F32)


def normalize(values):
    center = values - jnp.mean(values, axis=-1, keepdims=True)
    spread = jnp.mean(center * center, axis=-1, keepdims=True)
    scale = lax.rsqrt(spread + EPSILON)
    return center * scale, scale


def normalize_back(grad, unit, scale, gain_row):
    inner = grad * gain_row
    return scale * (
        inner
        - jnp.mean(inner, axis=-1, keepdims=True)
        - unit * jnp.mean(inner * unit, axis=-1, keepdims=True)
    )


def folded(values):
    return jnp.sum(values.reshape(values.shape[0] // 8, 8, values.shape[1]), axis=0)


def gelu_of(v):
    return 0.5 * v * (1.0 + jnp.tanh(v * (GELU_A + GELU_B * (v * v))))


def gelu_and_slope(v):
    square = v * v
    bend = jnp.tanh(v * (GELU_A + GELU_B * square))
    half = 0.5 * (1.0 + bend)
    slope = half + 0.5 * v * (1.0 - bend * bend) * (GELU_A + 3.0 * GELU_B * square)
    return v * half, slope


def flat(block):
    return block.reshape(-1, block.shape[-1])


def cols_in(table, rows, store, at):
    halves = [mm(table, rows[half * 512 : (half + 1) * 512]).reshape(64, 8, D) for half in range(2)]
    store[:, pl.ds(at, HB), :] = jnp.concatenate(halves, axis=1).astype(BF)


def cols_out(table, store, at):
    block = store[:, pl.ds(at, HB), :].astype(F32)
    return jnp.concatenate(
        [
            mm(table, block[:, half * 8 : half * 8 + 8].reshape(512, D).astype(BF))
            for half in range(2)
        ],
        axis=0,
    )


def lanes_of(rows, group):
    lanes = slice(group * 128, group * 128 + 128)
    return jnp.concatenate(
        [rows[:, :32, lanes].reshape(KB * 32, 128), rows[:, 32:, lanes].reshape(KB * 32, 128)],
        axis=1,
    )


def put_lanes(store, group, values):
    lanes = slice(group * 128, group * 128 + 128)
    store[:, :32, lanes] = values[:, :128].reshape(KB, 32, 128)
    store[:, 32:, lanes] = values[:, 128:].reshape(KB, 32, 128)


def spectral_forward_kernel(
    x_ref, gain, shift, into, outof, rows_in, rows_out, w1, b1, w2, b2, mid_ref, spec_ref, cols, mixed
):
    step = pl.program_id(1)
    n_rows, n_freq = H // HB, KW // KB

    @pl.when(step < n_rows)
    def _():
        unit, _ = normalize(flat(x_ref[...]).astype(F32))
        normed = unit * gain[...] + shift[...]
        cols_in(into[...], normed.astype(BF), cols, pl.multiple_of(step * HB, HB))

    @pl.when((step >= n_rows) & (step < n_rows + n_freq))
    def _():
        first_plane = (step - n_rows) * (2 * KB)
        for two in range(KB // 2):
            planes = cols[pl.ds(first_plane + 4 * two, 4)]
            spec_ref[0, 2 * two : 2 * two + 2] = (
                mm(rows_in[...], planes.reshape(256, D)).astype(BF).reshape(2, 64, D)
            )
        modes = spec_ref[0]
        for group in range(GROUPS):
            first = mm(lanes_of(modes, group), w1[group]) + b1[group]
            second = mm(gelu_of(first).astype(BF), w2[group]) + b2[group]
            shrunk = second - THRESHOLD * jnp.tanh(second * (1.0 / THRESHOLD))
            put_lanes(mixed, group, shrunk.astype(BF))
        for two in range(KB // 2):
            planes = mixed[2 * two : 2 * two + 2].reshape(128, D)
            cols[pl.ds(first_plane + 4 * two, 4)] = (
                mm(rows_out[...], planes).astype(BF).reshape(4, 64, D)
            )

    @pl.when(step >= n_rows + n_freq)
    def _():
        block = step - n_rows - n_freq
        x = flat(x_ref[...]).astype(F32)
        unit, _ = normalize(x)
        normed = unit * gain[...] + shift[...]
        filtered = cols_out(outof[...], cols, pl.multiple_of(block * HB, HB))
        mid_ref[...] = (x + filtered + normed).astype(mid_ref.dtype).reshape(mid_ref.shape)


def spectral_backward_kernel(
    x_ref, grad_ref, spec_ref, gain, outof_t, into_t, rows_out_t, rows_in_t,
    w1, b1, w2, b2, w1_t, w2_t,
    new_ref, dw1, db1, dw2, db2, dgain, dshift, cols, mixed, kept,
):
    step = pl.program_id(0)
    n_rows, n_freq = H // HB, KW // KB

    @pl.when(step == 0)
    def _():
        for ref in (dw1, db1, dw2, db2, dgain, dshift):
            ref[...] = jnp.zeros_like(ref)

    @pl.when(step < n_rows)
    def _():
        cols_in(outof_t[...], flat(grad_ref[...]), cols, pl.multiple_of(step * HB, HB))

    @pl.when((step >= n_rows) & (step < n_rows + n_freq))
    def _():
        first_plane = (step - n_rows) * (2 * KB)
        for two in range(KB // 2):
            planes = cols[pl.ds(first_plane + 4 * two, 4)]
            kept[2 * two : 2 * two + 2] = mm(rows_out_t[...], planes.reshape(256, D)).reshape(
                2, 64, D
            )
        modes = spec_ref[0]
        grads = kept[...]
        for group in range(GROUPS):
            mode = lanes_of(modes, group)
            first = mm(mode, w1[group]) + b1[group]
            active, slope = gelu_and_slope(first)
            active = active.astype(BF)
            second = mm(active, w2[group]) + b2[group]
            bend = jnp.tanh(second * (1.0 / THRESHOLD))
            d_second = bend * bend * lanes_of(grads, group)
            db2[group] += folded(d_second)
            d_second = d_second.astype(BF)
            dw2[group] += mm(active.T, d_second)
            d_first = slope * mm(d_second, w2_t[group])
            db1[group] += folded(d_first)
            d_first = d_first.astype(BF)
            dw1[group] += mm(mode.T, d_first)
            put_lanes(mixed, group, mm(d_first, w1_t[group]).astype(BF))
        for two in range(KB // 2):
            planes = mixed[2 * two : 2 * two + 2].reshape(128, D)
            cols[pl.ds(first_plane + 4 * two, 4)] = (
                mm(rows_in_t[...], planes).astype(BF).reshape(4, 64, D)
            )

    @pl.when(step >= n_rows + n_freq)
    def _():
        block = step - n_rows - n_freq
        unit, scale = normalize(flat(x_ref[...]).astype(F32))
        mid_grad = flat(grad_ref[...]).astype(F32)
        grad = cols_out(into_t[...], cols, pl.multiple_of(block * HB, HB)) + mid_grad
        dgain[...] += folded(grad * unit)
        dshift[...] += folded(grad)
        new = mid_grad + normalize_back(grad, unit, scale, gain[...])
        new_ref[...] = new.astype(new_ref.dtype).reshape(new_ref.shape)


def feed_forward_kernel(mid_ref, gain, shift, w_in, b_in, w_out, b_out, out_ref, pre_ref):
    middle = flat(mid_ref[...]).astype(F32)
    unit, _ = normalize(middle)
    lowered = (unit * gain[...] + shift[...]).astype(BF)
    total = middle + b_out[...]
    for part in range(FF // FC):
        at = slice(part * FC, part * FC + FC)
        pre = mm(lowered, w_in[:, at]) + b_in[:, at]
        pre_ref[0, :, at] = pre.astype(BF)
        total += mm(gelu_of(pre).astype(BF), w_out[at, :])
    out_ref[...] = total.astype(out_ref.dtype).reshape(out_ref.shape)


def feed_backward_kernel(with_start, *refs):
    (g_ref, mid_ref, pre_ref, gain, shift, w_out_t, w_in_t), refs = refs[:7], refs[7:]
    if with_start:
        (start_in, start_out), refs = refs[:2], refs[2:]
    mid_grad_ref, dw_in, dw_out, db_in, db_out, dgain, dshift = refs
    step = pl.program_id(0)

    @pl.when(step == 0)
    def _():
        for ref in (db_in, db_out, dgain, dshift):
            ref[...] = jnp.zeros_like(ref)
        if with_start:
            dw_in[...] = start_in[...]
            dw_out[...] = start_out[...]
        else:
            dw_in[...] = jnp.zeros_like(dw_in)
            dw_out[...] = jnp.zeros_like(dw_out)

    upstream = flat(g_ref[...])
    unit, scale = normalize(flat(mid_ref[...]).astype(F32))
    lowered = (unit * gain[...] + shift[...]).astype(BF)
    db_out[...] += folded(upstream.astype(F32))
    upstream_t = upstream.T
    lowered_t = lowered.T
    low_grad = jnp.zeros((TT, D), F32)
    for part in range(FF // FC):
        at = slice(part * FC, part * FC + FC)
        active, slope = gelu_and_slope(pre_ref[0, :, at].astype(F32))
        dw_out[:, at] += mm(upstream_t, active.astype(BF))
        pre_grad = slope * mm(upstream, w_out_t[:, at])
        db_in[:, at] += folded(pre_grad)
        pre_grad = pre_grad.astype(BF)
        dw_in[:, at] += mm(lowered_t, pre_grad)
        low_grad += mm(pre_grad, w_in_t[at, :])
    dgain[...] += folded(low_grad * unit)
    dshift[...] += folded(low_grad)
    new = upstream.astype(F32) + normalize_back(low_grad, unit, scale, gain[...])
    mid_grad_ref[...] = new.astype(mid_grad_ref.dtype).reshape(mid_grad_ref.shape)


def whole(array, grid_rank):
    zeros = (0,) * array.ndim
    return pl.BlockSpec(array.shape, lambda *_: zeros, pipeline_mode=pl.Buffered(1))


def rows_spec(shape, rows, item_of, block_of):
    if len(shape) == 3:
        return pl.BlockSpec((1, rows * W, D), lambda *at: (item_of(*at), block_of(*at), 0))
    own = shape[2]
    if own <= rows:
        return pl.BlockSpec(
            (rows // own, 1, own, W, D), lambda *at: (block_of(*at), item_of(*at), 0, 0, 0)
        )
    parts = own // rows
    return pl.BlockSpec(
        (1, 1, rows, W, D),
        lambda *at: (block_of(*at) // parts, item_of(*at), block_of(*at) % parts, 0, 0),
    )


def params(rank):
    return pltpu.CompilerParams(
        dimension_semantics=("arbitrary",) * rank, vmem_limit_bytes=VMEM
    )


N_ROWS, N_FREQ = H // HB, KW // KB
SPECTRAL_STEPS = 2 * N_ROWS + N_FREQ


def both_ends(step):
    return jnp.where(
        step < N_ROWS, step, jnp.where(step < N_ROWS + N_FREQ, 0, step - N_ROWS - N_FREQ)
    )


def last_end(step):
    return jnp.maximum(step - N_ROWS - N_FREQ, 0)


def middle_part(step):
    return jnp.clip(step - N_ROWS, 0, N_FREQ - 1)


def spectral_forward(x, items, gain, shift, tables, mix):
    small = (gain, shift, *tables[:4], *mix[:4])
    return pl.pallas_call(
        spectral_forward_kernel,
        grid=(items, SPECTRAL_STEPS),
        in_specs=[rows_spec(x.shape, HB, lambda i, s: i, lambda i, s: both_ends(s))]
        + [whole(array, 2) for array in small],
        out_specs=[
            pl.BlockSpec((1, HB * W, D), lambda i, s: (i, last_end(s), 0)),
            pl.BlockSpec((1, KB, 64, D), lambda i, s: (i, middle_part(s), 0, 0)),
        ],
        out_shape=[
            jax.ShapeDtypeStruct((items, H * W, D), BF),
            jax.ShapeDtypeStruct((items, KW, 64, D), BF),
        ],
        scratch_shapes=[pltpu.VMEM((64, 64, D), BF), pltpu.VMEM((KB, 64, D), BF)],
        compiler_params=params(2),
        cost_estimate=pl.CostEstimate(
            flops=items * 12_000_000_000, bytes_accessed=items * 14_000_000, transcendentals=0
        ),
        name="spectral_forward",
    )(x, *small)


def spectral_backward(x, item_x, grad, spec, item, gain, tables, mix, out_shape):
    small = (gain, *tables[4:], *mix)
    rows = functools.partial(rows_spec, rows=HB)
    sums = [(GROUPS, 256, 256), (GROUPS, 8, 256)] * 2 + [(8, D)] * 2
    return pl.pallas_call(
        spectral_backward_kernel,
        grid=(SPECTRAL_STEPS,),
        in_specs=[
            rows_spec(x.shape, HB, lambda s: item_x, both_ends),
            rows_spec(grad.shape, HB, lambda s: 0, both_ends),
            pl.BlockSpec((1, KB, 64, D), lambda s: (item, middle_part(s), 0, 0)),
        ]
        + [whole(array, 1) for array in small],
        out_specs=[rows_spec(out_shape, HB, lambda s: 0, last_end)]
        + [pl.BlockSpec(dims, lambda s, rank=len(dims): (0,) * rank) for dims in sums],
        out_shape=[jax.ShapeDtypeStruct(out_shape, BF)]
        + [jax.ShapeDtypeStruct(dims, F32) for dims in sums],
        scratch_shapes=[
            pltpu.VMEM((64, 64, D), BF),
            pltpu.VMEM((KB, 64, D), BF),
            pltpu.VMEM((KB, 64, D), F32),
        ],
        compiler_params=params(1),
        cost_estimate=pl.CostEstimate(
            flops=20_000_000_000, bytes_accessed=20_000_000, transcendentals=0
        ),
        name="spectral_backward",
    )(x, grad, spec, *small)


def feed_forward(middle, gain, shift, w_in, b_in, w_out, b_out, out_shape):
    items = middle.shape[0]
    small = (gain, shift, w_in, b_in, w_out, b_out)
    rows = TT // W
    return pl.pallas_call(
        feed_forward_kernel,
        grid=(items, H * W // TT),
        in_specs=[pl.BlockSpec((1, TT, D), lambda i, s: (i, s, 0))]
        + [whole(array, 2) for array in small],
        out_specs=[
            rows_spec(out_shape, rows, lambda i, s: i, lambda i, s: s),
            pl.BlockSpec((1, TT, FF), lambda i, s: (i, s, 0)),
        ],
        out_shape=[
            jax.ShapeDtypeStruct(out_shape, BF),
            jax.ShapeDtypeStruct((items, H * W, FF), BF),
        ],
        compiler_params=params(2),
        cost_estimate=pl.CostEstimate(
            flops=items * 20_000_000_000, bytes_accessed=items * 25_000_000, transcendentals=0
        ),
        name="feed_forward",
    )(middle, *small)


def feed_backward(g, item_g, middle, pre, item, gain, shift, w_out_t, w_in_t, start):
    small = (gain, shift, w_out_t, w_in_t) + start
    rows = TT // W
    sums = [(D, FF), (D, FF), (8, FF), (8, D), (8, D), (8, D)]
    return pl.pallas_call(
        functools.partial(feed_backward_kernel, len(start) > 0),
        grid=(H * W // TT,),
        in_specs=[
            rows_spec(g.shape, rows, lambda s: item_g, lambda s: s),
            pl.BlockSpec((1, TT, D), lambda s: (item, s, 0)),
            pl.BlockSpec((1, TT, FF), lambda s: (item, s, 0)),
        ]
        + [whole(array, 1) for array in small],
        out_specs=[pl.BlockSpec((1, TT, D), lambda s: (0, s, 0))]
        + [pl.BlockSpec(dims, lambda s: (0, 0)) for dims in sums],
        out_shape=[jax.ShapeDtypeStruct((1, H * W, D), BF)]
        + [jax.ShapeDtypeStruct(dims, F32) for dims in sums],
        compiler_params=params(1),
        cost_estimate=pl.CostEstimate(
            flops=45_000_000_000, bytes_accessed=60_000_000, transcendentals=0
        ),
        name="feed_backward",
    )(g, middle, pre, *small)


def exchange(array):
    return lax.all_to_all(array, "wide", split_axis=0, concat_axis=0, tiled=True)


def after(array, other):
    return lax.optimization_barrier((array, other))[0]


def traded(kept, sent, axis_name, bit):
    size = lax.axis_size(axis_name)
    arrived = lax.ppermute(sent.astype(BF), axis_name, [(i, i ^ (1 << bit)) for i in range(size)])
    return kept.astype(F32) + arrived.astype(F32)


def own_bit(axis_name, bit):
    return (lax.axis_index(axis_name) >> bit) & 1


def reversed_bits(value, bits):
    return sum(((value >> bit) & 1) << (bits - 1 - bit) for bit in range(bits))


def summed_shard(array):
    rep_bits = lax.axis_size("rep").bit_length() - 1
    wide_bits = lax.axis_size("wide").bit_length() - 1
    shard = array.shape[0] >> wide_bits
    for bit in range(rep_bits):
        mine, half = own_bit("rep", bit), array.shape[1] // 2
        array = traded(
            lax.dynamic_slice_in_dim(array, mine * half, half, 1),
            lax.dynamic_slice_in_dim(array, (1 - mine) * half, half, 1),
            "rep",
            bit,
        )
    columns = array.shape[1]
    for bit in range(wide_bits):
        mine = own_bit("wide", bit)
        blocks = array.reshape(-1, 2, shard, columns)
        array = traded(
            lax.dynamic_slice_in_dim(blocks, mine, 1, 1),
            lax.dynamic_slice_in_dim(blocks, 1 - mine, 1, 1),
            "wide",
            bit,
        )
    gathered = lax.all_gather(array.reshape(shard, columns).astype(BF), "rep")
    return jnp.concatenate(
        [gathered[reversed_bits(block, rep_bits)] for block in range(1 << rep_bits)], axis=1
    ).astype(F32)


def whole_items(
    tokens, cotangent, norm_gain, norm_shift, mix_in, mix_in_bias, mix_out, mix_out_bias,
    w_in, b_in, w_out, b_out,
):
    wide = lax.axis_size("wide")
    rows = tokens.shape[1]
    items = tokens.shape[0] // wide
    abroad = (wide, items, rows, W, D)
    arrived = exchange(tokens.reshape(abroad))
    upstream = exchange(after(cotangent.astype(BF).reshape(abroad), arrived))
    tables = matrix_tables()
    first_mats = [big_matrices(mix_in[layer]) for layer in range(LAYERS)]
    second_mats = [big_matrices(mix_out[layer]) for layer in range(LAYERS)]
    mixes = [
        (
            first_mats[layer],
            big_bias(mix_in_bias[layer]),
            second_mats[layer],
            big_bias(mix_out_bias[layer]),
            first_mats[layer].transpose(0, 2, 1),
            second_mats[layer].transpose(0, 2, 1),
        )
        for layer in range(LAYERS)
    ]

    def row(array, *at):
        return array[at].reshape(1, -1)

    current = arrived
    stored = []
    for layer in range(LAYERS):
        middle, spec = spectral_forward(
            current, items, row(norm_gain, layer, 0), row(norm_shift, layer, 0), tables, mixes[layer]
        )
        following, pre = feed_forward(
            middle, row(norm_gain, layer, 1), row(norm_shift, layer, 1), w_in[layer],
            row(b_in, layer), w_out[layer], row(b_out, layer),
            abroad if layer == LAYERS - 1 else (items, H * W, D),
        )
        stored.append((current, middle, spec, pre))
        current = following
    output = exchange(current).reshape(tokens.shape).astype(F32)

    sums = [None] * LAYERS
    matrices = [()] * LAYERS
    returned = []
    for item in range(items):
        grad, item_grad = upstream, item
        for layer in reversed(range(LAYERS)):
            layer_input, middle, spec, pre = stored[layer]
            mid_grad, dw_in, dw_out, *ff_sums = feed_backward(
                grad, item_grad, middle, pre, item, row(norm_gain, layer, 1),
                row(norm_shift, layer, 1), w_out[layer].T, w_in[layer].T, matrices[layer],
            )
            matrices[layer] = (dw_in, dw_out)
            grad, *mix_sums = spectral_backward(
                layer_input, item, mid_grad, spec, item, row(norm_gain, layer, 0), tables,
                mixes[layer], (1, H * W, D) if layer else (wide, 1, rows, W, D),
            )
            item_grad = 0
            own = ff_sums + mix_sums
            sums[layer] = own if item == 0 else [a + b for a, b in zip(sums[layer], own)]
        returned.append(exchange(grad))
    input_grad = jnp.concatenate(returned, axis=1).reshape(tokens.shape).astype(F32)

    shards = []
    for layer in reversed(range(LAYERS)):
        parts = list(matrices[layer])
        if layer == 0:
            for slot in (4, 6):
                parts += [small_matrix(sums[each][slot]) for each in range(LAYERS)]
        shards.append(summed_shard(jnp.concatenate(parts, axis=1)))
    shards.reverse()
    w_in_grad = jnp.stack([shard[:, :FF] for shard in shards])
    w_out_grad = jnp.stack([shard[:, FF : 2 * FF].T for shard in shards])
    mix_grads = shards[0][:, 2 * FF :].reshape(-1, 2, LAYERS, 2 * BS).transpose(1, 2, 0, 3)

    def of_both(slot, change):
        return jnp.stack([change(sums[layer][slot]) for layer in range(LAYERS)])

    def line(array):
        return jnp.sum(array, axis=0)

    gain_grad, shift_grad, in_bias, out_bias, b_in_grad, b_out_grad = lax.psum(
        (
            jnp.stack([of_both(8, line), of_both(2, line)], axis=1),
            jnp.stack([of_both(9, line), of_both(3, line)], axis=1),
            of_both(5, small_bias),
            of_both(7, small_bias),
            of_both(0, line),
            of_both(1, line),
        ),
        ("wide", "rep"),
    )
    return (
        output, input_grad, gain_grad, shift_grad, mix_grads[0], in_bias, mix_grads[1], out_bias,
        w_in_grad, b_in_grad, w_out_grad, b_out_grad,
    )


def power_of_two(number):
    return number > 0 and number & (number - 1) == 0


def any_size(tokens, *others):
    wide, rep = lax.axis_size("wide"), lax.axis_size("rep")
    if tokens.shape[0] % wide == 0 and power_of_two(wide) and power_of_two(rep) and wide <= 16:
        return whole_items(tokens, *others)
    return body(tokens, *others)


def solution(mesh):
    placed = (
        P("rep", "wide", None, None),
        P("rep", "wide", None, None),
        P(),
        P(),
        P(),
        P(),
        P(),
        P(),
        P(),
        P(),
        P(),
        P(),
    )
    return jax.shard_map(
        any_size,
        mesh=mesh,
        in_specs=placed,
        out_specs=(
            P("rep", "wide", None, None),
            P("rep", "wide", None, None),
            P(),
            P(),
            P(None, "wide", None),
            P(),
            P(None, "wide", None),
            P(),
            P(None, "wide", None),
            P(),
            P(None, None, "wide"),
            P(),
        ),
        check_vma=False,
    )
```

```python
import functools
import math

import jax
import jax.numpy as jnp
import ml_dtypes
import numpy as np
from jax import lax
from jax.experimental import pallas as pl
from jax.experimental.pallas import tpu as pltpu
from jax.sharding import PartitionSpec as P

D = 512
NB = 8
BS = 64
KW = 32
KH = 32
H = 64
W = 64
LAYERS = 2


EPSILON = 1e-05
THRESHOLD = 0.1
HIGHEST = lax.Precision.HIGHEST


def dft_tables():
    col_index = jnp.arange(W, dtype=jnp.int32)
    col_freq = jnp.arange(KW, dtype=jnp.int32)
    col_phase = (col_index[:, None] * col_freq[None, :] % W).astype(jnp.float32) * (
        2.0 * math.pi / W
    )
    col_scale = 1.0 / math.sqrt(W)
    forward_cols = jnp.stack([jnp.cos(col_phase), -jnp.sin(col_phase)], axis=1) * col_scale
    doubling = jnp.where(col_freq == 0, 1.0, 2.0).astype(jnp.float32)
    inverse_cols = (
        jnp.stack(
            [jnp.cos(col_phase).T * doubling[:, None], -jnp.sin(col_phase).T * doubling[:, None]],
            axis=0,
        )
        * col_scale
    )
    row_index = jnp.arange(H, dtype=jnp.int32)
    mode_index = jnp.arange(KH, dtype=jnp.int32)
    row_freq = jnp.where(mode_index < KH // 2, mode_index, H - KH + mode_index)
    row_phase = (row_freq[:, None] * row_index[None, :] % H).astype(jnp.float32) * (
        2.0 * math.pi / H
    )
    cosine = jnp.cos(row_phase) / math.sqrt(H)
    sine = jnp.sin(row_phase) / math.sqrt(H)
    forward_rows = jnp.stack([jnp.stack([cosine, sine], -1), jnp.stack([-sine, cosine], -1)], 1)
    inverse_rows = jnp.stack(
        [jnp.stack([cosine.T, -sine.T], -1), jnp.stack([sine.T, cosine.T], -1)], 1
    )
    return (forward_cols, inverse_cols, forward_rows, inverse_rows)


def layer_norm(values, gain_row, shift_row):
    center = values - jnp.mean(values, axis=-1, keepdims=True)
    spread = jnp.mean(center * center, axis=-1, keepdims=True)
    return center * lax.rsqrt(spread + EPSILON) * gain_row + shift_row


def gelu_tanh(values):
    return jax.nn.gelu(values, approximate=True)


def shrink(values):
    return values - THRESHOLD * jnp.tanh(values / THRESHOLD)


def block_matrix(weights, onehot_low):
    picked = jnp.einsum(
        "ac,cbd->abd",
        onehot_low,
        weights.reshape(NB, BS, 2 * BS),
        preferred_element_type=jnp.float32,
    ).astype(jnp.bfloat16)
    real_part = picked[:, :, :BS]
    imag_part = picked[:, :, BS:]
    upper = jnp.concatenate([real_part, imag_part], -1)
    lower = jnp.concatenate([-imag_part, real_part], -1)
    return jnp.concatenate([upper, lower], 1)


def mode_forward(arriving, forward_rows, mixing):
    first_big, first_bias, second_big, second_bias = mixing
    item_count, pair_count = (arriving.shape[0], arriving.shape[1])
    halves = arriving.reshape(item_count, pair_count, H, 2, BS)
    mode_data = jnp.einsum(
        "jphq,iahqb->iajpb", forward_rows, halves, preferred_element_type=jnp.float32
    )
    mode_data = mode_data.reshape(item_count, pair_count, KH, 2 * BS).astype(jnp.bfloat16)
    first_pre = (
        jnp.einsum("iakc,acd->iakd", mode_data, first_big, preferred_element_type=jnp.float32)
        + first_bias[None, :, None, :]
    )
    active = gelu_tanh(first_pre).astype(jnp.bfloat16)
    second = (
        jnp.einsum("iakc,acd->iakd", active, second_big, preferred_element_type=jnp.float32)
        + second_bias[None, :, None, :]
    )
    return (mode_data, first_pre, active, second)


def mode_inverse(second, inverse_rows):
    item_count, pair_count = (second.shape[0], second.shape[1])
    shrunk = shrink(second).astype(jnp.bfloat16).reshape(item_count, pair_count, KH, 2, BS)
    rows_out = jnp.einsum(
        "hpjq,iajqb->iahpb", inverse_rows, shrunk, preferred_element_type=jnp.float32
    )
    return rows_out.reshape(item_count, pair_count, H, 2 * BS).astype(jnp.bfloat16)


def mode_backward(first_pre, second, arrived, forward_rows, inverse_rows, mixing):
    first_big, first_bias, second_big, second_bias = mixing
    item_count, pair_count = (arrived.shape[0], arrived.shape[1])
    halves = arrived.reshape(item_count, pair_count, H, 2, BS)
    d_shrunk = jnp.einsum(
        "hpjq,iahpb->iajqb", inverse_rows, halves, preferred_element_type=jnp.float32
    )
    d_shrunk = d_shrunk.reshape(item_count, pair_count, KH, 2 * BS)
    unused, shrink_pull = jax.vjp(shrink, second)
    d_second = shrink_pull(d_shrunk)[0].astype(jnp.bfloat16)
    d_active = jnp.einsum(
        "iakd,acd->iakc", d_second, second_big, preferred_element_type=jnp.float32
    )
    unused, gelu_pull = jax.vjp(gelu_tanh, first_pre)
    d_first = gelu_pull(d_active)[0].astype(jnp.bfloat16)
    d_modes = jnp.einsum(
        "iakd,acd->iakc", d_first, first_big, preferred_element_type=jnp.float32
    ).astype(jnp.bfloat16)
    d_halves = d_modes.reshape(item_count, pair_count, KH, 2, BS)
    d_rows = jnp.einsum(
        "jphq,iajpb->iahqb", forward_rows, d_halves, preferred_element_type=jnp.float32
    )
    return (
        d_rows.reshape(item_count, pair_count, H, 2 * BS).astype(jnp.bfloat16),
        d_first,
        d_second,
    )


def block_grads(inputs, grads, onehot_full):
    product = jnp.einsum("iakc,iakd->acd", inputs, grads, preferred_element_type=jnp.float32)
    real_grad = product[:, :BS, :BS] + product[:, BS:, BS:]
    imag_grad = product[:, :BS, BS:] - product[:, BS:, :BS]
    pair_grad = jnp.concatenate([real_grad, imag_grad], -1)
    weight_grad = jnp.einsum("ac,abd->cbd", onehot_full, pair_grad, precision=HIGHEST).reshape(
        D, 2 * BS
    )
    bias_terms = jnp.sum(grads.astype(jnp.float32), axis=(0, 2))
    bias_grad = jnp.dot(onehot_full.T, bias_terms, precision=HIGHEST)
    return (weight_grad, bias_grad)


def body(
    tokens,
    cotangent,
    norm_gain,
    norm_shift,
    mix_in,
    mix_in_bias,
    mix_out,
    mix_out_bias,
    w_in,
    b_in,
    w_out,
    b_out,
):
    forward_cols, inverse_cols, forward_rows, inverse_rows = [
        table_item.astype(jnp.bfloat16) for table_item in dft_tables()
    ]
    devices = lax.axis_size("wide")
    per_device = NB * KW // devices
    global_pair = lax.axis_index("wide") * per_device + jnp.arange(per_device, dtype=jnp.int32)
    onehot_full = (global_pair[:, None] // KW == jnp.arange(NB, dtype=jnp.int32)[None, :]).astype(
        jnp.float32
    )
    onehot_low = onehot_full.astype(jnp.bfloat16)
    item_count, rows_dev = (tokens.shape[0], tokens.shape[1])
    current = tokens.astype(jnp.float32)
    stored = []
    for depth_index in range(LAYERS):
        mixing = (
            block_matrix(mix_in[depth_index], onehot_low),
            jnp.dot(onehot_full, mix_in_bias[depth_index], precision=HIGHEST),
            block_matrix(mix_out[depth_index], onehot_low),
            jnp.dot(onehot_full, mix_out_bias[depth_index], precision=HIGHEST),
        )
        normed = layer_norm(current, norm_gain[depth_index, 0], norm_shift[depth_index, 0])
        spectra = jnp.einsum(
            "irwcb,wpk->ickrpb",
            normed.astype(jnp.bfloat16).reshape(item_count, rows_dev, W, NB, BS),
            forward_cols,
            preferred_element_type=jnp.float32,
        )
        spectra = spectra.reshape(item_count, NB * KW, rows_dev, 2 * BS).astype(jnp.bfloat16)
        forward_mode_data, first_pre, forward_active, second = mode_forward(
            lax.all_to_all(spectra, "wide", split_axis=1, concat_axis=2, tiled=True),
            forward_rows,
            mixing,
        )
        returning = lax.all_to_all(
            mode_inverse(second, inverse_rows), "wide", split_axis=2, concat_axis=1, tiled=True
        )
        returned = (returning,)
        back_rows = returned[0].reshape(item_count, NB, KW, rows_dev, 2, BS)
        filtered = jnp.einsum(
            "pkw,ickrpb->irwcb", inverse_cols, back_rows, preferred_element_type=jnp.float32
        )
        middle = current + filtered.reshape(item_count, rows_dev, W, D) + normed
        lowered = layer_norm(middle, norm_gain[depth_index, 1], norm_shift[depth_index, 1]).astype(
            jnp.bfloat16
        )
        hidden_pre = (
            jnp.einsum(
                "irwd,df->irwf", lowered, w_in[depth_index], preferred_element_type=jnp.float32
            )
            + b_in[depth_index]
        )
        hidden_act = gelu_tanh(hidden_pre).astype(jnp.bfloat16)
        branch = (
            jnp.einsum(
                "irwf,fd->irwd", hidden_act, w_out[depth_index], preferred_element_type=jnp.float32
            )
            + b_out[depth_index]
        )
        stored.append(
            (
                current,
                normed,
                spectra,
                middle,
                lowered,
                hidden_pre,
                hidden_act,
                mixing,
                returned[1:],
            )
        )
        current = middle + branch
    upstream = cotangent
    collected = [None] * LAYERS
    for depth_index in reversed(range(LAYERS)):
        (
            layer_input,
            normed,
            spectra,
            middle,
            lowered,
            hidden_pre,
            hidden_act,
            mixing,
            kept_modes,
        ) = stored[depth_index]
        branch_grad = upstream.astype(jnp.bfloat16)
        w_out_part = jnp.einsum(
            "irwf,irwd->fd", hidden_act, branch_grad, preferred_element_type=jnp.float32
        )
        b_out_part = jnp.sum(branch_grad.astype(jnp.float32), axis=(0, 1, 2))
        act_grad = jnp.einsum(
            "irwd,fd->irwf", branch_grad, w_out[depth_index], preferred_element_type=jnp.float32
        )
        unused, gelu_pull = jax.vjp(gelu_tanh, hidden_pre)
        pre_grad = gelu_pull(act_grad)[0].astype(jnp.bfloat16)
        w_in_part = jnp.einsum(
            "irwd,irwf->df", lowered, pre_grad, preferred_element_type=jnp.float32
        )
        b_in_part = jnp.sum(pre_grad.astype(jnp.float32), axis=(0, 1, 2))
        low_grad = jnp.einsum(
            "irwf,df->irwd", pre_grad, w_in[depth_index], preferred_element_type=jnp.float32
        )
        unused, second_norm_pull = jax.vjp(
            layer_norm, middle, norm_gain[depth_index, 1], norm_shift[depth_index, 1]
        )
        mid_norm_grad, gain_second, shift_second = second_norm_pull(low_grad)
        mid_grad = upstream + mid_norm_grad
        filt_grad = mid_grad.astype(jnp.bfloat16).reshape(item_count, rows_dev, W, NB, BS)
        back_grad = jnp.einsum(
            "pkw,irwcb->ickrpb", inverse_cols, filt_grad, preferred_element_type=jnp.float32
        )
        back_grad = back_grad.reshape(item_count, NB * KW, rows_dev, 2 * BS).astype(jnp.bfloat16)
        backward_arriving = lax.all_to_all(spectra, "wide", split_axis=1, concat_axis=2, tiled=True)
        arrived = lax.all_to_all(back_grad, "wide", split_axis=1, concat_axis=2, tiled=True)
        backward_mode_data, backward_first_pre, backward_active, backward_second = mode_forward(
            backward_arriving, forward_rows, mixing
        )
        d_rows, d_first, d_second = mode_backward(
            backward_first_pre, backward_second, arrived, forward_rows, inverse_rows, mixing
        )
        sent_back = lax.all_to_all(d_rows, "wide", split_axis=2, concat_axis=1, tiled=True)
        col_grad, mode_data, active, d_first, d_second = (
            sent_back,
            backward_mode_data,
            backward_active,
            d_first,
            d_second,
        )
        mix_in_part, mix_in_bias_part = block_grads(mode_data, d_first, onehot_full)
        mix_out_part, mix_out_bias_part = block_grads(active, d_second, onehot_full)
        col_grad = col_grad.reshape(item_count, NB, KW, rows_dev, 2, BS)
        normed_grad = jnp.einsum(
            "wpk,ickrpb->irwcb", forward_cols, col_grad, preferred_element_type=jnp.float32
        )
        normed_grad = normed_grad.reshape(item_count, rows_dev, W, D) + mid_grad
        unused, first_norm_pull = jax.vjp(
            layer_norm, layer_input, norm_gain[depth_index, 0], norm_shift[depth_index, 0]
        )
        input_part, gain_first, shift_first = first_norm_pull(normed_grad)
        upstream = mid_grad + input_part
        collected[depth_index] = (
            jnp.stack([gain_first, gain_second]),
            jnp.stack([shift_first, shift_second]),
            mix_in_part,
            mix_in_bias_part,
            mix_out_part,
            mix_out_bias_part,
            w_in_part,
            b_in_part,
            w_out_part,
            b_out_part,
        )
    stacked = [
        jnp.stack([collected[depth_index][slot] for depth_index in range(LAYERS)])
        for slot in range(10)
    ]
    small_grads = lax.psum(
        (stacked[0], stacked[1], stacked[3], stacked[5], stacked[7], stacked[9]), ("wide", "rep")
    )
    large_grads = (stacked[2], stacked[4], stacked[6], stacked[8])
    pieces = (
        lax.psum_scatter(large_grads[0], "wide", scatter_dimension=1, tiled=True),
        lax.psum_scatter(large_grads[1], "wide", scatter_dimension=1, tiled=True),
        lax.psum_scatter(large_grads[2], "wide", scatter_dimension=1, tiled=True),
        lax.psum_scatter(large_grads[3], "wide", scatter_dimension=2, tiled=True),
    )
    pieces = (
        lax.psum(pieces[0].astype(jnp.bfloat16), "rep").astype(jnp.float32),
        lax.psum(pieces[1].astype(jnp.bfloat16), "rep").astype(jnp.float32),
        lax.psum(pieces[2].astype(jnp.bfloat16), "rep").astype(jnp.float32),
        lax.psum(pieces[3].astype(jnp.bfloat16), "rep").astype(jnp.float32),
    )
    return (
        current,
        upstream,
        small_grads[0],
        small_grads[1],
        pieces[0],
        small_grads[2],
        pieces[1],
        small_grads[3],
        pieces[2],
        small_grads[4],
        pieces[3],
        small_grads[5],
    )


BF = jnp.bfloat16
F32 = jnp.float32
FF = 2048
GROUPS = 4
GELU_A = math.sqrt(2.0 / math.pi)
GELU_B = GELU_A * 0.044715
HB = 16
KB = 16
TT = 512
FC = 1024
VMEM = 58 * 1024 * 1024


def plain_tables():
    def low(table):
        return table.astype(np.float32).astype(ml_dtypes.bfloat16).astype(np.float64)

    index = np.arange(64)
    col_phase = 2.0 * np.pi * ((index[:, None] * np.arange(KW)[None, :]) % W) / W
    forward_cols = np.stack([np.cos(col_phase), -np.sin(col_phase)], axis=1) / math.sqrt(W)
    doubling = np.where(np.arange(KW) == 0, 1.0, 2.0)[:, None]
    inverse_cols = (
        np.stack([np.cos(col_phase).T * doubling, -np.sin(col_phase).T * doubling], axis=0)
        / math.sqrt(W)
    )
    modes = np.arange(KH)
    row_freq = np.where(modes < KH // 2, modes, H - KH + modes)
    row_phase = 2.0 * np.pi * ((row_freq[:, None] * index[None, :]) % H) / H
    cosine = np.cos(row_phase) / math.sqrt(H)
    sine = np.sin(row_phase) / math.sqrt(H)
    forward_rows = np.stack([np.stack([cosine, sine], -1), np.stack([-sine, cosine], -1)], 1)
    inverse_rows = np.stack(
        [np.stack([cosine.T, -sine.T], -1), np.stack([sine.T, cosine.T], -1)], 1
    )
    return [low(table) for table in (forward_cols, inverse_cols, forward_rows, inverse_rows)]


def matrix_tables():
    forward_cols, inverse_cols, forward_rows, inverse_rows = plain_tables()
    eye = np.eye(8)
    into = np.einsum("wpk,gh->kpghw", forward_cols, eye).reshape(512, 512)
    outof = np.einsum("pkw,gh->gwkph", inverse_cols, eye).reshape(512, 512)
    pair = np.eye(2)
    rows_in = np.einsum("jphq,ab->apjbqh", forward_rows, pair).reshape(128, 256)
    rows_out = np.einsum("hpjq,ab->aphbqj", inverse_rows, pair).reshape(256, 128)
    return [
        jnp.asarray(np.ascontiguousarray(table).astype(ml_dtypes.bfloat16))
        for table in (into, outof, rows_in, rows_out, outof.T, into.T, rows_out.T, rows_in.T)
    ]


def big_matrices(weight):
    four = weight.reshape(GROUPS, 2, BS, 2, BS)
    eye = jnp.eye(2, dtype=weight.dtype)
    real = (four[:, :, :, 0][:, :, :, None, :] * eye[None, :, None, :, None]).reshape(
        GROUPS, 128, 128
    )
    imag = (four[:, :, :, 1][:, :, :, None, :] * eye[None, :, None, :, None]).reshape(
        GROUPS, 128, 128
    )
    upper = jnp.concatenate([real, imag], -1)
    lower = jnp.concatenate([-imag, real], -1)
    return jnp.concatenate([upper, lower], 1)


def big_bias(bias):
    return bias.reshape(GROUPS, 2, 2, BS).transpose(0, 2, 1, 3).reshape(GROUPS, 1, 256)


def small_bias(line):
    parts = line.reshape(-1, GROUPS, 2, 2, BS).transpose(0, 1, 3, 2, 4)
    return parts.reshape(-1, NB, 2 * BS)


def mm(left, right):
    return jnp.dot(left, right, preferred_element_type=F32)


def mm_t(left, right):
    return lax.dot_general(left, right, (((1,), (1,)), ((), ())), preferred_element_type=F32)


def normalize(values):
    center = values - jnp.mean(values, axis=-1, keepdims=True)
    spread = jnp.mean(center * center, axis=-1, keepdims=True)
    scale = lax.rsqrt(spread + EPSILON)
    return center * scale, scale


def normalize_back(grad, unit, scale, gain_row):
    inner = grad * gain_row
    return scale * (
        inner
        - jnp.mean(inner, axis=-1, keepdims=True)
        - unit * jnp.mean(inner * unit, axis=-1, keepdims=True)
    )


def folded(values):
    return jnp.sum(values.reshape(values.shape[0] // 8, 8, values.shape[1]), axis=0)


def gelu_of(v):
    return 0.5 * v * (1.0 + jnp.tanh(v * (GELU_A + GELU_B * (v * v))))


def gelu_and_slope(v):
    square = v * v
    bend = jnp.tanh(v * (GELU_A + GELU_B * square))
    half = 0.5 * (1.0 + bend)
    slope = half + 0.5 * v * (1.0 - bend * bend) * (GELU_A + 3.0 * GELU_B * square)
    return v * half, slope


def cols_in(table, rows, store, at):
    halves = [mm(table, rows[half * 512 : (half + 1) * 512]).reshape(64, 8, D) for half in range(2)]
    store[:, pl.ds(at, HB), :] = jnp.concatenate(halves, axis=1).astype(BF)


def cols_out(table, store, at):
    block = store[:, pl.ds(at, HB), :].astype(F32)
    return jnp.concatenate(
        [
            mm(table, block[:, half * 8 : half * 8 + 8].reshape(512, D).astype(BF))
            for half in range(2)
        ],
        axis=0,
    )


def lanes_of(rows, group):
    lanes = slice(group * 128, group * 128 + 128)
    return jnp.concatenate(
        [rows[:, :32, lanes].reshape(KB * 32, 128), rows[:, 32:, lanes].reshape(KB * 32, 128)],
        axis=1,
    )


def put_lanes(store, group, values):
    lanes = slice(group * 128, group * 128 + 128)
    store[:, :32, lanes] = values[:, :128].reshape(KB, 32, 128)
    store[:, 32:, lanes] = values[:, 128:].reshape(KB, 32, 128)


def spectral_forward_kernel(
    x_ref, gain, shift, into, outof, rows_in, rows_out, w1, b1, w2, b2, mid_ref, spec_ref,
    cols, mixed, held,
):
    step = pl.program_id(0)
    n_rows, n_freq = H // HB, KW // KB

    @pl.when(step < n_rows)
    def _():
        x = lines_of(x_ref)
        held[step] = x
        unit, _ = normalize(x.astype(F32))
        normed = unit * gain[...] + shift[...]
        cols_in(into[...], normed.astype(BF), cols, pl.multiple_of(step * HB, HB))

    @pl.when((step >= n_rows) & (step < n_rows + n_freq))
    def _():
        first_plane = (step - n_rows) * (2 * KB)
        for two in range(KB // 2):
            planes = cols[pl.ds(first_plane + 4 * two, 4)]
            spec_ref[2 * two : 2 * two + 2] = (
                mm(rows_in[...], planes.reshape(256, D)).astype(BF).reshape(2, 64, D)
            )
        modes = spec_ref[...]
        for group in range(GROUPS):
            first = mm(lanes_of(modes, group), w1[group]) + b1[group]
            second = mm(gelu_of(first).astype(BF), w2[group]) + b2[group]
            shrunk = second - THRESHOLD * jnp.tanh(second * (1.0 / THRESHOLD))
            put_lanes(mixed, group, shrunk.astype(BF))
        for two in range(KB // 2):
            planes = mixed[2 * two : 2 * two + 2].reshape(128, D)
            cols[pl.ds(first_plane + 4 * two, 4)] = (
                mm(rows_out[...], planes).astype(BF).reshape(4, 64, D)
            )

    @pl.when(step >= n_rows + n_freq)
    def _():
        block = step - n_rows - n_freq
        x = held[block].astype(F32)
        unit, _ = normalize(x)
        normed = unit * gain[...] + shift[...]
        filtered = cols_out(outof[...], cols, pl.multiple_of(block * HB, HB))
        mid_ref[...] = (x + filtered + normed).astype(mid_ref.dtype)


def compact(big):
    low_lanes = lax.broadcasted_iota(jnp.int32, (BS, 128), 1) < BS
    parts = []
    for c in range(2):
        real_rows, imag_rows = slice(c * BS, c * BS + BS), slice(128 + c * BS, 128 + c * BS + BS)
        real = big[real_rows, :128] + big[imag_rows, 128:]
        imag = big[real_rows, 128:] - big[imag_rows, :128]
        if c == 0:
            parts.append(jnp.where(low_lanes, real, pltpu.roll(imag, BS, 1)))
        else:
            parts.append(jnp.where(low_lanes, pltpu.roll(real, BS, 1), imag))
    return jnp.concatenate(parts, axis=0)


def spectral_backward_kernel(with_start, *refs):
    (
        x_ref, grad_ref, spec_ref, gain, outof_t, into_t, rows_out_t, rows_in_t,
        w1, b1, w2, b2, w1_t, w2_t,
    ), refs = refs[:14], refs[14:]
    starts, refs = refs[:2] if with_start else (), refs[2:] if with_start else refs
    new_ref, blocks, lines, dw1, dw2, cols, mixed, kept, held = refs
    step = pl.program_id(0)
    n_rows, n_freq = H // HB, KW // KB

    @pl.when(step == 0)
    def _():
        lines[...] = starts[1][...] if with_start else jnp.zeros_like(lines)
        for ref in (dw1, dw2):
            ref[...] = jnp.zeros_like(ref)

    @pl.when(step < n_rows)
    def _():
        grad = grad_ref[...]
        held[step] = grad
        cols_in(outof_t[...], grad, cols, pl.multiple_of(step * HB, HB))

    @pl.when((step >= n_rows) & (step < n_rows + n_freq))
    def _():
        first_plane = (step - n_rows) * (2 * KB)
        for two in range(KB // 2):
            planes = cols[pl.ds(first_plane + 4 * two, 4)]
            kept[2 * two : 2 * two + 2] = mm(rows_out_t[...], planes.reshape(256, D)).reshape(
                2, 64, D
            )
        modes = spec_ref[...]
        grads = kept[...]
        for group in range(GROUPS):
            mode = lanes_of(modes, group)
            first = mm(mode, w1[group]) + b1[group]
            active, slope = gelu_and_slope(first)
            active = active.astype(BF)
            second = mm(active, w2[group]) + b2[group]
            bend = jnp.tanh(second * (1.0 / THRESHOLD))
            d_second = bend * bend * lanes_of(grads, group)
            at = slice(group * 256, group * 256 + 256)
            lines[:, 1024 + group * 256 : 1280 + group * 256] += folded(d_second)
            d_second = d_second.astype(BF)
            dw2[group] += mm(active.T, d_second)
            d_first = slope * mm(d_second, w2_t[group])
            lines[:, at] += folded(d_first)
            d_first = d_first.astype(BF)
            dw1[group] += mm(mode.T, d_first)
            put_lanes(mixed, group, mm(d_first, w1_t[group]).astype(BF))
        for two in range(KB // 2):
            planes = mixed[2 * two : 2 * two + 2].reshape(128, D)
            cols[pl.ds(first_plane + 4 * two, 4)] = (
                mm(rows_in_t[...], planes).astype(BF).reshape(4, 64, D)
            )

    @pl.when(step == n_rows + n_freq)
    def _():
        for group in range(GROUPS):
            at = slice(group * 128, group * 128 + 128)
            for slot, ref in enumerate((dw1, dw2)):
                lanes = slice(slot * 128, slot * 128 + 128)
                block = compact(ref[group])
                blocks[at, lanes] = block + starts[0][at, lanes] if with_start else block

    @pl.when(step >= n_rows + n_freq)
    def _():
        block = step - n_rows - n_freq
        unit, scale = normalize(lines_of(x_ref).astype(F32))
        mid_grad = held[block].astype(F32)
        grad = cols_out(into_t[...], cols, pl.multiple_of(block * HB, HB)) + mid_grad
        lines[:, 2048:2560] += folded(grad * unit)
        lines[:, 2560:3072] += folded(grad)
        new = mid_grad + normalize_back(grad, unit, scale, gain[...])
        new_ref[...] = new.astype(new_ref.dtype)


def feed_forward_kernel(mid_ref, gain, shift, w_in, b_in, w_out, b_out, *refs):
    out_ref, pre_ref = refs[-2:]
    middle = mid_ref[...].astype(F32)
    unit, _ = normalize(middle)
    lowered = (unit * gain[...] + shift[...]).astype(BF)
    total = middle + b_out[...]
    for part in range(FF // FC):
        at = slice(part * FC, part * FC + FC)
        pre = mm(lowered, w_in[:, at]) + b_in[:, at]
        pre = pre.astype(BF)
        pre_ref[:, at] = pre
        total += mm(gelu_of(pre), w_out[at, :])
    out_ref[...] = total.astype(out_ref.dtype)


def feed_backward_kernel(with_start, *refs):
    (g_ref, mid_ref, pre_ref, gain, shift, w_out, w_in), refs = refs[:7], refs[7:]
    if with_start:
        (start_far, start_lines, mid_grad_ref, sent, lines, dw, start, arrival) = refs
        copy = pltpu.make_async_copy(start_far, start, arrival)
    else:
        mid_grad_ref, dw, lines = refs
    step = pl.program_id(0)

    @pl.when(step == 0)
    def _():
        lines[...] = start_lines[...] if with_start else jnp.zeros_like(lines)
        dw[...] = jnp.zeros_like(dw)
        if with_start:
            copy.start()

    upstream = lines_of(g_ref)
    unit, scale = normalize(mid_ref[...].astype(F32))
    lowered = (unit * gain[...] + shift[...]).astype(BF)
    lines[:, FF : FF + D] += folded(upstream.astype(F32))
    upstream_t = upstream.T
    lowered_t = lowered.T
    low_grad = jnp.zeros((TT, D), F32)
    for part in range(FF // FC):
        at = slice(part * FC, part * FC + FC)
        active, slope = gelu_and_slope(pre_ref[:, at])
        dw[:, FF + part * FC : FF + part * FC + FC] += mm(upstream_t, active)
        pre_grad = slope * mm_t(upstream, w_out[at, :]).astype(BF)
        lines[:, at] += folded(pre_grad.astype(F32))
        dw[:, at] += mm(lowered_t, pre_grad)
        low_grad += mm_t(pre_grad, w_in[:, at])
    lines[:, FF + D : FF + 2 * D] += folded(low_grad * unit)
    lines[:, FF + 2 * D : FF + 3 * D] += folded(low_grad)
    new = upstream.astype(F32) + normalize_back(low_grad, unit, scale, gain[...])
    mid_grad_ref[...] = new.astype(mid_grad_ref.dtype)
    if with_start:

        @pl.when(step == H * W // TT - 1)
        def _():
            copy.wait()
            sent[...] = (dw[...] + start[...]).astype(BF)


def whole(array):
    zeros = (0,) * array.ndim
    return pl.BlockSpec(array.shape, lambda *_: zeros, pipeline_mode=pl.Buffered(1))


def of_layer(array, layer):
    at = (layer,) + (0,) * (array.ndim - 1)
    return pl.BlockSpec((None, *array.shape[1:]), lambda *_: at, pipeline_mode=pl.Buffered(1))


def rows_spec(rows, block_of, array=None, kind=None):
    if kind is None:
        return pl.BlockSpec((rows * W, D), lambda s: (block_of(s), 0))
    own = array.shape[2]
    return pl.BlockSpec((rows * W // own, None, own, D), lambda s: (block_of(s), kind, 0, 0))


def lines_of(ref):
    return ref[...].reshape(-1, D)


PARAMS = pltpu.CompilerParams(dimension_semantics=("arbitrary",), vmem_limit_bytes=VMEM)
COST = pl.CostEstimate(flops=1_000_000, bytes_accessed=1_000_000, transcendentals=0)


N_ROWS, N_FREQ = H // HB, KW // KB
SPECTRAL_STEPS = 2 * N_ROWS + N_FREQ


def first_end(step):
    return jnp.minimum(step, N_ROWS - 1)


def last_end(step):
    return jnp.maximum(step - N_ROWS - N_FREQ, 0)


def middle_part(step):
    return jnp.clip(step - N_ROWS, 0, N_FREQ - 1)


def spectral_forward(x, kind, gain, shift, tables, mix):
    small = (gain, shift, *tables[:4], *mix[:4])
    return pl.pallas_call(
        spectral_forward_kernel,
        grid=(SPECTRAL_STEPS,),
        in_specs=[rows_spec(HB, first_end, x, kind)] + [whole(array) for array in small],
        out_specs=[
            rows_spec(HB, last_end),
            pl.BlockSpec((KB, 64, D), lambda s: (middle_part(s), 0, 0)),
        ],
        out_shape=[
            jax.ShapeDtypeStruct((H * W, D), BF),
            jax.ShapeDtypeStruct((KW, 64, D), BF),
        ],
        scratch_shapes=[
            pltpu.VMEM((64, 64, D), BF),
            pltpu.VMEM((KB, 64, D), BF),
            pltpu.VMEM((N_ROWS, HB * W, D), BF),
        ],
        compiler_params=PARAMS,
        cost_estimate=COST,
        name="spectral_forward",
    )(x, *small)


def spectral_backward(x, kind, grad, spec, gain, tables, mix, start):
    small = (gain, *tables[4:], *mix, *start)
    sums = [(D, 256), (8, 3072)]
    return pl.pallas_call(
        functools.partial(spectral_backward_kernel, len(start) > 0),
        grid=(SPECTRAL_STEPS,),
        in_specs=[
            rows_spec(HB, last_end, x, kind),
            rows_spec(HB, first_end),
            pl.BlockSpec((KB, 64, D), lambda s: (middle_part(s), 0, 0)),
        ]
        + [whole(array) for array in small],
        out_specs=[rows_spec(HB, last_end)] + [pl.BlockSpec(dims, lambda s: (0, 0)) for dims in sums],
        out_shape=[jax.ShapeDtypeStruct((H * W, D), BF)]
        + [jax.ShapeDtypeStruct(dims, F32) for dims in sums],
        scratch_shapes=[
            pltpu.VMEM((GROUPS, 256, 256), F32),
            pltpu.VMEM((GROUPS, 256, 256), F32),
            pltpu.VMEM((64, 64, D), BF),
            pltpu.VMEM((KB, 64, D), BF),
            pltpu.VMEM((KB, 64, D), F32),
            pltpu.VMEM((N_ROWS, HB * W, D), BF),
        ],
        compiler_params=PARAMS,
        cost_estimate=COST,
        name="spectral_backward",
    )(x, grad, spec, *small)


def feed_forward(middle, layer, gain, shift, w_in, b_in, w_out, b_out, abroad=None, onto=None):
    rows = rows_spec(TT // W, lambda s: s)
    shape = jax.ShapeDtypeStruct((H * W, D), BF)
    if abroad is not None:
        receivers, chunks, own, chunk = abroad
        shape = jax.ShapeDtypeStruct((receivers, chunks, own * W, D), BF)
        rows = pl.BlockSpec((None, None, TT, D), lambda s: (s, chunk, 0, 0))
    more = [] if onto is None else [onto]
    return pl.pallas_call(
        feed_forward_kernel,
        grid=(H * W // TT,),
        in_specs=[
            rows_spec(TT // W, lambda s: s),
            whole(gain),
            whole(shift),
            of_layer(w_in, layer),
            whole(b_in),
            of_layer(w_out, layer),
            whole(b_out),
        ]
        + [pl.BlockSpec(memory_space=pl.ANY) for _ in more],
        out_specs=[rows, pl.BlockSpec((TT, FF), lambda s: (s, 0))],
        out_shape=[shape, jax.ShapeDtypeStruct((H * W, FF), BF)],
        input_output_aliases={7: 0} if more else {},
        compiler_params=PARAMS,
        cost_estimate=COST,
        name="feed_forward",
    )(middle, gain, shift, w_in, b_in, w_out, b_out, *more)


def start_of(fb):
    return (fb[1], fb[2])


def feed_backward(g, kind, middle, pre, layer, gain, shift, w_out, w_in, start):
    sums = [(D, 2 * FF), (8, FF + 3 * D)]
    return pl.pallas_call(
        functools.partial(feed_backward_kernel, len(start) > 0),
        grid=(H * W // TT,),
        in_specs=[
            rows_spec(TT // W, lambda s: s, g, kind),
            rows_spec(TT // W, lambda s: s),
            pl.BlockSpec((TT, FF), lambda s: (s, 0)),
            whole(gain),
            whole(shift),
            of_layer(w_out, layer),
            of_layer(w_in, layer),
        ]
        + ([pl.BlockSpec(memory_space=pl.ANY), whole(start[1])] if start else []),
        out_specs=[rows_spec(TT // W, lambda s: s)]
        + [pl.BlockSpec(dims, lambda s: (0, 0)) for dims in sums],
        out_shape=[
            jax.ShapeDtypeStruct((H * W, D), BF),
            jax.ShapeDtypeStruct(sums[0], BF if start else F32),
            jax.ShapeDtypeStruct(sums[1], F32),
        ],
        scratch_shapes=[
            pltpu.VMEM(sums[0], F32),
            pltpu.VMEM(sums[0], F32),
            pltpu.SemaphoreType.DMA,
        ]
        if start
        else [],
        compiler_params=PARAMS,
        cost_estimate=COST,
        name="feed_backward",
    )(g, middle, pre, gain, shift, w_out, w_in, *start)


def widen_kernel(part, *refs):
    refs[-1][...] = part[...].astype(F32)


def widened(part, chunk, chunks, onto):
    items, parts = part.shape[:2]
    block = (None, None, *part.shape[2:])
    more = [] if onto is None else [onto]
    return pl.pallas_call(
        widen_kernel,
        grid=(parts, items),
        in_specs=[pl.BlockSpec(block, lambda p, s: (s, p, 0, 0, 0))]
        + [pl.BlockSpec(memory_space=pl.ANY) for _ in more],
        out_specs=pl.BlockSpec(block, lambda p, s: (chunk + p, s, 0, 0, 0)),
        out_shape=jax.ShapeDtypeStruct((chunks, items, *part.shape[2:]), F32),
        input_output_aliases={1: 0} if more else {},
        compiler_params=pltpu.CompilerParams(
            dimension_semantics=("arbitrary", "arbitrary"), vmem_limit_bytes=VMEM
        ),
        cost_estimate=COST,
        name="widen",
    )(part, *more)


def exchange(array):
    return lax.all_to_all(array, "wide", split_axis=0, concat_axis=0, tiled=True)


def after(array, other):
    return lax.optimization_barrier((array, other))[0]


def swapped(array, axis_name, far):
    size = lax.axis_size(axis_name)
    return lax.ppermute(array, axis_name, [(i, i ^ far) for i in range(size)])


def tree_sum(parts):
    parts = [part.astype(F32) for part in parts]
    while len(parts) > 1:
        parts = [parts[at] + parts[at + 1] for at in range(0, len(parts), 2)]
    return parts[0]


def share(array, index, size, axis):
    return lax.dynamic_slice_in_dim(array, index * size, size, axis)


def own_half(array, axis_name, bit, axis):
    mine, half = (lax.axis_index(axis_name) >> bit) & 1, array.shape[axis] // 2
    other = share(array, 1 - mine, half, axis).astype(BF)
    return tree_sum([share(array, mine, half, axis), swapped(other, axis_name, 1 << bit)])


def own_rows(array, bits, parts):
    for bit in bits:
        blocks = array.reshape(parts // 2, 2, -1, array.shape[1])
        array = own_half(blocks, "wide", bit, 1).reshape(-1, array.shape[1])
        parts //= 2
    return array


def wide_step(blocks, packed, bit, wide):
    mine = (lax.axis_index("wide") >> bit) & 1
    halves = blocks.reshape(wide >> (bit + 1), 2, -1, 128)
    own, other = (share(halves, at, 1, 1).reshape(-1, 128) for at in (mine, 1 - mine))
    arrived = swapped(jnp.concatenate([other, packed]), "wide", 1 << bit)
    return own + arrived[: own.shape[0]], packed + arrived[own.shape[0] :]


def reversed_bits(value, bits):
    return sum(((value >> bit) & 1) << (bits - 1 - bit) for bit in range(bits))


def gathered(array):
    me = lax.axis_index("rep")
    parts = [array]
    for bit in reversed(range(lax.axis_size("rep").bit_length() - 1)):
        mine = ((me >> bit) & 1) == 0
        others = [swapped(part, "rep", 1 << bit) for part in (jnp.concatenate(parts, axis=1),)][0]
        others = jnp.split(others, len(parts), axis=1)
        parts = [
            jnp.where(mine == (side == 0), part, other)
            for side in range(2)
            for part, other in zip(parts, others)
        ]
    bits = lax.axis_size("rep").bit_length() - 1
    return [parts[reversed_bits(index, bits)] for index in range(len(parts))]


def whole_items(
    tokens, cotangent, norm_gain, norm_shift, mix_in, mix_in_bias, mix_out, mix_out_bias,
    w_in, b_in, w_out, b_out,
):
    wide = lax.axis_size("wide")
    chunks = tokens.shape[0] // wide
    abroad = (wide, *tokens.shape[1:])

    def rows_by_layer(array):
        return [array[layer].reshape(-1, 1, array.shape[-1]) for layer in range(LAYERS)]

    lines = [
        [[line for line in group] for group in rows_by_layer(array)]
        for array in (norm_gain, norm_shift, b_in, b_out)
    ]

    tables = matrix_tables()
    mixes = []
    for layer in range(LAYERS):
        first_mats, second_mats = big_matrices(mix_in[layer]), big_matrices(mix_out[layer])
        mixes.append(
            (
                first_mats,
                big_bias(mix_in_bias[layer]),
                second_mats,
                big_bias(mix_out_bias[layer]),
                first_mats.transpose(0, 2, 1),
                second_mats.transpose(0, 2, 1),
            )
        )

    stored = {}
    feed_sums = [()] * LAYERS
    mix_sums = [()] * LAYERS
    tie = lax.optimization_barrier

    def rows_of(array, chunk):
        return array[chunk * wide : chunk * wide + wide].astype(BF)

    def forward(chunk, current, kind, onto):
        for layer in range(LAYERS):
            middle, spec = spectral_forward(
                current, kind, gains[layer][0], shifts[layer][0], tables, mixes[layer]
            )
            last = layer == LAYERS - 1
            following, pre = feed_forward(
                middle, layer, gains[layer][1], shifts[layer][1], w_in,
                in_biases[layer][0], w_out, out_biases[layer][0],
                abroad=(wide, chunks, tokens.shape[1], chunk) if last else None,
                onto=onto if last else None,
            )
            stored[layer, chunk] = (current, kind, middle, spec, pre)
            current, kind = following, None
        return current

    def backward_feed(chunk, layer, grad, kind=None):
        _, _, middle, _, pre = stored[layer, chunk]
        mid_grad, *feed_sums[layer] = feed_backward(
            grad, kind, middle, pre, layer, gains[layer][1], shifts[layer][1], w_out, w_in,
            feed_sums[layer],
        )
        return mid_grad

    def backward_spectral(chunk, layer, mid_grad):
        layer_input, kind, _, spec, _ = stored[layer, chunk]
        grad, *mix_sums[layer] = spectral_backward(
            layer_input, kind, mid_grad, spec, gains[layer][0], tables, mixes[layer], mix_sums[layer]
        )
        return grad

    def backward(chunk, layer, grad):
        return backward_spectral(chunk, layer, backward_feed(chunk, layer, grad))

    def as_item(array):
        return array.reshape(H * W, D)

    def one_part(array):
        return array.reshape(wide, 1, *tokens.shape[1:])

    def both(first, second):
        return jnp.stack([first, second], axis=1).reshape(wide, 2, -1, D)

    sent, tokens_here, cotangent_here = tie((rows_of(tokens, 0), tokens, cotangent))
    arrived = exchange(sent)
    arrived, mixes, lines, sent, later = tie(
        (
            arrived,
            mixes,
            lines,
            rows_of(cotangent_here, 0),
            both(rows_of(tokens_here, 1), rows_of(cotangent_here, 1)),
        )
    )
    gains, shifts, in_biases, out_biases = lines
    upstream = exchange(sent)
    output = forward(0, as_item(arrived), None, None)

    upstream, output, later = tie((upstream, output, later))
    arrived = exchange(later)
    grad = backward(0, 1, as_item(upstream))
    grad = backward(0, 0, grad)

    grad, arrived, output = tie((grad, arrived, output))
    returned = exchange(grad.reshape(abroad))
    output = forward(1, arrived, 0, output)

    returned, output, arrived = tie((returned, output, arrived))
    delivered = exchange(output)
    mid_grad = backward_feed(1, 1, arrived, 1)
    grad = backward_spectral(1, 1, mid_grad)
    last_sum, grad = tie((own_half(feed_sums[1][0], "rep", 0, 1), grad))
    mid_grad = backward_feed(1, 0, grad)
    last_sum = own_half(last_sum, "rep", 1, 1)
    first_sum = own_half(after(feed_sums[0][0], last_sum), "rep", 0, 1)
    mid_grad, last_sum, first_sum = tie((mid_grad, last_sum, first_sum))
    grad = backward_spectral(1, 0, mid_grad)
    last_sum = own_rows(last_sum, [0], wide)
    first_sum = own_half(first_sum, "rep", 1, 1)

    delivered, grad, last_sum, first_sum, feed_sums, mix_sums = tie(
        (delivered, grad, last_sum, first_sum, feed_sums, mix_sums)
    )
    input_grad = widened(one_part(returned), 0, chunks, None)
    returned = exchange(grad.reshape(abroad))
    output = widened(
        delivered.reshape(wide, chunks, *tokens.shape[1:]), 0, chunks, None
    ).reshape(tokens.shape)
    packed = jnp.stack(
        [
            jnp.concatenate([jnp.sum(sums[layer][1], axis=0) for sums in (feed_sums, mix_sums)])
            for layer in range(LAYERS)
        ]
    ).reshape(-1, 128)
    blocks = jnp.concatenate([sums[0] for sums in mix_sums], axis=1)
    rep, rep_at, wide_at = lax.axis_size("rep"), lax.axis_index("rep"), lax.axis_index("wide")
    width = blocks.shape[1] // rep

    def mixed_message(far):
        return jnp.concatenate([share(blocks, rep_at ^ far, width, 1).reshape(-1, 128), packed])

    summed = tree_sum(
        [mixed_message(0)] + [swapped(mixed_message(far), "rep", far) for far in range(1, rep)]
    )
    blocks, packed = summed[: D * width // 128], summed[D * width // 128 :]
    extra = (input_grad, output)
    top = wide.bit_length() - 2
    for bit in range(top):
        if bit + 1 < top:
            last_sum = own_rows(last_sum, [bit + 1], wide >> (bit + 1))
        first_sum = own_rows(first_sum, [bit], wide >> bit)
        if bit:
            blocks, packed = wide_step(blocks, packed, bit - 1, wide)
        last_sum, first_sum, blocks, packed, extra = tie(
            (last_sum, first_sum, blocks, packed, extra)
        )
    blocks, packed = wide_step(blocks, packed, top - 1, wide)
    blocks, packed = wide_step(blocks, packed, top, wide)
    last_sum, first_sum = (own_rows(each, [top], wide >> top) for each in (last_sum, first_sum))
    input_grad, output = extra
    returned, output, packed, blocks, last_sum, first_sum = tie(
        (returned, output, packed, blocks, last_sum, first_sum)
    )
    pieces = gathered(
        jnp.concatenate([first_sum, last_sum, blocks.reshape(-1, width)], axis=1).astype(BF)
    )
    columns = first_sum.shape[1]
    in_order = [pieces[reversed_bits(index, rep.bit_length() - 1)] for index in range(rep)]
    matrices = [
        jnp.concatenate([piece[:, at : at + columns] for piece in in_order], axis=1).astype(F32)
        for at in (0, columns)
    ]
    blocks = jnp.concatenate([piece[:, 2 * columns :] for piece in pieces], axis=1).astype(F32)
    w_in_grad = jnp.stack([matrix[:, :FF] for matrix in matrices])
    w_out_grad = jnp.stack([matrix[:, FF:].T for matrix in matrices])
    mix_grads = blocks.reshape(-1, LAYERS, 2, 2 * BS).transpose(2, 1, 0, 3)
    packed = packed.reshape(LAYERS, -1)
    input_grad = widened(one_part(returned), 1, chunks, input_grad).reshape(tokens.shape)

    b_in_grad, b_out_grad, gain_two, shift_two, in_bias, out_bias, gain_one, shift_one = (
        jnp.split(packed, np.cumsum([FF, D, D, D, 1024, 1024, D]), axis=1)
    )
    return (
        output, input_grad, jnp.stack([gain_one, gain_two], axis=1),
        jnp.stack([shift_one, shift_two], axis=1), mix_grads[0], small_bias(in_bias),
        mix_grads[1], small_bias(out_bias), w_in_grad, b_in_grad, w_out_grad, b_out_grad,
    )


def power_of_two(number):
    return number > 0 and number & (number - 1) == 0


def any_size(tokens, *others):
    wide, rep = lax.axis_size("wide"), lax.axis_size("rep")
    if tokens.shape[0] == 2 * wide and tokens.shape[1] * W == TT and power_of_two(rep):
        return whole_items(tokens, *others)
    return body(tokens, *others)


def solution(mesh):
    placed = (
        P("rep", "wide", None, None),
        P("rep", "wide", None, None),
        P(),
        P(),
        P(),
        P(),
        P(),
        P(),
        P(),
        P(),
        P(),
        P(),
    )
    return jax.shard_map(
        any_size,
        mesh=mesh,
        in_specs=placed,
        out_specs=(
            P("rep", "wide", None, None),
            P("rep", "wide", None, None),
            P(),
            P(),
            P(None, "wide", None),
            P(),
            P(None, "wide", None),
            P(),
            P(None, "wide", None),
            P(),
            P(None, None, "wide"),
            P(),
        ),
        check_vma=False,
    )
```

```python
import functools
import math

import jax
import jax.numpy as jnp
import ml_dtypes
import numpy as np
from jax import lax
from jax.experimental import pallas as pl
from jax.experimental.pallas import tpu as pltpu
from jax.sharding import PartitionSpec as P

D = 512
NB = 8
BS = 64
KW = 32
KH = 32
H = 64
W = 64
LAYERS = 2


EPSILON = 1e-05
THRESHOLD = 0.1
HIGHEST = lax.Precision.HIGHEST


def dft_tables():
    col_index = jnp.arange(W, dtype=jnp.int32)
    col_freq = jnp.arange(KW, dtype=jnp.int32)
    col_phase = (col_index[:, None] * col_freq[None, :] % W).astype(jnp.float32) * (
        2.0 * math.pi / W
    )
    col_scale = 1.0 / math.sqrt(W)
    forward_cols = jnp.stack([jnp.cos(col_phase), -jnp.sin(col_phase)], axis=1) * col_scale
    doubling = jnp.where(col_freq == 0, 1.0, 2.0).astype(jnp.float32)
    inverse_cols = (
        jnp.stack(
            [jnp.cos(col_phase).T * doubling[:, None], -jnp.sin(col_phase).T * doubling[:, None]],
            axis=0,
        )
        * col_scale
    )
    row_index = jnp.arange(H, dtype=jnp.int32)
    mode_index = jnp.arange(KH, dtype=jnp.int32)
    row_freq = jnp.where(mode_index < KH // 2, mode_index, H - KH + mode_index)
    row_phase = (row_freq[:, None] * row_index[None, :] % H).astype(jnp.float32) * (
        2.0 * math.pi / H
    )
    cosine = jnp.cos(row_phase) / math.sqrt(H)
    sine = jnp.sin(row_phase) / math.sqrt(H)
    forward_rows = jnp.stack([jnp.stack([cosine, sine], -1), jnp.stack([-sine, cosine], -1)], 1)
    inverse_rows = jnp.stack(
        [jnp.stack([cosine.T, -sine.T], -1), jnp.stack([sine.T, cosine.T], -1)], 1
    )
    return (forward_cols, inverse_cols, forward_rows, inverse_rows)


def layer_norm(values, gain_row, shift_row):
    center = values - jnp.mean(values, axis=-1, keepdims=True)
    spread = jnp.mean(center * center, axis=-1, keepdims=True)
    return center * lax.rsqrt(spread + EPSILON) * gain_row + shift_row


def gelu_tanh(values):
    return jax.nn.gelu(values, approximate=True)


def shrink(values):
    return values - THRESHOLD * jnp.tanh(values / THRESHOLD)


def block_matrix(weights, onehot_low):
    picked = jnp.einsum(
        "ac,cbd->abd",
        onehot_low,
        weights.reshape(NB, BS, 2 * BS),
        preferred_element_type=jnp.float32,
    ).astype(jnp.bfloat16)
    real_part = picked[:, :, :BS]
    imag_part = picked[:, :, BS:]
    upper = jnp.concatenate([real_part, imag_part], -1)
    lower = jnp.concatenate([-imag_part, real_part], -1)
    return jnp.concatenate([upper, lower], 1)


def mode_forward(arriving, forward_rows, mixing):
    first_big, first_bias, second_big, second_bias = mixing
    item_count, pair_count = (arriving.shape[0], arriving.shape[1])
    halves = arriving.reshape(item_count, pair_count, H, 2, BS)
    mode_data = jnp.einsum(
        "jphq,iahqb->iajpb", forward_rows, halves, preferred_element_type=jnp.float32
    )
    mode_data = mode_data.reshape(item_count, pair_count, KH, 2 * BS).astype(jnp.bfloat16)
    first_pre = (
        jnp.einsum("iakc,acd->iakd", mode_data, first_big, preferred_element_type=jnp.float32)
        + first_bias[None, :, None, :]
    )
    active = gelu_tanh(first_pre).astype(jnp.bfloat16)
    second = (
        jnp.einsum("iakc,acd->iakd", active, second_big, preferred_element_type=jnp.float32)
        + second_bias[None, :, None, :]
    )
    return (mode_data, first_pre, active, second)


def mode_inverse(second, inverse_rows):
    item_count, pair_count = (second.shape[0], second.shape[1])
    shrunk = shrink(second).astype(jnp.bfloat16).reshape(item_count, pair_count, KH, 2, BS)
    rows_out = jnp.einsum(
        "hpjq,iajqb->iahpb", inverse_rows, shrunk, preferred_element_type=jnp.float32
    )
    return rows_out.reshape(item_count, pair_count, H, 2 * BS).astype(jnp.bfloat16)


def mode_backward(first_pre, second, arrived, forward_rows, inverse_rows, mixing):
    first_big, first_bias, second_big, second_bias = mixing
    item_count, pair_count = (arrived.shape[0], arrived.shape[1])
    halves = arrived.reshape(item_count, pair_count, H, 2, BS)
    d_shrunk = jnp.einsum(
        "hpjq,iahpb->iajqb", inverse_rows, halves, preferred_element_type=jnp.float32
    )
    d_shrunk = d_shrunk.reshape(item_count, pair_count, KH, 2 * BS)
    unused, shrink_pull = jax.vjp(shrink, second)
    d_second = shrink_pull(d_shrunk)[0].astype(jnp.bfloat16)
    d_active = jnp.einsum(
        "iakd,acd->iakc", d_second, second_big, preferred_element_type=jnp.float32
    )
    unused, gelu_pull = jax.vjp(gelu_tanh, first_pre)
    d_first = gelu_pull(d_active)[0].astype(jnp.bfloat16)
    d_modes = jnp.einsum(
        "iakd,acd->iakc", d_first, first_big, preferred_element_type=jnp.float32
    ).astype(jnp.bfloat16)
    d_halves = d_modes.reshape(item_count, pair_count, KH, 2, BS)
    d_rows = jnp.einsum(
        "jphq,iajpb->iahqb", forward_rows, d_halves, preferred_element_type=jnp.float32
    )
    return (
        d_rows.reshape(item_count, pair_count, H, 2 * BS).astype(jnp.bfloat16),
        d_first,
        d_second,
    )


def block_grads(inputs, grads, onehot_full):
    product = jnp.einsum("iakc,iakd->acd", inputs, grads, preferred_element_type=jnp.float32)
    real_grad = product[:, :BS, :BS] + product[:, BS:, BS:]
    imag_grad = product[:, :BS, BS:] - product[:, BS:, :BS]
    pair_grad = jnp.concatenate([real_grad, imag_grad], -1)
    weight_grad = jnp.einsum("ac,abd->cbd", onehot_full, pair_grad, precision=HIGHEST).reshape(
        D, 2 * BS
    )
    bias_terms = jnp.sum(grads.astype(jnp.float32), axis=(0, 2))
    bias_grad = jnp.dot(onehot_full.T, bias_terms, precision=HIGHEST)
    return (weight_grad, bias_grad)


def body(
    tokens,
    cotangent,
    norm_gain,
    norm_shift,
    mix_in,
    mix_in_bias,
    mix_out,
    mix_out_bias,
    w_in,
    b_in,
    w_out,
    b_out,
):
    forward_cols, inverse_cols, forward_rows, inverse_rows = [
        table_item.astype(jnp.bfloat16) for table_item in dft_tables()
    ]
    devices = lax.axis_size("wide")
    per_device = NB * KW // devices
    global_pair = lax.axis_index("wide") * per_device + jnp.arange(per_device, dtype=jnp.int32)
    onehot_full = (global_pair[:, None] // KW == jnp.arange(NB, dtype=jnp.int32)[None, :]).astype(
        jnp.float32
    )
    onehot_low = onehot_full.astype(jnp.bfloat16)
    item_count, rows_dev = (tokens.shape[0], tokens.shape[1])
    current = tokens.astype(jnp.float32)
    stored = []
    for depth_index in range(LAYERS):
        mixing = (
            block_matrix(mix_in[depth_index], onehot_low),
            jnp.dot(onehot_full, mix_in_bias[depth_index], precision=HIGHEST),
            block_matrix(mix_out[depth_index], onehot_low),
            jnp.dot(onehot_full, mix_out_bias[depth_index], precision=HIGHEST),
        )
        normed = layer_norm(current, norm_gain[depth_index, 0], norm_shift[depth_index, 0])
        spectra = jnp.einsum(
            "irwcb,wpk->ickrpb",
            normed.astype(jnp.bfloat16).reshape(item_count, rows_dev, W, NB, BS),
            forward_cols,
            preferred_element_type=jnp.float32,
        )
        spectra = spectra.reshape(item_count, NB * KW, rows_dev, 2 * BS).astype(jnp.bfloat16)
        forward_mode_data, first_pre, forward_active, second = mode_forward(
            lax.all_to_all(spectra, "wide", split_axis=1, concat_axis=2, tiled=True),
            forward_rows,
            mixing,
        )
        returning = lax.all_to_all(
            mode_inverse(second, inverse_rows), "wide", split_axis=2, concat_axis=1, tiled=True
        )
        returned = (returning,)
        back_rows = returned[0].reshape(item_count, NB, KW, rows_dev, 2, BS)
        filtered = jnp.einsum(
            "pkw,ickrpb->irwcb", inverse_cols, back_rows, preferred_element_type=jnp.float32
        )
        middle = current + filtered.reshape(item_count, rows_dev, W, D) + normed
        lowered = layer_norm(middle, norm_gain[depth_index, 1], norm_shift[depth_index, 1]).astype(
            jnp.bfloat16
        )
        hidden_pre = (
            jnp.einsum(
                "irwd,df->irwf", lowered, w_in[depth_index], preferred_element_type=jnp.float32
            )
            + b_in[depth_index]
        )
        hidden_act = gelu_tanh(hidden_pre).astype(jnp.bfloat16)
        branch = (
            jnp.einsum(
                "irwf,fd->irwd", hidden_act, w_out[depth_index], preferred_element_type=jnp.float32
            )
            + b_out[depth_index]
        )
        stored.append(
            (
                current,
                normed,
                spectra,
                middle,
                lowered,
                hidden_pre,
                hidden_act,
                mixing,
                returned[1:],
            )
        )
        current = middle + branch
    upstream = cotangent
    collected = [None] * LAYERS
    for depth_index in reversed(range(LAYERS)):
        (
            layer_input,
            normed,
            spectra,
            middle,
            lowered,
            hidden_pre,
            hidden_act,
            mixing,
            kept_modes,
        ) = stored[depth_index]
        branch_grad = upstream.astype(jnp.bfloat16)
        w_out_part = jnp.einsum(
            "irwf,irwd->fd", hidden_act, branch_grad, preferred_element_type=jnp.float32
        )
        b_out_part = jnp.sum(branch_grad.astype(jnp.float32), axis=(0, 1, 2))
        act_grad = jnp.einsum(
            "irwd,fd->irwf", branch_grad, w_out[depth_index], preferred_element_type=jnp.float32
        )
        unused, gelu_pull = jax.vjp(gelu_tanh, hidden_pre)
        pre_grad = gelu_pull(act_grad)[0].astype(jnp.bfloat16)
        w_in_part = jnp.einsum(
            "irwd,irwf->df", lowered, pre_grad, preferred_element_type=jnp.float32
        )
        b_in_part = jnp.sum(pre_grad.astype(jnp.float32), axis=(0, 1, 2))
        low_grad = jnp.einsum(
            "irwf,df->irwd", pre_grad, w_in[depth_index], preferred_element_type=jnp.float32
        )
        unused, second_norm_pull = jax.vjp(
            layer_norm, middle, norm_gain[depth_index, 1], norm_shift[depth_index, 1]
        )
        mid_norm_grad, gain_second, shift_second = second_norm_pull(low_grad)
        mid_grad = upstream + mid_norm_grad
        filt_grad = mid_grad.astype(jnp.bfloat16).reshape(item_count, rows_dev, W, NB, BS)
        back_grad = jnp.einsum(
            "pkw,irwcb->ickrpb", inverse_cols, filt_grad, preferred_element_type=jnp.float32
        )
        back_grad = back_grad.reshape(item_count, NB * KW, rows_dev, 2 * BS).astype(jnp.bfloat16)
        backward_arriving = lax.all_to_all(spectra, "wide", split_axis=1, concat_axis=2, tiled=True)
        arrived = lax.all_to_all(back_grad, "wide", split_axis=1, concat_axis=2, tiled=True)
        backward_mode_data, backward_first_pre, backward_active, backward_second = mode_forward(
            backward_arriving, forward_rows, mixing
        )
        d_rows, d_first, d_second = mode_backward(
            backward_first_pre, backward_second, arrived, forward_rows, inverse_rows, mixing
        )
        sent_back = lax.all_to_all(d_rows, "wide", split_axis=2, concat_axis=1, tiled=True)
        col_grad, mode_data, active, d_first, d_second = (
            sent_back,
            backward_mode_data,
            backward_active,
            d_first,
            d_second,
        )
        mix_in_part, mix_in_bias_part = block_grads(mode_data, d_first, onehot_full)
        mix_out_part, mix_out_bias_part = block_grads(active, d_second, onehot_full)
        col_grad = col_grad.reshape(item_count, NB, KW, rows_dev, 2, BS)
        normed_grad = jnp.einsum(
            "wpk,ickrpb->irwcb", forward_cols, col_grad, preferred_element_type=jnp.float32
        )
        normed_grad = normed_grad.reshape(item_count, rows_dev, W, D) + mid_grad
        unused, first_norm_pull = jax.vjp(
            layer_norm, layer_input, norm_gain[depth_index, 0], norm_shift[depth_index, 0]
        )
        input_part, gain_first, shift_first = first_norm_pull(normed_grad)
        upstream = mid_grad + input_part
        collected[depth_index] = (
            jnp.stack([gain_first, gain_second]),
            jnp.stack([shift_first, shift_second]),
            mix_in_part,
            mix_in_bias_part,
            mix_out_part,
            mix_out_bias_part,
            w_in_part,
            b_in_part,
            w_out_part,
            b_out_part,
        )
    stacked = [
        jnp.stack([collected[depth_index][slot] for depth_index in range(LAYERS)])
        for slot in range(10)
    ]
    small_grads = lax.psum(
        (stacked[0], stacked[1], stacked[3], stacked[5], stacked[7], stacked[9]), ("wide", "rep")
    )
    large_grads = (stacked[2], stacked[4], stacked[6], stacked[8])
    pieces = (
        lax.psum_scatter(large_grads[0], "wide", scatter_dimension=1, tiled=True),
        lax.psum_scatter(large_grads[1], "wide", scatter_dimension=1, tiled=True),
        lax.psum_scatter(large_grads[2], "wide", scatter_dimension=1, tiled=True),
        lax.psum_scatter(large_grads[3], "wide", scatter_dimension=2, tiled=True),
    )
    pieces = (
        lax.psum(pieces[0].astype(jnp.bfloat16), "rep").astype(jnp.float32),
        lax.psum(pieces[1].astype(jnp.bfloat16), "rep").astype(jnp.float32),
        lax.psum(pieces[2].astype(jnp.bfloat16), "rep").astype(jnp.float32),
        lax.psum(pieces[3].astype(jnp.bfloat16), "rep").astype(jnp.float32),
    )
    return (
        current,
        upstream,
        small_grads[0],
        small_grads[1],
        pieces[0],
        small_grads[2],
        pieces[1],
        small_grads[3],
        pieces[2],
        small_grads[4],
        pieces[3],
        small_grads[5],
    )


BF = jnp.bfloat16
F32 = jnp.float32
FF = 2048
GROUPS = 4
GELU_A = math.sqrt(2.0 / math.pi)
GELU_B = GELU_A * 0.044715
HB = 16
KB = 16
TT = 512
FC = 1024
VMEM = 58 * 1024 * 1024


def plain_tables():
    def low(table):
        return table.astype(np.float32).astype(ml_dtypes.bfloat16).astype(np.float64)

    index = np.arange(64)
    col_phase = 2.0 * np.pi * ((index[:, None] * np.arange(KW)[None, :]) % W) / W
    forward_cols = np.stack([np.cos(col_phase), -np.sin(col_phase)], axis=1) / math.sqrt(W)
    doubling = np.where(np.arange(KW) == 0, 1.0, 2.0)[:, None]
    inverse_cols = (
        np.stack([np.cos(col_phase).T * doubling, -np.sin(col_phase).T * doubling], axis=0)
        / math.sqrt(W)
    )
    modes = np.arange(KH)
    row_freq = np.where(modes < KH // 2, modes, H - KH + modes)
    row_phase = 2.0 * np.pi * ((row_freq[:, None] * index[None, :]) % H) / H
    cosine = np.cos(row_phase) / math.sqrt(H)
    sine = np.sin(row_phase) / math.sqrt(H)
    forward_rows = np.stack([np.stack([cosine, sine], -1), np.stack([-sine, cosine], -1)], 1)
    inverse_rows = np.stack(
        [np.stack([cosine.T, -sine.T], -1), np.stack([sine.T, cosine.T], -1)], 1
    )
    return [low(table) for table in (forward_cols, inverse_cols, forward_rows, inverse_rows)]


def matrix_tables():
    forward_cols, inverse_cols, forward_rows, inverse_rows = plain_tables()
    eye = np.eye(4)
    into = np.einsum("wpk,gh->kpghw", forward_cols, eye).reshape(256, 256)
    outof = np.einsum("pkw,gh->gwkph", inverse_cols, eye).reshape(256, 256)
    pair = np.eye(2)
    forward_rows = forward_rows.reshape(KH, 2, H // 4, 4, 2)
    inverse_rows = inverse_rows.reshape(H // 4, 4, 2, KH, 2)
    rows_in = np.einsum("jphsq,ab->apjbhqs", forward_rows, pair).reshape(128, 256)
    rows_out = np.einsum("hspjq,ab->ahpsbqj", inverse_rows, pair).reshape(256, 128)
    return [
        jnp.asarray(np.ascontiguousarray(table).astype(ml_dtypes.bfloat16))
        for table in (into, outof, rows_in, rows_out, outof.T, into.T, rows_out.T, rows_in.T)
    ]


def big_matrices(weight):
    four = weight.reshape(GROUPS, 2, BS, 2, BS)
    eye = jnp.eye(2, dtype=weight.dtype)
    real = (four[:, :, :, 0][:, :, :, None, :] * eye[None, :, None, :, None]).reshape(
        GROUPS, 128, 128
    )
    imag = (four[:, :, :, 1][:, :, :, None, :] * eye[None, :, None, :, None]).reshape(
        GROUPS, 128, 128
    )
    upper = jnp.concatenate([real, imag], -1)
    lower = jnp.concatenate([-imag, real], -1)
    return jnp.concatenate([upper, lower], 1)


def big_bias(bias):
    return bias.reshape(GROUPS, 2, 2, BS).transpose(0, 2, 1, 3).reshape(GROUPS, 1, 256)


def small_bias(line):
    parts = line.reshape(-1, GROUPS, 2, 2, BS).transpose(0, 1, 3, 2, 4)
    return parts.reshape(-1, NB, 2 * BS)


def mm(left, right):
    return jnp.dot(left, right, preferred_element_type=F32)


def mm_t(left, right):
    return lax.dot_general(left, right, (((1,), (1,)), ((), ())), preferred_element_type=F32)


def normalize(values):
    center = values - jnp.mean(values, axis=-1, keepdims=True)
    spread = jnp.mean(center * center, axis=-1, keepdims=True)
    scale = lax.rsqrt(spread + EPSILON)
    return center * scale, scale


def normalize_back(grad, unit, scale, gain_row):
    inner = grad * gain_row
    return scale * (
        inner
        - jnp.mean(inner, axis=-1, keepdims=True)
        - unit * jnp.mean(inner * unit, axis=-1, keepdims=True)
    )


def folded(values):
    return jnp.sum(values.reshape(values.shape[0] // 8, 8, values.shape[1]), axis=0)


def gelu_of(v):
    return 0.5 * v * (1.0 + jnp.tanh(v * (GELU_A + GELU_B * (v * v))))


def gelu_and_slope(v):
    square = v * v
    bend = jnp.tanh(v * (GELU_A + GELU_B * square))
    half = 0.5 * (1.0 + bend)
    slope = half + 0.5 * v * (1.0 - bend * bend) * (GELU_A + 3.0 * GELU_B * square)
    return v * half, slope


def cols_in(table, rows, store, block):
    parts = [
        mm(table, rows[at * 256 : at * 256 + 256]).reshape(KW, 8, D) for at in range(HB // 4)
    ]
    store[:, pl.ds(pl.multiple_of(block * 2 * HB, 2 * HB), 2 * HB), :] = jnp.concatenate(
        parts, axis=1
    ).astype(BF)


def cols_out(table, store, block):
    part = store[:, pl.ds(pl.multiple_of(block * 2 * HB, 2 * HB), 2 * HB), :].astype(F32)
    return jnp.concatenate(
        [
            mm(table, part[:, at * 8 : at * 8 + 8].reshape(256, D).astype(BF))
            for at in range(HB // 4)
        ],
        axis=0,
    )


def lanes_of(rows, group):
    lanes = slice(group * 128, group * 128 + 128)
    return jnp.concatenate(
        [rows[:, :32, lanes].reshape(KB * 32, 128), rows[:, 32:, lanes].reshape(KB * 32, 128)],
        axis=1,
    )


def put_lanes(store, group, values):
    lanes = slice(group * 128, group * 128 + 128)
    store[:, :32, lanes] = values[:, :128].reshape(KB, 32, 128)
    store[:, 32:, lanes] = values[:, 128:].reshape(KB, 32, 128)


def spectral_forward_kernel(
    x_ref, gain, shift, into, outof, rows_in, rows_out, w1, b1, w2, b2, mid_ref, spec_ref,
    cols, mixed, held,
):
    step = pl.program_id(0)
    n_rows, n_freq = H // HB, KW // KB

    @pl.when(step < n_rows)
    def _():
        x = lines_of(x_ref)
        held[step] = x
        unit, _ = normalize(x.astype(F32))
        normed = unit * gain[...] + shift[...]
        cols_in(into[...], normed.astype(BF), cols, step)

    @pl.when((step >= n_rows) & (step < n_rows + n_freq))
    def _():
        first_plane = (step - n_rows) * KB
        for two in range(KB // 2):
            planes = cols[pl.ds(first_plane + 2 * two, 2)]
            spec_ref[2 * two : 2 * two + 2] = (
                mm(rows_in[...], planes.reshape(256, D)).astype(BF).reshape(2, 64, D)
            )
        modes = spec_ref[...]
        for group in range(GROUPS):
            first = mm(lanes_of(modes, group), w1[group]) + b1[group]
            second = mm(gelu_of(first).astype(BF), w2[group]) + b2[group]
            shrunk = second - THRESHOLD * jnp.tanh(second * (1.0 / THRESHOLD))
            put_lanes(mixed, group, shrunk.astype(BF))
        for two in range(KB // 2):
            planes = mixed[2 * two : 2 * two + 2].reshape(128, D)
            cols[pl.ds(first_plane + 2 * two, 2)] = (
                mm(rows_out[...], planes).astype(BF).reshape(2, 128, D)
            )

    @pl.when(step >= n_rows + n_freq)
    def _():
        block = step - n_rows - n_freq
        x = held[block].astype(F32)
        unit, _ = normalize(x)
        normed = unit * gain[...] + shift[...]
        filtered = cols_out(outof[...], cols, block)
        mid_ref[...] = (x + filtered + normed).astype(mid_ref.dtype)


def compact(big):
    low_lanes = lax.broadcasted_iota(jnp.int32, (BS, 128), 1) < BS
    parts = []
    for c in range(2):
        real_rows, imag_rows = slice(c * BS, c * BS + BS), slice(128 + c * BS, 128 + c * BS + BS)
        real = big[real_rows, :128] + big[imag_rows, 128:]
        imag = big[real_rows, 128:] - big[imag_rows, :128]
        if c == 0:
            parts.append(jnp.where(low_lanes, real, pltpu.roll(imag, BS, 1)))
        else:
            parts.append(jnp.where(low_lanes, pltpu.roll(real, BS, 1), imag))
    return jnp.concatenate(parts, axis=0)


def spectral_backward_kernel(with_start, *refs):
    (
        x_ref, grad_ref, spec_ref, gain, outof_t, into_t, rows_out_t, rows_in_t,
        w1, b1, w2, b2, w1_t, w2_t,
    ), refs = refs[:14], refs[14:]
    starts, refs = refs[:2] if with_start else (), refs[2:] if with_start else refs
    new_ref, blocks, lines, dw1, dw2, cols, mixed, kept, held = refs
    step = pl.program_id(0)
    n_rows, n_freq = H // HB, KW // KB

    @pl.when(step == 0)
    def _():
        lines[...] = starts[1][...] if with_start else jnp.zeros_like(lines)
        for ref in (dw1, dw2):
            ref[...] = jnp.zeros_like(ref)

    @pl.when(step < n_rows)
    def _():
        grad = grad_ref[...]
        held[step] = grad
        cols_in(outof_t[...], grad, cols, step)

    @pl.when((step >= n_rows) & (step < n_rows + n_freq))
    def _():
        first_plane = (step - n_rows) * KB
        for two in range(KB // 2):
            planes = cols[pl.ds(first_plane + 2 * two, 2)]
            kept[2 * two : 2 * two + 2] = mm(rows_out_t[...], planes.reshape(256, D)).reshape(
                2, 64, D
            )
        modes = spec_ref[...]
        grads = kept[...]
        for group in range(GROUPS):
            mode = lanes_of(modes, group)
            first = mm(mode, w1[group]) + b1[group]
            active, slope = gelu_and_slope(first)
            active = active.astype(BF)
            second = mm(active, w2[group]) + b2[group]
            bend = jnp.tanh(second * (1.0 / THRESHOLD))
            d_second = bend * bend * lanes_of(grads, group)
            at = slice(group * 256, group * 256 + 256)
            lines[:, 1024 + group * 256 : 1280 + group * 256] += folded(d_second)
            d_second = d_second.astype(BF)
            dw2[group] += mm(active.T, d_second)
            d_first = slope * mm(d_second, w2_t[group])
            lines[:, at] += folded(d_first)
            d_first = d_first.astype(BF)
            dw1[group] += mm(mode.T, d_first)
            put_lanes(mixed, group, mm(d_first, w1_t[group]).astype(BF))
        for two in range(KB // 2):
            planes = mixed[2 * two : 2 * two + 2].reshape(128, D)
            cols[pl.ds(first_plane + 2 * two, 2)] = (
                mm(rows_in_t[...], planes).astype(BF).reshape(2, 128, D)
            )

    @pl.when(step == n_rows + n_freq)
    def _():
        for group in range(GROUPS):
            at = slice(group * 128, group * 128 + 128)
            for slot, ref in enumerate((dw1, dw2)):
                lanes = slice(slot * 128, slot * 128 + 128)
                block = compact(ref[group])
                blocks[at, lanes] = block + starts[0][at, lanes] if with_start else block

    @pl.when(step >= n_rows + n_freq)
    def _():
        block = step - n_rows - n_freq
        unit, scale = normalize(lines_of(x_ref).astype(F32))
        mid_grad = held[block].astype(F32)
        grad = cols_out(into_t[...], cols, block) + mid_grad
        lines[:, 2048:2560] += folded(grad * unit)
        lines[:, 2560:3072] += folded(grad)
        new = mid_grad + normalize_back(grad, unit, scale, gain[...])
        new_ref[...] = new.astype(new_ref.dtype)


def feed_forward_kernel(mid_ref, gain, shift, w_in, b_in, w_out, b_out, *refs):
    out_ref, pre_ref = refs[-2:]
    middle = mid_ref[...].astype(F32)
    unit, _ = normalize(middle)
    lowered = (unit * gain[...] + shift[...]).astype(BF)
    total = middle + b_out[...]
    for part in range(FF // FC):
        at = slice(part * FC, part * FC + FC)
        pre = mm(lowered, w_in[:, at]) + b_in[:, at]
        pre = pre.astype(BF)
        pre_ref[:, at] = pre
        total += mm(gelu_of(pre), w_out[at, :])
    out_ref[...] = total.astype(out_ref.dtype)


def feed_backward_kernel(with_start, *refs):
    (g_ref, mid_ref, pre_ref, gain, shift, w_out, w_in), refs = refs[:7], refs[7:]
    if with_start:
        (start_far, start_lines, side, mid_grad_ref, kept, sent, lines, dw, start, arrival) = refs
        copy = pltpu.make_async_copy(start_far, start, arrival)
    else:
        mid_grad_ref, dw, lines = refs
    step = pl.program_id(0)

    @pl.when(step == 0)
    def _():
        lines[...] = start_lines[...] if with_start else jnp.zeros_like(lines)
        dw[...] = jnp.zeros_like(dw)
        if with_start:
            copy.start()

    upstream = lines_of(g_ref)
    unit, scale = normalize(mid_ref[...].astype(F32))
    lowered = (unit * gain[...] + shift[...]).astype(BF)
    lines[:, FF : FF + D] += folded(upstream.astype(F32))
    upstream_t = upstream.T
    lowered_t = lowered.T
    low_grad = jnp.zeros((TT, D), F32)
    for part in range(FF // FC):
        at = slice(part * FC, part * FC + FC)
        active, slope = gelu_and_slope(pre_ref[:, at])
        dw[:, FF + part * FC : FF + part * FC + FC] += mm(upstream_t, active)
        pre_grad = slope * mm_t(upstream, w_out[at, :]).astype(BF)
        lines[:, at] += folded(pre_grad.astype(F32))
        dw[:, at] += mm(lowered_t, pre_grad)
        low_grad += mm_t(pre_grad, w_in[:, at])
    lines[:, FF + D : FF + 2 * D] += folded(low_grad * unit)
    lines[:, FF + 2 * D : FF + 3 * D] += folded(low_grad)
    new = upstream.astype(F32) + normalize_back(low_grad, unit, scale, gain[...])
    mid_grad_ref[...] = new.astype(mid_grad_ref.dtype)
    if with_start:

        @pl.when(step == H * W // TT - 1)
        def _():
            copy.wait()
            for ref, half in ((kept, side[0]), (sent, 1 - side[0])):
                at = pl.ds(pl.multiple_of(half * FF, FF), FF)
                ref[...] = (dw[:, at] + start[:, at]).astype(BF)


def whole(array):
    zeros = (0,) * array.ndim
    return pl.BlockSpec(array.shape, lambda *_: zeros, pipeline_mode=pl.Buffered(1))


def of_layer(array, layer):
    at = (layer,) + (0,) * (array.ndim - 1)
    return pl.BlockSpec((None, *array.shape[1:]), lambda *_: at, pipeline_mode=pl.Buffered(1))


def rows_spec(rows, block_of, array=None, kind=None):
    if kind is None:
        return pl.BlockSpec((rows * W, D), lambda s: (block_of(s), 0))
    own = array.shape[2]
    return pl.BlockSpec((rows * W // own, None, own, D), lambda s: (block_of(s), kind, 0, 0))


def lines_of(ref):
    return ref[...].reshape(-1, D)


PARAMS = pltpu.CompilerParams(dimension_semantics=("arbitrary",), vmem_limit_bytes=VMEM)


def cost(microseconds):
    return pl.CostEstimate(
        flops=microseconds * 400_000_000, bytes_accessed=1_000_000, transcendentals=0
    )


N_ROWS, N_FREQ = H // HB, KW // KB
SPECTRAL_STEPS = 2 * N_ROWS + N_FREQ


def first_end(step):
    return jnp.minimum(step, N_ROWS - 1)


def last_end(step):
    return jnp.maximum(step - N_ROWS - N_FREQ, 0)


def middle_part(step):
    return jnp.clip(step - N_ROWS, 0, N_FREQ - 1)


def spectral_forward(x, kind, gain, shift, tables, mix):
    small = (gain, shift, *tables[:4], *mix[:4])
    return pl.pallas_call(
        spectral_forward_kernel,
        grid=(SPECTRAL_STEPS,),
        in_specs=[rows_spec(HB, first_end, x, kind)] + [whole(array) for array in small],
        out_specs=[
            rows_spec(HB, last_end),
            pl.BlockSpec((KB, 64, D), lambda s: (middle_part(s), 0, 0)),
        ],
        out_shape=[
            jax.ShapeDtypeStruct((H * W, D), BF),
            jax.ShapeDtypeStruct((KW, 64, D), BF),
        ],
        scratch_shapes=[
            pltpu.VMEM((KW, 128, D), BF),
            pltpu.VMEM((KB, 64, D), BF),
            pltpu.VMEM((N_ROWS, HB * W, D), BF),
        ],
        compiler_params=PARAMS,
        cost_estimate=cost(16),
        name="spectral_forward",
    )(x, *small)


def spectral_backward(x, kind, grad, spec, gain, tables, mix, start):
    small = (gain, *tables[4:], *mix, *start)
    sums = [(D, 256), (8, 3072)]
    return pl.pallas_call(
        functools.partial(spectral_backward_kernel, len(start) > 0),
        grid=(SPECTRAL_STEPS,),
        in_specs=[
            rows_spec(HB, last_end, x, kind),
            rows_spec(HB, first_end),
            pl.BlockSpec((KB, 64, D), lambda s: (middle_part(s), 0, 0)),
        ]
        + [whole(array) for array in small],
        out_specs=[rows_spec(HB, last_end)] + [pl.BlockSpec(dims, lambda s: (0, 0)) for dims in sums],
        out_shape=[jax.ShapeDtypeStruct((H * W, D), BF)]
        + [jax.ShapeDtypeStruct(dims, F32) for dims in sums],
        scratch_shapes=[
            pltpu.VMEM((GROUPS, 256, 256), F32),
            pltpu.VMEM((GROUPS, 256, 256), F32),
            pltpu.VMEM((KW, 128, D), BF),
            pltpu.VMEM((KB, 64, D), BF),
            pltpu.VMEM((KB, 64, D), F32),
            pltpu.VMEM((N_ROWS, HB * W, D), BF),
        ],
        compiler_params=PARAMS,
        cost_estimate=cost(24),
        name="spectral_backward",
    )(x, grad, spec, *small)


def feed_forward(middle, layer, gain, shift, w_in, b_in, w_out, b_out, abroad=None, onto=None):
    rows = rows_spec(TT // W, lambda s: s)
    shape = jax.ShapeDtypeStruct((H * W, D), BF)
    if abroad is not None:
        receivers, chunks, own, chunk = abroad
        shape = jax.ShapeDtypeStruct((receivers, chunks, own * W, D), BF)
        rows = pl.BlockSpec((None, None, TT, D), lambda s: (s, chunk, 0, 0))
    more = [] if onto is None else [onto]
    return pl.pallas_call(
        feed_forward_kernel,
        grid=(H * W // TT,),
        in_specs=[
            rows_spec(TT // W, lambda s: s),
            whole(gain),
            whole(shift),
            of_layer(w_in, layer),
            whole(b_in),
            of_layer(w_out, layer),
            whole(b_out),
        ]
        + [pl.BlockSpec(memory_space=pl.ANY) for _ in more],
        out_specs=[rows, pl.BlockSpec((TT, FF), lambda s: (s, 0))],
        out_shape=[shape, jax.ShapeDtypeStruct((H * W, FF), BF)],
        input_output_aliases={7: 0} if more else {},
        compiler_params=PARAMS,
        cost_estimate=cost(24),
        name="feed_forward",
    )(middle, gain, shift, w_in, b_in, w_out, b_out, *more)


def feed_backward(g, kind, middle, pre, layer, gain, shift, w_out, w_in, start, side):
    matrices, lines = (D, 2 * FF), (8, FF + 3 * D)
    halves = [(D, FF), (D, FF)]
    sums = [(dims, BF) for dims in halves] if start else [(matrices, F32)]
    sums.append((lines, F32))
    return pl.pallas_call(
        functools.partial(feed_backward_kernel, len(start) > 0),
        grid=(H * W // TT,),
        in_specs=[
            rows_spec(TT // W, lambda s: s, g, kind),
            rows_spec(TT // W, lambda s: s),
            pl.BlockSpec((TT, FF), lambda s: (s, 0)),
            whole(gain),
            whole(shift),
            of_layer(w_out, layer),
            of_layer(w_in, layer),
        ]
        + (
            [
                pl.BlockSpec(memory_space=pl.ANY),
                whole(start[1]),
                pl.BlockSpec(memory_space=pltpu.SMEM),
            ]
            if start
            else []
        ),
        out_specs=[rows_spec(TT // W, lambda s: s)]
        + [pl.BlockSpec(dims, lambda s: (0, 0)) for dims, _ in sums],
        out_shape=[jax.ShapeDtypeStruct((H * W, D), BF)]
        + [jax.ShapeDtypeStruct(dims, kind_of) for dims, kind_of in sums],
        scratch_shapes=[
            pltpu.VMEM(matrices, F32),
            pltpu.VMEM(matrices, F32),
            pltpu.SemaphoreType.DMA,
        ]
        if start
        else [],
        compiler_params=PARAMS,
        cost_estimate=cost(49),
        name="feed_backward",
    )(g, middle, pre, gain, shift, w_out, w_in, *start, *([side] if start else []))


def widen_kernel(part, *refs):
    refs[-1][...] = part[...].astype(F32)


def widened(part, chunk, chunks, onto):
    items, parts = part.shape[:2]
    block = (None, None, *part.shape[2:])
    more = [] if onto is None else [onto]
    return pl.pallas_call(
        widen_kernel,
        grid=(parts, items),
        in_specs=[pl.BlockSpec(block, lambda p, s: (s, p, 0, 0, 0))]
        + [pl.BlockSpec(memory_space=pl.ANY) for _ in more],
        out_specs=pl.BlockSpec(block, lambda p, s: (chunk + p, s, 0, 0, 0)),
        out_shape=jax.ShapeDtypeStruct((chunks, items, *part.shape[2:]), F32),
        input_output_aliases={1: 0} if more else {},
        compiler_params=pltpu.CompilerParams(
            dimension_semantics=("arbitrary", "arbitrary"), vmem_limit_bytes=VMEM
        ),
        cost_estimate=cost(0),
        name="widen",
    )(part, *more)


def exchange(array):
    return lax.all_to_all(array, "wide", split_axis=0, concat_axis=0, tiled=True)


def after(array, other):
    return lax.optimization_barrier((array, other))[0]


def swapped(array, axis_name, far):
    size = lax.axis_size(axis_name)
    return lax.ppermute(array, axis_name, [(i, i ^ far) for i in range(size)])


def share(array, index, size, axis):
    return lax.dynamic_slice_in_dim(array, index * size, size, axis)


def own_bit(axis_name, bit):
    return (lax.axis_index(axis_name) >> bit) & 1


def halves(array, side, axis):
    half = array.shape[axis] // 2
    return share(array, side, half, axis), share(array, 1 - side, half, axis)


def row_halves(array, bit, shard):
    blocks = array.reshape(-1, 2, shard, array.shape[1])
    return [half.reshape(-1, array.shape[1]) for half in halves(blocks, own_bit("wide", bit), 1)]


def traded(kept, sent, axis_name, bit, behind=()):
    arrived = swapped(sent.astype(BF), axis_name, 1 << bit)
    return after(kept, behind).astype(F32) + arrived.astype(F32)


def traded_with(kept, sent, extra, axis_name, bit, behind=()):
    extra = extra.astype(BF)
    message = jnp.concatenate([sent.astype(BF), extra.reshape(-1, sent.shape[1])], axis=0)
    arrived = swapped(message, axis_name, 1 << bit).astype(F32)
    rows = sent.shape[0]
    return (
        after(kept, behind).astype(F32) + arrived[:rows],
        extra.astype(F32) + arrived[rows:].reshape(extra.shape),
    )


def side_by_side(own, other, bit):
    first = own_bit("rep", bit) == 0
    return jnp.concatenate(
        [jnp.where(first, own, other), jnp.where(first, other, own)], axis=1
    )


def whole_items(
    tokens, cotangent, norm_gain, norm_shift, mix_in, mix_in_bias, mix_out, mix_out_bias,
    w_in, b_in, w_out, b_out,
):
    wide = lax.axis_size("wide")
    chunks = tokens.shape[0] // wide
    abroad = (wide, *tokens.shape[1:])

    def rows_by_layer(array):
        return [array[layer].reshape(-1, 1, array.shape[-1]) for layer in range(LAYERS)]

    lines = [
        [[line for line in group] for group in rows_by_layer(array)]
        for array in (norm_gain, norm_shift, b_in, b_out)
    ]

    tables = matrix_tables()
    mixes = []
    for layer in range(LAYERS):
        first_mats, second_mats = big_matrices(mix_in[layer]), big_matrices(mix_out[layer])
        mixes.append(
            (
                first_mats,
                big_bias(mix_in_bias[layer]),
                second_mats,
                big_bias(mix_out_bias[layer]),
                first_mats.transpose(0, 2, 1),
                second_mats.transpose(0, 2, 1),
            )
        )

    stored = {}
    feed_sums = [()] * LAYERS
    mix_sums = [()] * LAYERS
    tie = lax.optimization_barrier

    def rows_of(array, chunk):
        return array[chunk * wide : chunk * wide + wide].astype(BF)

    def forward(chunk, current, kind, onto):
        for layer in range(LAYERS):
            middle, spec = spectral_forward(
                current, kind, gains[layer][0], shifts[layer][0], tables, mixes[layer]
            )
            last = layer == LAYERS - 1
            following, pre = feed_forward(
                middle, layer, gains[layer][1], shifts[layer][1], w_in,
                in_biases[layer][0], w_out, out_biases[layer][0],
                abroad=(wide, chunks, tokens.shape[1], chunk) if last else None,
                onto=onto if last else None,
            )
            stored[layer, chunk] = (current, kind, middle, spec, pre)
            current, kind = following, None
        return current

    def backward_feed(chunk, layer, grad, kind=None):
        _, _, middle, _, pre = stored[layer, chunk]
        mid_grad, *feed_sums[layer] = feed_backward(
            grad, kind, middle, pre, layer, gains[layer][1], shifts[layer][1], w_out, w_in,
            feed_sums[layer], side,
        )
        return mid_grad

    def backward_spectral(chunk, layer, mid_grad):
        layer_input, kind, _, spec, _ = stored[layer, chunk]
        grad, *mix_sums[layer] = spectral_backward(
            layer_input, kind, mid_grad, spec, gains[layer][0], tables, mixes[layer], mix_sums[layer]
        )
        return grad

    def backward(chunk, layer, grad):
        return backward_spectral(chunk, layer, backward_feed(chunk, layer, grad))

    def as_item(array):
        return array.reshape(H * W, D)

    def one_part(array):
        return array.reshape(wide, 1, *tokens.shape[1:])

    def both(first, second):
        return jnp.stack([first, second], axis=1).reshape(wide, 2, -1, D)

    sent, tokens_here, cotangent_here = tie((rows_of(tokens, 0), tokens, cotangent))
    arrived = exchange(sent)
    arrived, mixes, lines, sent, later = tie(
        (
            arrived,
            mixes,
            lines,
            rows_of(cotangent_here, 0),
            both(rows_of(tokens_here, 1), rows_of(cotangent_here, 1)),
        )
    )
    gains, shifts, in_biases, out_biases = lines
    upstream = exchange(sent)
    wide_at, rep_at = lax.axis_index("wide"), lax.axis_index("rep")
    side = (rep_at & 1).astype(jnp.int32).reshape(1)
    output = forward(0, as_item(arrived), None, None)

    upstream, output, later = tie((upstream, output, later))
    arrived = exchange(later)
    grad = backward(0, 1, as_item(upstream))
    grad = backward(0, 0, grad)

    grad, arrived, output = tie((grad, arrived, output))
    returned = exchange(grad.reshape(abroad))
    output = forward(1, arrived, 0, output)

    returned, output, arrived = tie((returned, output, arrived))
    delivered = exchange(output)
    mid_grad = backward_feed(1, 1, arrived, 1)
    shard = D // wide
    last_kept, last_sent = feed_sums[1][:2]
    grad = backward_spectral(1, 1, mid_grad)
    last_sum, grad = tie((traded(last_kept, last_sent, "rep", 0, grad), grad))
    mid_grad = backward_feed(1, 0, grad)
    kept, sent = halves(last_sum, own_bit("rep", 1), 1)
    last_sum, mid_grad, ready = tie(
        (traded(kept, sent, "rep", 1, mid_grad), mid_grad, feed_sums[0][:2])
    )
    first_sum = traded(*ready, "rep", 0)
    first_sum, mid_grad = tie((first_sum, mid_grad))
    grad = backward_spectral(1, 0, mid_grad)
    kept, sent = row_halves(last_sum, 0, shard)
    last_sum = traded(kept, sent, "wide", 0, grad)
    kept, sent = halves(first_sum, own_bit("rep", 1), 1)
    first_sum = traded(kept, sent, "rep", 1, grad)

    last_sum, first_sum, grad, feed_sums, mix_sums = tie(
        (last_sum, first_sum, grad, feed_sums, mix_sums)
    )
    last_kept, last_sent = row_halves(last_sum, 1, shard)
    kept, sent = row_halves(first_sum, 0, shard)
    first_sum = traded(kept, sent, "wide", 0)
    delivered, grad, returned_first, first_sum, feed_sums, mix_sums = tie(
        (delivered, grad, returned, first_sum, feed_sums, mix_sums)
    )
    returned = exchange(grad.reshape(abroad))
    lines = jnp.stack(
        [
            jnp.concatenate([jnp.sum(sums[layer][-1], axis=0) for sums in (feed_sums, mix_sums)])
            for layer in range(LAYERS)
        ]
    )
    lines_size = lines.size
    kept, sent = (
        jnp.concatenate(each, axis=1)
        for each in zip(*[halves(sums[0], own_bit("rep", 0), 1) for sums in mix_sums])
    )
    lines = jnp.pad(lines.reshape(-1), (0, -lines_size % (16 * sent.shape[1])))
    blocks, lines = traded_with(kept, sent, lines, "rep", 0)
    last_sum = traded(last_kept, last_sent, "wide", 1, blocks)
    blocks, returned_first, delivered = tie((blocks, returned_first, delivered))
    input_grad = widened(one_part(returned_first), 0, chunks, None)
    output = widened(
        delivered.reshape(wide, chunks, *tokens.shape[1:]), 0, chunks, None
    ).reshape(tokens.shape)
    kept, sent = row_halves(blocks, 0, shard)
    blocks, lines = traded_with(kept, sent, lines, "wide", 0)
    high_kept, high_sent = row_halves(blocks, 1, shard)
    kept, sent = row_halves(first_sum, 1, shard)
    first_sum = traded(kept, sent, "wide", 1, (high_sent, lines))
    kept, sent = row_halves(first_sum, 2, shard)
    first_sum = traded(kept, sent, "wide", 2)
    kept, sent = row_halves(last_sum, 2, shard)
    last_sum = traded(kept, sent, "wide", 2, first_sum)
    blocks, lines = traded_with(high_kept, high_sent, lines, "wide", 1)
    kept, sent = row_halves(blocks, 2, shard)
    blocks, lines = traded_with(kept, sent, lines, "wide", 2)
    returned, output, input_grad, first_sum, last_sum, blocks, lines = tie(
        (returned, output, input_grad, first_sum, last_sum, blocks, lines)
    )
    chain = jnp.concatenate([first_sum, blocks], axis=1)
    columns = last_sum.shape[1]
    part = lines.size // shard
    lines = lines.astype(BF)
    message = jnp.concatenate(
        [chain[:, :columns], last_sum, chain[:, columns:], lines.reshape(shard, part)], axis=1
    ).astype(BF)
    arrived = swapped(message, "rep", 2)
    input_grad = widened(one_part(returned), 1, chunks, input_grad).reshape(tokens.shape)
    arrived, input_grad = tie((arrived, input_grad))
    first_sum, last_sum = (
        side_by_side(message[:, at : at + columns], arrived[:, at : at + columns], 1)
        for at in (0, columns)
    )
    blocks = message[:, 2 * columns : -part].astype(F32) + arrived[:, 2 * columns : -part].astype(F32)
    lines = lines.astype(F32) + arrived[:, -part:].astype(F32).reshape(-1)
    packed = lines[:lines_size].reshape(LAYERS, -1)
    message = jnp.concatenate([first_sum, last_sum, blocks.astype(BF)], axis=1)
    arrived = swapped(message, "rep", 1)
    b_in_grad, b_out_grad, gain_two, shift_two, in_bias, out_bias, gain_one, shift_one = (
        jnp.split(packed, np.cumsum([FF, D, D, D, 1024, 1024, D]), axis=1)
    )
    gain_grad, shift_grad = (
        jnp.stack(pair, axis=1) for pair in ((gain_one, gain_two), (shift_one, shift_two))
    )
    in_bias_grad, out_bias_grad = small_bias(in_bias), small_bias(out_bias)
    arrived, gain_grad, shift_grad, in_bias_grad, out_bias_grad, b_in_grad, b_out_grad = tie(
        (arrived, gain_grad, shift_grad, in_bias_grad, out_bias_grad, b_in_grad, b_out_grad)
    )
    matrices = [
        side_by_side(message[:, at : at + 2 * columns], arrived[:, at : at + 2 * columns], 0).astype(
            F32
        )
        for at in (0, 2 * columns)
    ]
    blocks = side_by_side(message[:, 4 * columns :], arrived[:, 4 * columns :], 0).astype(F32)
    mix_grads = blocks.reshape(shard, 2, LAYERS, 2 * BS).transpose(1, 2, 0, 3)
    w_in_grad = jnp.stack([matrix[:, :FF] for matrix in matrices])
    w_out_grad = jnp.stack([matrix[:, FF:].T for matrix in matrices])

    return (
        output, input_grad, gain_grad, shift_grad, mix_grads[0], in_bias_grad,
        mix_grads[1], out_bias_grad, w_in_grad, b_in_grad, w_out_grad, b_out_grad,
    )


def any_size(tokens, *others):
    wide, rep = lax.axis_size("wide"), lax.axis_size("rep")
    if tokens.shape[0] == 2 * wide and tokens.shape[1] * W == TT and rep == 4 and wide == 8:
        return whole_items(tokens, *others)
    return body(tokens, *others)


def solution(mesh):
    placed = (
        P("rep", "wide", None, None),
        P("rep", "wide", None, None),
        P(),
        P(),
        P(),
        P(),
        P(),
        P(),
        P(),
        P(),
        P(),
        P(),
    )
    return jax.shard_map(
        any_size,
        mesh=mesh,
        in_specs=placed,
        out_specs=(
            P("rep", "wide", None, None),
            P("rep", "wide", None, None),
            P(),
            P(),
            P(None, "wide", None),
            P(),
            P(None, "wide", None),
            P(),
            P(None, "wide", None),
            P(),
            P(None, None, "wide"),
            P(),
        ),
        check_vma=False,
    )
```

```python
import functools
import math

import jax
import jax.numpy as jnp
import ml_dtypes
import numpy as np
from jax import lax
from jax.experimental import pallas as pl
from jax.experimental.pallas import tpu as pltpu
from jax.sharding import PartitionSpec as P

D = 512
NB = 8
BS = 64
KW = 32
KH = 32
H = 64
W = 64
LAYERS = 2


EPSILON = 1e-05
THRESHOLD = 0.1
HIGHEST = lax.Precision.HIGHEST


def dft_tables():
    col_index = jnp.arange(W, dtype=jnp.int32)
    col_freq = jnp.arange(KW, dtype=jnp.int32)
    col_phase = (col_index[:, None] * col_freq[None, :] % W).astype(jnp.float32) * (
        2.0 * math.pi / W
    )
    col_scale = 1.0 / math.sqrt(W)
    forward_cols = jnp.stack([jnp.cos(col_phase), -jnp.sin(col_phase)], axis=1) * col_scale
    doubling = jnp.where(col_freq == 0, 1.0, 2.0).astype(jnp.float32)
    inverse_cols = (
        jnp.stack(
            [jnp.cos(col_phase).T * doubling[:, None], -jnp.sin(col_phase).T * doubling[:, None]],
            axis=0,
        )
        * col_scale
    )
    row_index = jnp.arange(H, dtype=jnp.int32)
    mode_index = jnp.arange(KH, dtype=jnp.int32)
    row_freq = jnp.where(mode_index < KH // 2, mode_index, H - KH + mode_index)
    row_phase = (row_freq[:, None] * row_index[None, :] % H).astype(jnp.float32) * (
        2.0 * math.pi / H
    )
    cosine = jnp.cos(row_phase) / math.sqrt(H)
    sine = jnp.sin(row_phase) / math.sqrt(H)
    forward_rows = jnp.stack([jnp.stack([cosine, sine], -1), jnp.stack([-sine, cosine], -1)], 1)
    inverse_rows = jnp.stack(
        [jnp.stack([cosine.T, -sine.T], -1), jnp.stack([sine.T, cosine.T], -1)], 1
    )
    return (forward_cols, inverse_cols, forward_rows, inverse_rows)


def layer_norm(values, gain_row, shift_row):
    center = values - jnp.mean(values, axis=-1, keepdims=True)
    spread = jnp.mean(center * center, axis=-1, keepdims=True)
    return center * lax.rsqrt(spread + EPSILON) * gain_row + shift_row


def gelu_tanh(values):
    return jax.nn.gelu(values, approximate=True)


def shrink(values):
    return values - THRESHOLD * jnp.tanh(values / THRESHOLD)


def block_matrix(weights, onehot_low):
    picked = jnp.einsum(
        "ac,cbd->abd",
        onehot_low,
        weights.reshape(NB, BS, 2 * BS),
        preferred_element_type=jnp.float32,
    ).astype(jnp.bfloat16)
    real_part = picked[:, :, :BS]
    imag_part = picked[:, :, BS:]
    upper = jnp.concatenate([real_part, imag_part], -1)
    lower = jnp.concatenate([-imag_part, real_part], -1)
    return jnp.concatenate([upper, lower], 1)


def mode_forward(arriving, forward_rows, mixing):
    first_big, first_bias, second_big, second_bias = mixing
    item_count, pair_count = (arriving.shape[0], arriving.shape[1])
    halves = arriving.reshape(item_count, pair_count, H, 2, BS)
    mode_data = jnp.einsum(
        "jphq,iahqb->iajpb", forward_rows, halves, preferred_element_type=jnp.float32
    )
    mode_data = mode_data.reshape(item_count, pair_count, KH, 2 * BS).astype(jnp.bfloat16)
    first_pre = (
        jnp.einsum("iakc,acd->iakd", mode_data, first_big, preferred_element_type=jnp.float32)
        + first_bias[None, :, None, :]
    )
    active = gelu_tanh(first_pre).astype(jnp.bfloat16)
    second = (
        jnp.einsum("iakc,acd->iakd", active, second_big, preferred_element_type=jnp.float32)
        + second_bias[None, :, None, :]
    )
    return (mode_data, first_pre, active, second)


def mode_inverse(second, inverse_rows):
    item_count, pair_count = (second.shape[0], second.shape[1])
    shrunk = shrink(second).astype(jnp.bfloat16).reshape(item_count, pair_count, KH, 2, BS)
    rows_out = jnp.einsum(
        "hpjq,iajqb->iahpb", inverse_rows, shrunk, preferred_element_type=jnp.float32
    )
    return rows_out.reshape(item_count, pair_count, H, 2 * BS).astype(jnp.bfloat16)


def mode_backward(first_pre, second, arrived, forward_rows, inverse_rows, mixing):
    first_big, first_bias, second_big, second_bias = mixing
    item_count, pair_count = (arrived.shape[0], arrived.shape[1])
    halves = arrived.reshape(item_count, pair_count, H, 2, BS)
    d_shrunk = jnp.einsum(
        "hpjq,iahpb->iajqb", inverse_rows, halves, preferred_element_type=jnp.float32
    )
    d_shrunk = d_shrunk.reshape(item_count, pair_count, KH, 2 * BS)
    unused, shrink_pull = jax.vjp(shrink, second)
    d_second = shrink_pull(d_shrunk)[0].astype(jnp.bfloat16)
    d_active = jnp.einsum(
        "iakd,acd->iakc", d_second, second_big, preferred_element_type=jnp.float32
    )
    unused, gelu_pull = jax.vjp(gelu_tanh, first_pre)
    d_first = gelu_pull(d_active)[0].astype(jnp.bfloat16)
    d_modes = jnp.einsum(
        "iakd,acd->iakc", d_first, first_big, preferred_element_type=jnp.float32
    ).astype(jnp.bfloat16)
    d_halves = d_modes.reshape(item_count, pair_count, KH, 2, BS)
    d_rows = jnp.einsum(
        "jphq,iajpb->iahqb", forward_rows, d_halves, preferred_element_type=jnp.float32
    )
    return (
        d_rows.reshape(item_count, pair_count, H, 2 * BS).astype(jnp.bfloat16),
        d_first,
        d_second,
    )


def block_grads(inputs, grads, onehot_full):
    product = jnp.einsum("iakc,iakd->acd", inputs, grads, preferred_element_type=jnp.float32)
    real_grad = product[:, :BS, :BS] + product[:, BS:, BS:]
    imag_grad = product[:, :BS, BS:] - product[:, BS:, :BS]
    pair_grad = jnp.concatenate([real_grad, imag_grad], -1)
    weight_grad = jnp.einsum("ac,abd->cbd", onehot_full, pair_grad, precision=HIGHEST).reshape(
        D, 2 * BS
    )
    bias_terms = jnp.sum(grads.astype(jnp.float32), axis=(0, 2))
    bias_grad = jnp.dot(onehot_full.T, bias_terms, precision=HIGHEST)
    return (weight_grad, bias_grad)


def body(
    tokens,
    cotangent,
    norm_gain,
    norm_shift,
    mix_in,
    mix_in_bias,
    mix_out,
    mix_out_bias,
    w_in,
    b_in,
    w_out,
    b_out,
):
    forward_cols, inverse_cols, forward_rows, inverse_rows = [
        table_item.astype(jnp.bfloat16) for table_item in dft_tables()
    ]
    devices = lax.axis_size("wide")
    per_device = NB * KW // devices
    global_pair = lax.axis_index("wide") * per_device + jnp.arange(per_device, dtype=jnp.int32)
    onehot_full = (global_pair[:, None] // KW == jnp.arange(NB, dtype=jnp.int32)[None, :]).astype(
        jnp.float32
    )
    onehot_low = onehot_full.astype(jnp.bfloat16)
    item_count, rows_dev = (tokens.shape[0], tokens.shape[1])
    current = tokens.astype(jnp.float32)
    stored = []
    for depth_index in range(LAYERS):
        mixing = (
            block_matrix(mix_in[depth_index], onehot_low),
            jnp.dot(onehot_full, mix_in_bias[depth_index], precision=HIGHEST),
            block_matrix(mix_out[depth_index], onehot_low),
            jnp.dot(onehot_full, mix_out_bias[depth_index], precision=HIGHEST),
        )
        normed = layer_norm(current, norm_gain[depth_index, 0], norm_shift[depth_index, 0])
        spectra = jnp.einsum(
            "irwcb,wpk->ickrpb",
            normed.astype(jnp.bfloat16).reshape(item_count, rows_dev, W, NB, BS),
            forward_cols,
            preferred_element_type=jnp.float32,
        )
        spectra = spectra.reshape(item_count, NB * KW, rows_dev, 2 * BS).astype(jnp.bfloat16)
        forward_mode_data, first_pre, forward_active, second = mode_forward(
            lax.all_to_all(spectra, "wide", split_axis=1, concat_axis=2, tiled=True),
            forward_rows,
            mixing,
        )
        returning = lax.all_to_all(
            mode_inverse(second, inverse_rows), "wide", split_axis=2, concat_axis=1, tiled=True
        )
        returned = (returning,)
        back_rows = returned[0].reshape(item_count, NB, KW, rows_dev, 2, BS)
        filtered = jnp.einsum(
            "pkw,ickrpb->irwcb", inverse_cols, back_rows, preferred_element_type=jnp.float32
        )
        middle = current + filtered.reshape(item_count, rows_dev, W, D) + normed
        lowered = layer_norm(middle, norm_gain[depth_index, 1], norm_shift[depth_index, 1]).astype(
            jnp.bfloat16
        )
        hidden_pre = (
            jnp.einsum(
                "irwd,df->irwf", lowered, w_in[depth_index], preferred_element_type=jnp.float32
            )
            + b_in[depth_index]
        )
        hidden_act = gelu_tanh(hidden_pre).astype(jnp.bfloat16)
        branch = (
            jnp.einsum(
                "irwf,fd->irwd", hidden_act, w_out[depth_index], preferred_element_type=jnp.float32
            )
            + b_out[depth_index]
        )
        stored.append(
            (
                current,
                normed,
                spectra,
                middle,
                lowered,
                hidden_pre,
                hidden_act,
                mixing,
                returned[1:],
            )
        )
        current = middle + branch
    upstream = cotangent
    collected = [None] * LAYERS
    for depth_index in reversed(range(LAYERS)):
        (
            layer_input,
            normed,
            spectra,
            middle,
            lowered,
            hidden_pre,
            hidden_act,
            mixing,
            kept_modes,
        ) = stored[depth_index]
        branch_grad = upstream.astype(jnp.bfloat16)
        w_out_part = jnp.einsum(
            "irwf,irwd->fd", hidden_act, branch_grad, preferred_element_type=jnp.float32
        )
        b_out_part = jnp.sum(branch_grad.astype(jnp.float32), axis=(0, 1, 2))
        act_grad = jnp.einsum(
            "irwd,fd->irwf", branch_grad, w_out[depth_index], preferred_element_type=jnp.float32
        )
        unused, gelu_pull = jax.vjp(gelu_tanh, hidden_pre)
        pre_grad = gelu_pull(act_grad)[0].astype(jnp.bfloat16)
        w_in_part = jnp.einsum(
            "irwd,irwf->df", lowered, pre_grad, preferred_element_type=jnp.float32
        )
        b_in_part = jnp.sum(pre_grad.astype(jnp.float32), axis=(0, 1, 2))
        low_grad = jnp.einsum(
            "irwf,df->irwd", pre_grad, w_in[depth_index], preferred_element_type=jnp.float32
        )
        unused, second_norm_pull = jax.vjp(
            layer_norm, middle, norm_gain[depth_index, 1], norm_shift[depth_index, 1]
        )
        mid_norm_grad, gain_second, shift_second = second_norm_pull(low_grad)
        mid_grad = upstream + mid_norm_grad
        filt_grad = mid_grad.astype(jnp.bfloat16).reshape(item_count, rows_dev, W, NB, BS)
        back_grad = jnp.einsum(
            "pkw,irwcb->ickrpb", inverse_cols, filt_grad, preferred_element_type=jnp.float32
        )
        back_grad = back_grad.reshape(item_count, NB * KW, rows_dev, 2 * BS).astype(jnp.bfloat16)
        backward_arriving = lax.all_to_all(spectra, "wide", split_axis=1, concat_axis=2, tiled=True)
        arrived = lax.all_to_all(back_grad, "wide", split_axis=1, concat_axis=2, tiled=True)
        backward_mode_data, backward_first_pre, backward_active, backward_second = mode_forward(
            backward_arriving, forward_rows, mixing
        )
        d_rows, d_first, d_second = mode_backward(
            backward_first_pre, backward_second, arrived, forward_rows, inverse_rows, mixing
        )
        sent_back = lax.all_to_all(d_rows, "wide", split_axis=2, concat_axis=1, tiled=True)
        col_grad, mode_data, active, d_first, d_second = (
            sent_back,
            backward_mode_data,
            backward_active,
            d_first,
            d_second,
        )
        mix_in_part, mix_in_bias_part = block_grads(mode_data, d_first, onehot_full)
        mix_out_part, mix_out_bias_part = block_grads(active, d_second, onehot_full)
        col_grad = col_grad.reshape(item_count, NB, KW, rows_dev, 2, BS)
        normed_grad = jnp.einsum(
            "wpk,ickrpb->irwcb", forward_cols, col_grad, preferred_element_type=jnp.float32
        )
        normed_grad = normed_grad.reshape(item_count, rows_dev, W, D) + mid_grad
        unused, first_norm_pull = jax.vjp(
            layer_norm, layer_input, norm_gain[depth_index, 0], norm_shift[depth_index, 0]
        )
        input_part, gain_first, shift_first = first_norm_pull(normed_grad)
        upstream = mid_grad + input_part
        collected[depth_index] = (
            jnp.stack([gain_first, gain_second]),
            jnp.stack([shift_first, shift_second]),
            mix_in_part,
            mix_in_bias_part,
            mix_out_part,
            mix_out_bias_part,
            w_in_part,
            b_in_part,
            w_out_part,
            b_out_part,
        )
    stacked = [
        jnp.stack([collected[depth_index][slot] for depth_index in range(LAYERS)])
        for slot in range(10)
    ]
    small_grads = lax.psum(
        (stacked[0], stacked[1], stacked[3], stacked[5], stacked[7], stacked[9]), ("wide", "rep")
    )
    large_grads = (stacked[2], stacked[4], stacked[6], stacked[8])
    pieces = (
        lax.psum_scatter(large_grads[0], "wide", scatter_dimension=1, tiled=True),
        lax.psum_scatter(large_grads[1], "wide", scatter_dimension=1, tiled=True),
        lax.psum_scatter(large_grads[2], "wide", scatter_dimension=1, tiled=True),
        lax.psum_scatter(large_grads[3], "wide", scatter_dimension=2, tiled=True),
    )
    pieces = (
        lax.psum(pieces[0].astype(jnp.bfloat16), "rep").astype(jnp.float32),
        lax.psum(pieces[1].astype(jnp.bfloat16), "rep").astype(jnp.float32),
        lax.psum(pieces[2].astype(jnp.bfloat16), "rep").astype(jnp.float32),
        lax.psum(pieces[3].astype(jnp.bfloat16), "rep").astype(jnp.float32),
    )
    return (
        current,
        upstream,
        small_grads[0],
        small_grads[1],
        pieces[0],
        small_grads[2],
        pieces[1],
        small_grads[3],
        pieces[2],
        small_grads[4],
        pieces[3],
        small_grads[5],
    )


BF = jnp.bfloat16
F32 = jnp.float32
FF = 2048
GROUPS = 4
GELU_A = math.sqrt(2.0 / math.pi)
GELU_B = GELU_A * 0.044715
HB = 16
KB = 16
TT = 512
FC = 1024
VMEM = 58 * 1024 * 1024


def plain_tables():
    def low(table):
        return table.astype(np.float32).astype(ml_dtypes.bfloat16).astype(np.float64)

    index = np.arange(64)
    col_phase = 2.0 * np.pi * ((index[:, None] * np.arange(KW)[None, :]) % W) / W
    forward_cols = np.stack([np.cos(col_phase), -np.sin(col_phase)], axis=1) / math.sqrt(W)
    doubling = np.where(np.arange(KW) == 0, 1.0, 2.0)[:, None]
    inverse_cols = (
        np.stack([np.cos(col_phase).T * doubling, -np.sin(col_phase).T * doubling], axis=0)
        / math.sqrt(W)
    )
    modes = np.arange(KH)
    row_freq = np.where(modes < KH // 2, modes, H - KH + modes)
    row_phase = 2.0 * np.pi * ((row_freq[:, None] * index[None, :]) % H) / H
    cosine = np.cos(row_phase) / math.sqrt(H)
    sine = np.sin(row_phase) / math.sqrt(H)
    forward_rows = np.stack([np.stack([cosine, sine], -1), np.stack([-sine, cosine], -1)], 1)
    inverse_rows = np.stack(
        [np.stack([cosine.T, -sine.T], -1), np.stack([sine.T, cosine.T], -1)], 1
    )
    return [low(table) for table in (forward_cols, inverse_cols, forward_rows, inverse_rows)]


def matrix_tables():
    forward_cols, inverse_cols, forward_rows, inverse_rows = plain_tables()
    eye = np.eye(4)
    into = np.einsum("wpk,gh->kpghw", forward_cols, eye).reshape(256, 256)
    outof = np.einsum("pkw,gh->gwkph", inverse_cols, eye).reshape(256, 256)
    pair = np.eye(2)
    forward_rows = forward_rows.reshape(KH, 2, H // 4, 4, 2)
    inverse_rows = inverse_rows.reshape(H // 4, 4, 2, KH, 2)
    rows_in = np.einsum("jphsq,ab->apjbhqs", forward_rows, pair).reshape(128, 256)
    rows_out = np.einsum("hspjq,ab->ahpsbqj", inverse_rows, pair).reshape(256, 128)
    return [
        jnp.asarray(np.ascontiguousarray(table).astype(ml_dtypes.bfloat16))
        for table in (into, outof, rows_in, rows_out, outof.T, into.T, rows_out.T, rows_in.T)
    ]


def big_matrices(weight):
    four = weight.reshape(GROUPS, 2, BS, 2, BS)
    eye = jnp.eye(2, dtype=weight.dtype)
    real = (four[:, :, :, 0][:, :, :, None, :] * eye[None, :, None, :, None]).reshape(
        GROUPS, 128, 128
    )
    imag = (four[:, :, :, 1][:, :, :, None, :] * eye[None, :, None, :, None]).reshape(
        GROUPS, 128, 128
    )
    upper = jnp.concatenate([real, imag], -1)
    lower = jnp.concatenate([-imag, real], -1)
    return jnp.concatenate([upper, lower], 1)


def big_bias(bias):
    return bias.reshape(GROUPS, 2, 2, BS).transpose(0, 2, 1, 3).reshape(GROUPS, 1, 256)


def small_bias(line):
    parts = line.reshape(-1, GROUPS, 2, 2, BS).transpose(0, 1, 3, 2, 4)
    return parts.reshape(-1, NB, 2 * BS)


def mm(left, right):
    return jnp.dot(left, right, preferred_element_type=F32)


def mm_t(left, right):
    return lax.dot_general(left, right, (((1,), (1,)), ((), ())), preferred_element_type=F32)


def normalize(values):
    center = values - jnp.mean(values, axis=-1, keepdims=True)
    spread = jnp.mean(center * center, axis=-1, keepdims=True)
    scale = lax.rsqrt(spread + EPSILON)
    return center * scale, scale


def normalize_back(grad, unit, scale, gain_row):
    inner = grad * gain_row
    return scale * (
        inner
        - jnp.mean(inner, axis=-1, keepdims=True)
        - unit * jnp.mean(inner * unit, axis=-1, keepdims=True)
    )


def folded(values):
    return jnp.sum(values.reshape(values.shape[0] // 8, 8, values.shape[1]), axis=0)


def gelu_of(v):
    return 0.5 * v * (1.0 + jnp.tanh(v * (GELU_A + GELU_B * (v * v))))


def gelu_and_slope(v):
    square = v * v
    bend = jnp.tanh(v * (GELU_A + GELU_B * square))
    half = 0.5 * (1.0 + bend)
    slope = half + 0.5 * v * (1.0 - bend * bend) * (GELU_A + 3.0 * GELU_B * square)
    return v * half, slope


def cols_in(table, rows, store, block):
    parts = [
        mm(table, rows[at * 256 : at * 256 + 256]).reshape(KW, 8, D) for at in range(HB // 4)
    ]
    store[:, pl.ds(pl.multiple_of(block * 2 * HB, 2 * HB), 2 * HB), :] = jnp.concatenate(
        parts, axis=1
    ).astype(BF)


def cols_out(table, store, block):
    part = store[:, pl.ds(pl.multiple_of(block * 2 * HB, 2 * HB), 2 * HB), :].astype(F32)
    return jnp.concatenate(
        [
            mm(table, part[:, at * 8 : at * 8 + 8].reshape(256, D).astype(BF))
            for at in range(HB // 4)
        ],
        axis=0,
    )


def lanes_of(rows, group):
    lanes = slice(group * 128, group * 128 + 128)
    return jnp.concatenate(
        [rows[:, :32, lanes].reshape(KB * 32, 128), rows[:, 32:, lanes].reshape(KB * 32, 128)],
        axis=1,
    )


def put_lanes(store, group, values):
    lanes = slice(group * 128, group * 128 + 128)
    store[:, :32, lanes] = values[:, :128].reshape(KB, 32, 128)
    store[:, 32:, lanes] = values[:, 128:].reshape(KB, 32, 128)


def spectral_forward_kernel(
    x_ref, gain, shift, into, outof, rows_in, rows_out, w1, b1, w2, b2, mid_ref, spec_ref,
    cols, mixed, held,
):
    step = pl.program_id(0)
    n_rows, n_freq = H // HB, KW // KB

    @pl.when(step < n_rows)
    def _():
        x = lines_of(x_ref)
        held[step] = x
        unit, _ = normalize(x.astype(F32))
        normed = unit * gain[...] + shift[...]
        cols_in(into[...], normed.astype(BF), cols, step)

    @pl.when((step >= n_rows) & (step < n_rows + n_freq))
    def _():
        first_plane = (step - n_rows) * KB
        for two in range(KB // 2):
            planes = cols[pl.ds(first_plane + 2 * two, 2)]
            spec_ref[2 * two : 2 * two + 2] = (
                mm(rows_in[...], planes.reshape(256, D)).astype(BF).reshape(2, 64, D)
            )
        modes = spec_ref[...]
        for group in range(GROUPS):
            first = mm(lanes_of(modes, group), w1[group]) + b1[group]
            second = mm(gelu_of(first).astype(BF), w2[group]) + b2[group]
            shrunk = second - THRESHOLD * jnp.tanh(second * (1.0 / THRESHOLD))
            put_lanes(mixed, group, shrunk.astype(BF))
        for two in range(KB // 2):
            planes = mixed[2 * two : 2 * two + 2].reshape(128, D)
            cols[pl.ds(first_plane + 2 * two, 2)] = (
                mm(rows_out[...], planes).astype(BF).reshape(2, 128, D)
            )

    @pl.when(step >= n_rows + n_freq)
    def _():
        block = step - n_rows - n_freq
        x = held[block].astype(F32)
        unit, _ = normalize(x)
        normed = unit * gain[...] + shift[...]
        filtered = cols_out(outof[...], cols, block)
        mid_ref[...] = (x + filtered + normed).astype(mid_ref.dtype)


def compact(big):
    low_lanes = lax.broadcasted_iota(jnp.int32, (BS, 128), 1) < BS
    parts = []
    for c in range(2):
        real_rows, imag_rows = slice(c * BS, c * BS + BS), slice(128 + c * BS, 128 + c * BS + BS)
        real = big[real_rows, :128] + big[imag_rows, 128:]
        imag = big[real_rows, 128:] - big[imag_rows, :128]
        if c == 0:
            parts.append(jnp.where(low_lanes, real, pltpu.roll(imag, BS, 1)))
        else:
            parts.append(jnp.where(low_lanes, pltpu.roll(real, BS, 1), imag))
    return jnp.concatenate(parts, axis=0)


def spectral_backward_kernel(with_start, *refs):
    (
        x_ref, grad_ref, spec_ref, gain, outof_t, into_t, rows_out_t, rows_in_t,
        w1, b1, w2, b2, w1_t, w2_t,
    ), refs = refs[:14], refs[14:]
    starts, refs = refs[:2] if with_start else (), refs[2:] if with_start else refs
    new_ref, blocks, lines, dw1, dw2, cols, mixed, kept, held = refs
    step = pl.program_id(0)
    n_rows, n_freq = H // HB, KW // KB

    @pl.when(step == 0)
    def _():
        lines[...] = starts[1][...] if with_start else jnp.zeros_like(lines)
        for ref in (dw1, dw2):
            ref[...] = jnp.zeros_like(ref)

    @pl.when(step < n_rows)
    def _():
        grad = grad_ref[...]
        held[step] = grad
        cols_in(outof_t[...], grad, cols, step)

    @pl.when((step >= n_rows) & (step < n_rows + n_freq))
    def _():
        first_plane = (step - n_rows) * KB
        for two in range(KB // 2):
            planes = cols[pl.ds(first_plane + 2 * two, 2)]
            kept[2 * two : 2 * two + 2] = mm(rows_out_t[...], planes.reshape(256, D)).reshape(
                2, 64, D
            )
        modes = spec_ref[...]
        grads = kept[...]
        for group in range(GROUPS):
            mode = lanes_of(modes, group)
            first = mm(mode, w1[group]) + b1[group]
            active, slope = gelu_and_slope(first)
            active = active.astype(BF)
            second = mm(active, w2[group]) + b2[group]
            bend = jnp.tanh(second * (1.0 / THRESHOLD))
            d_second = bend * bend * lanes_of(grads, group)
            at = slice(group * 256, group * 256 + 256)
            lines[:, 1024 + group * 256 : 1280 + group * 256] += folded(d_second)
            d_second = d_second.astype(BF)
            dw2[group] += mm(active.T, d_second)
            d_first = slope * mm(d_second, w2_t[group])
            lines[:, at] += folded(d_first)
            d_first = d_first.astype(BF)
            dw1[group] += mm(mode.T, d_first)
            put_lanes(mixed, group, mm(d_first, w1_t[group]).astype(BF))
        for two in range(KB // 2):
            planes = mixed[2 * two : 2 * two + 2].reshape(128, D)
            cols[pl.ds(first_plane + 2 * two, 2)] = (
                mm(rows_in_t[...], planes).astype(BF).reshape(2, 128, D)
            )

    @pl.when(step == n_rows + n_freq)
    def _():
        for group in range(GROUPS):
            at = slice(group * 128, group * 128 + 128)
            for slot, ref in enumerate((dw1, dw2)):
                lanes = slice(slot * 128, slot * 128 + 128)
                block = compact(ref[group])
                blocks[at, lanes] = block + starts[0][at, lanes] if with_start else block

    @pl.when(step >= n_rows + n_freq)
    def _():
        block = step - n_rows - n_freq
        unit, scale = normalize(lines_of(x_ref).astype(F32))
        mid_grad = held[block].astype(F32)
        grad = cols_out(into_t[...], cols, block) + mid_grad
        lines[:, 2048:2560] += folded(grad * unit)
        lines[:, 2560:3072] += folded(grad)
        new = mid_grad + normalize_back(grad, unit, scale, gain[...])
        new_ref[...] = new.astype(new_ref.dtype)


def feed_forward_kernel(mid_ref, gain, shift, w_in, b_in, w_out, b_out, *refs):
    out_ref, pre_ref = refs[-2:]
    middle = mid_ref[...].astype(F32)
    unit, _ = normalize(middle)
    lowered = (unit * gain[...] + shift[...]).astype(BF)
    total = middle + b_out[...]
    for part in range(FF // FC):
        at = slice(part * FC, part * FC + FC)
        pre = mm(lowered, w_in[:, at]) + b_in[:, at]
        pre = pre.astype(BF)
        pre_ref[:, at] = pre
        total += mm(gelu_of(pre), w_out[at, :])
    out_ref[...] = total.astype(out_ref.dtype)


def feed_backward_kernel(with_start, *refs):
    (g_ref, mid_ref, pre_ref, gain, shift, w_out, w_in), refs = refs[:7], refs[7:]
    if with_start:
        (start_far, start_lines, side, mid_grad_ref, kept, sent, lines, dw, start, arrival) = refs
        copy = pltpu.make_async_copy(start_far, start, arrival)
    else:
        mid_grad_ref, dw, lines = refs
    step = pl.program_id(0)

    @pl.when(step == 0)
    def _():
        lines[...] = start_lines[...] if with_start else jnp.zeros_like(lines)
        dw[...] = jnp.zeros_like(dw)
        if with_start:
            copy.start()

    upstream = lines_of(g_ref)
    unit, scale = normalize(mid_ref[...].astype(F32))
    lowered = (unit * gain[...] + shift[...]).astype(BF)
    lines[:, FF : FF + D] += folded(upstream.astype(F32))
    upstream_t = upstream.T
    lowered_t = lowered.T
    low_grad = jnp.zeros((TT, D), F32)
    for part in range(FF // FC):
        at = slice(part * FC, part * FC + FC)
        active, slope = gelu_and_slope(pre_ref[:, at])
        dw[:, FF + part * FC : FF + part * FC + FC] += mm(upstream_t, active)
        pre_grad = slope * mm_t(upstream, w_out[at, :]).astype(BF)
        lines[:, at] += folded(pre_grad.astype(F32))
        dw[:, at] += mm(lowered_t, pre_grad)
        low_grad += mm_t(pre_grad, w_in[:, at])
    lines[:, FF + D : FF + 2 * D] += folded(low_grad * unit)
    lines[:, FF + 2 * D : FF + 3 * D] += folded(low_grad)
    new = upstream.astype(F32) + normalize_back(low_grad, unit, scale, gain[...])
    mid_grad_ref[...] = new.astype(mid_grad_ref.dtype)
    if with_start:

        @pl.when(step == H * W // TT - 1)
        def _():
            copy.wait()
            for ref, half in ((kept, side[0]), (sent, 1 - side[0])):
                at = pl.ds(pl.multiple_of(half * FF, FF), FF)
                ref[...] = (dw[:, at] + start[:, at]).astype(BF)


def whole(array):
    zeros = (0,) * array.ndim
    return pl.BlockSpec(array.shape, lambda *_: zeros, pipeline_mode=pl.Buffered(1))


def of_layer(array, layer):
    at = (layer,) + (0,) * (array.ndim - 1)
    return pl.BlockSpec((None, *array.shape[1:]), lambda *_: at, pipeline_mode=pl.Buffered(1))


def rows_spec(rows, block_of, array=None, kind=None):
    if kind is None:
        return pl.BlockSpec((rows * W, D), lambda s: (block_of(s), 0))
    own = array.shape[2]
    return pl.BlockSpec((rows * W // own, None, own, D), lambda s: (block_of(s), kind, 0, 0))


def lines_of(ref):
    return ref[...].reshape(-1, D)


PARAMS = pltpu.CompilerParams(dimension_semantics=("arbitrary",), vmem_limit_bytes=VMEM)


def cost(microseconds):
    return pl.CostEstimate(
        flops=microseconds * 150_000_000, bytes_accessed=1_000_000, transcendentals=0
    )


N_ROWS, N_FREQ = H // HB, KW // KB
SPECTRAL_STEPS = 2 * N_ROWS + N_FREQ


def first_end(step):
    return jnp.minimum(step, N_ROWS - 1)


def last_end(step):
    return jnp.maximum(step - N_ROWS - N_FREQ, 0)


def middle_part(step):
    return jnp.clip(step - N_ROWS, 0, N_FREQ - 1)


def spectral_forward(x, kind, gain, shift, tables, mix):
    small = (gain, shift, *tables[:4], *mix[:4])
    return pl.pallas_call(
        spectral_forward_kernel,
        grid=(SPECTRAL_STEPS,),
        in_specs=[rows_spec(HB, first_end, x, kind)] + [whole(array) for array in small],
        out_specs=[
            rows_spec(HB, last_end),
            pl.BlockSpec((KB, 64, D), lambda s: (middle_part(s), 0, 0)),
        ],
        out_shape=[
            jax.ShapeDtypeStruct((H * W, D), BF),
            jax.ShapeDtypeStruct((KW, 64, D), BF),
        ],
        scratch_shapes=[
            pltpu.VMEM((KW, 128, D), BF),
            pltpu.VMEM((KB, 64, D), BF),
            pltpu.VMEM((N_ROWS, HB * W, D), BF),
        ],
        compiler_params=PARAMS,
        cost_estimate=cost(16),
        name="spectral_forward",
    )(x, *small)


def spectral_backward(x, kind, grad, spec, gain, tables, mix, start):
    small = (gain, *tables[4:], *mix, *start)
    sums = [(D, 256), (8, 3072)]
    return pl.pallas_call(
        functools.partial(spectral_backward_kernel, len(start) > 0),
        grid=(SPECTRAL_STEPS,),
        in_specs=[
            rows_spec(HB, last_end, x, kind),
            rows_spec(HB, first_end),
            pl.BlockSpec((KB, 64, D), lambda s: (middle_part(s), 0, 0)),
        ]
        + [whole(array) for array in small],
        out_specs=[rows_spec(HB, last_end)] + [pl.BlockSpec(dims, lambda s: (0, 0)) for dims in sums],
        out_shape=[jax.ShapeDtypeStruct((H * W, D), BF)]
        + [jax.ShapeDtypeStruct(dims, F32) for dims in sums],
        scratch_shapes=[
            pltpu.VMEM((GROUPS, 256, 256), F32),
            pltpu.VMEM((GROUPS, 256, 256), F32),
            pltpu.VMEM((KW, 128, D), BF),
            pltpu.VMEM((KB, 64, D), BF),
            pltpu.VMEM((KB, 64, D), F32),
            pltpu.VMEM((N_ROWS, HB * W, D), BF),
        ],
        compiler_params=PARAMS,
        cost_estimate=cost(24),
        name="spectral_backward",
    )(x, grad, spec, *small)


def feed_forward(middle, layer, gain, shift, w_in, b_in, w_out, b_out, abroad=None, onto=None):
    rows = rows_spec(TT // W, lambda s: s)
    shape = jax.ShapeDtypeStruct((H * W, D), BF)
    if abroad is not None:
        receivers, chunks, own, chunk = abroad
        shape = jax.ShapeDtypeStruct((receivers, chunks, own * W, D), BF)
        rows = pl.BlockSpec((None, None, TT, D), lambda s: (s, chunk, 0, 0))
    more = [] if onto is None else [onto]
    return pl.pallas_call(
        feed_forward_kernel,
        grid=(H * W // TT,),
        in_specs=[
            rows_spec(TT // W, lambda s: s),
            whole(gain),
            whole(shift),
            of_layer(w_in, layer),
            whole(b_in),
            of_layer(w_out, layer),
            whole(b_out),
        ]
        + [pl.BlockSpec(memory_space=pl.ANY) for _ in more],
        out_specs=[rows, pl.BlockSpec((TT, FF), lambda s: (s, 0))],
        out_shape=[shape, jax.ShapeDtypeStruct((H * W, FF), BF)],
        input_output_aliases={7: 0} if more else {},
        compiler_params=PARAMS,
        cost_estimate=cost(24),
        name="feed_forward",
    )(middle, gain, shift, w_in, b_in, w_out, b_out, *more)


def feed_backward(g, kind, middle, pre, layer, gain, shift, w_out, w_in, start, side):
    matrices, lines = (D, 2 * FF), (8, FF + 3 * D)
    halves = [(D, FF), (D, FF)]
    sums = [(dims, BF) for dims in halves] if start else [(matrices, F32)]
    sums.append((lines, F32))
    return pl.pallas_call(
        functools.partial(feed_backward_kernel, len(start) > 0),
        grid=(H * W // TT,),
        in_specs=[
            rows_spec(TT // W, lambda s: s, g, kind),
            rows_spec(TT // W, lambda s: s),
            pl.BlockSpec((TT, FF), lambda s: (s, 0)),
            whole(gain),
            whole(shift),
            of_layer(w_out, layer),
            of_layer(w_in, layer),
        ]
        + (
            [
                pl.BlockSpec(memory_space=pl.ANY),
                whole(start[1]),
                pl.BlockSpec(memory_space=pltpu.SMEM),
            ]
            if start
            else []
        ),
        out_specs=[rows_spec(TT // W, lambda s: s)]
        + [pl.BlockSpec(dims, lambda s: (0, 0)) for dims, _ in sums],
        out_shape=[jax.ShapeDtypeStruct((H * W, D), BF)]
        + [jax.ShapeDtypeStruct(dims, kind_of) for dims, kind_of in sums],
        scratch_shapes=[
            pltpu.VMEM(matrices, F32),
            pltpu.VMEM(matrices, F32),
            pltpu.SemaphoreType.DMA,
        ]
        if start
        else [],
        compiler_params=PARAMS,
        cost_estimate=cost(49),
        name="feed_backward",
    )(g, middle, pre, gain, shift, w_out, w_in, *start, *([side] if start else []))


def widen_kernel(part, *refs):
    refs[-1][...] = part[...].astype(F32)


def widened(part, chunk, chunks, onto):
    items, parts = part.shape[:2]
    block = (None, None, *part.shape[2:])
    more = [] if onto is None else [onto]
    return pl.pallas_call(
        widen_kernel,
        grid=(parts, items),
        in_specs=[pl.BlockSpec(block, lambda p, s: (s, p, 0, 0, 0))]
        + [pl.BlockSpec(memory_space=pl.ANY) for _ in more],
        out_specs=pl.BlockSpec(block, lambda p, s: (chunk + p, s, 0, 0, 0)),
        out_shape=jax.ShapeDtypeStruct((chunks, items, *part.shape[2:]), F32),
        input_output_aliases={1: 0} if more else {},
        compiler_params=pltpu.CompilerParams(
            dimension_semantics=("arbitrary", "arbitrary"), vmem_limit_bytes=VMEM
        ),
        cost_estimate=cost(0),
        name="widen",
    )(part, *more)


def exchange(array):
    return lax.all_to_all(array, "wide", split_axis=0, concat_axis=0, tiled=True)


def after(array, other):
    return lax.optimization_barrier((array, other))[0]


def swapped(array, axis_name, far):
    size = lax.axis_size(axis_name)
    return lax.ppermute(array, axis_name, [(i, i ^ far) for i in range(size)])


def share(array, index, size, axis):
    return lax.dynamic_slice_in_dim(array, index * size, size, axis)


def own_bit(axis_name, bit):
    return (lax.axis_index(axis_name) >> bit) & 1


def halves(array, side, axis):
    half = array.shape[axis] // 2
    return share(array, side, half, axis), share(array, 1 - side, half, axis)


def row_halves(array, bit, shard):
    blocks = array.reshape(-1, 2, shard, array.shape[1])
    return [half.reshape(-1, array.shape[1]) for half in halves(blocks, own_bit("wide", bit), 1)]


def traded(kept, sent, axis_name, bit, behind=()):
    arrived = swapped(sent.astype(BF), axis_name, 1 << bit)
    return after(kept, behind).astype(F32) + arrived.astype(F32)


def traded_with(kept, sent, extra, axis_name, bit, behind=()):
    extra = extra.astype(BF)
    message = jnp.concatenate([sent.astype(BF), extra.reshape(-1, sent.shape[1])], axis=0)
    arrived = swapped(message, axis_name, 1 << bit).astype(F32)
    rows = sent.shape[0]
    return (
        after(kept, behind).astype(F32) + arrived[:rows],
        extra.astype(F32) + arrived[rows:].reshape(extra.shape),
    )


def side_by_side(own, other, bit):
    first = own_bit("rep", bit) == 0
    return jnp.concatenate(
        [jnp.where(first, own, other), jnp.where(first, other, own)], axis=1
    )


def whole_items(
    tokens, cotangent, norm_gain, norm_shift, mix_in, mix_in_bias, mix_out, mix_out_bias,
    w_in, b_in, w_out, b_out,
):
    wide = lax.axis_size("wide")
    chunks = tokens.shape[0] // wide
    abroad = (wide, *tokens.shape[1:])

    def rows_by_layer(array):
        return [array[layer].reshape(-1, 1, array.shape[-1]) for layer in range(LAYERS)]

    lines = [
        [[line for line in group] for group in rows_by_layer(array)]
        for array in (norm_gain, norm_shift, b_in, b_out)
    ]

    tables = matrix_tables()
    mixes = []
    for layer in range(LAYERS):
        first_mats, second_mats = big_matrices(mix_in[layer]), big_matrices(mix_out[layer])
        mixes.append(
            (
                first_mats,
                big_bias(mix_in_bias[layer]),
                second_mats,
                big_bias(mix_out_bias[layer]),
                first_mats.transpose(0, 2, 1),
                second_mats.transpose(0, 2, 1),
            )
        )

    stored = {}
    feed_sums = [()] * LAYERS
    mix_sums = [()] * LAYERS
    tie = lax.optimization_barrier

    def rows_of(array, chunk):
        return array[chunk * wide : chunk * wide + wide].astype(BF)

    def forward(chunk, current, kind, onto):
        for layer in range(LAYERS):
            middle, spec = spectral_forward(
                current, kind, gains[layer][0], shifts[layer][0], tables, mixes[layer]
            )
            last = layer == LAYERS - 1
            following, pre = feed_forward(
                middle, layer, gains[layer][1], shifts[layer][1], w_in,
                in_biases[layer][0], w_out, out_biases[layer][0],
                abroad=(wide, chunks, tokens.shape[1], chunk) if last else None,
                onto=onto if last else None,
            )
            stored[layer, chunk] = (current, kind, middle, spec, pre)
            current, kind = following, None
        return current

    def backward_feed(chunk, layer, grad, kind=None):
        _, _, middle, _, pre = stored[layer, chunk]
        mid_grad, *feed_sums[layer] = feed_backward(
            grad, kind, middle, pre, layer, gains[layer][1], shifts[layer][1], w_out, w_in,
            feed_sums[layer], side,
        )
        return mid_grad

    def backward_spectral(chunk, layer, mid_grad):
        layer_input, kind, _, spec, _ = stored[layer, chunk]
        grad, *mix_sums[layer] = spectral_backward(
            layer_input, kind, mid_grad, spec, gains[layer][0], tables, mixes[layer], mix_sums[layer]
        )
        return grad

    def backward(chunk, layer, grad):
        return backward_spectral(chunk, layer, backward_feed(chunk, layer, grad))

    def as_item(array):
        return array.reshape(H * W, D)

    def one_part(array):
        return array.reshape(wide, 1, *tokens.shape[1:])

    def both(first, second):
        return jnp.stack([first, second], axis=1).reshape(wide, 2, -1, D)

    sent, tokens_here, cotangent_here = tie((rows_of(tokens, 0), tokens, cotangent))
    arrived = exchange(sent)
    arrived, mixes, lines, sent, later = tie(
        (
            arrived,
            mixes,
            lines,
            rows_of(cotangent_here, 0),
            both(rows_of(tokens_here, 1), rows_of(cotangent_here, 1)),
        )
    )
    gains, shifts, in_biases, out_biases = lines
    upstream = exchange(sent)
    wide_at, rep_at = lax.axis_index("wide"), lax.axis_index("rep")
    side = (rep_at & 1).astype(jnp.int32).reshape(1)
    output = forward(0, as_item(arrived), None, None)

    upstream, output, later = tie((upstream, output, later))
    arrived = exchange(later)
    grad = backward(0, 1, as_item(upstream))
    grad = backward(0, 0, grad)

    grad, arrived, output = tie((grad, arrived, output))
    returned = exchange(grad.reshape(abroad))
    output = forward(1, arrived, 0, output)

    returned, output, arrived = tie((returned, output, arrived))
    delivered = exchange(output)
    mid_grad = backward_feed(1, 1, arrived, 1)
    shard = D // wide
    last_kept, last_sent = feed_sums[1][:2]
    grad = backward_spectral(1, 1, mid_grad)
    last_sum, grad = tie((traded(last_kept, last_sent, "rep", 0, grad), grad))
    mid_grad = backward_feed(1, 0, grad)
    kept, sent = halves(last_sum, own_bit("rep", 1), 1)
    last_sum, mid_grad, ready = tie(
        (traded(kept, sent, "rep", 1, mid_grad), mid_grad, feed_sums[0][:2])
    )
    first_sum = traded(*ready, "rep", 0)
    first_sum, mid_grad = tie((first_sum, mid_grad))
    grad = backward_spectral(1, 0, mid_grad)
    kept, sent = row_halves(last_sum, 0, shard)
    last_sum = traded(kept, sent, "wide", 0, grad)
    kept, sent = halves(first_sum, own_bit("rep", 1), 1)
    first_sum = traded(kept, sent, "rep", 1, grad)

    last_sum, first_sum, grad, feed_sums, mix_sums = tie(
        (last_sum, first_sum, grad, feed_sums, mix_sums)
    )
    kept, sent = row_halves(first_sum, 0, shard)
    first_sum = traded(kept, sent, "wide", 0)
    kept, sent = row_halves(last_sum, 1, shard)
    last_sum = traded(kept, sent, "wide", 1, first_sum)
    lines = jnp.stack(
        [
            jnp.concatenate([jnp.sum(sums[layer][-1], axis=0) for sums in (feed_sums, mix_sums)])
            for layer in range(LAYERS)
        ]
    )
    lines_size = lines.size
    kept, sent = (
        jnp.concatenate(each, axis=1)
        for each in zip(*[halves(sums[0], own_bit("rep", 0), 1) for sums in mix_sums])
    )
    width = sent.shape[1]
    lines = jnp.pad(lines.reshape(-1), (0, -lines_size % (16 * width)))
    blocks, lines = traded_with(kept, sent, lines, "rep", 0)
    delivered, grad, returned_first, first_sum, last_sum, blocks, lines = tie(
        (delivered, grad, returned, first_sum, last_sum, blocks, lines)
    )
    kept, sent = row_halves(first_sum, 1, shard)
    near = traded(kept, sent, "wide", 1)
    kept, sent = row_halves(near, 2, shard)
    first_sum = traded(kept, sent, "wide", 2)
    kept, sent = row_halves(last_sum, 2, shard)
    last_sum = traded(kept, sent, "wide", 2)
    for bit in (0, 1):
        kept, sent = row_halves(blocks, bit, shard)
        blocks, lines = traded_with(kept, sent, lines, "wide", bit, near if bit else ())
        if bit == 0:
            blocks, lines, delivered, returned_first = tie(
                (blocks, lines, delivered, returned_first)
            )
    returned = exchange(grad.reshape(abroad))
    kept, sent = row_halves(blocks, 2, shard)
    blocks, lines = traded_with(kept, sent, lines, "wide", 2)
    input_grad = widened(one_part(returned_first), 0, chunks, None)
    output = widened(
        delivered.reshape(wide, chunks, *tokens.shape[1:]), 0, chunks, None
    ).reshape(tokens.shape)
    columns = last_sum.shape[1]
    message = jnp.concatenate([first_sum, last_sum], axis=1).astype(BF)
    arrived = swapped(message, "rep", 2)
    first_sum, last_sum = (
        side_by_side(message[:, at : at + columns], arrived[:, at : at + columns], 1)
        for at in (0, columns)
    )
    message = jnp.concatenate([first_sum, last_sum], axis=1)
    arrived = swapped(message, "rep", 1)
    matrices = [
        side_by_side(message[:, at : at + 2 * columns], arrived[:, at : at + 2 * columns], 0).astype(
            F32
        )
        for at in (0, 2 * columns)
    ]
    w_in_grad = jnp.stack([matrix[:, :FF] for matrix in matrices])
    w_out_grad = jnp.stack([matrix[:, FF:].T for matrix in matrices])
    returned, output, input_grad, w_in_grad, w_out_grad, blocks, lines = tie(
        (returned, output, input_grad, w_in_grad, w_out_grad, blocks, lines)
    )
    mixed = jnp.concatenate([blocks, lines.reshape(shard, -1)], axis=1).astype(BF)
    arrived = swapped(mixed, "rep", 2)
    input_grad = widened(one_part(returned), 1, chunks, input_grad).reshape(tokens.shape)
    arrived, input_grad = tie((arrived, input_grad))
    mixed = mixed.astype(F32) + arrived.astype(F32)
    blocks, lines = mixed[:, :width].astype(BF), mixed[:, width:].reshape(-1)
    packed = lines[:lines_size].reshape(LAYERS, -1)
    arrived = swapped(blocks, "rep", 1)
    b_in_grad, b_out_grad, gain_two, shift_two, in_bias, out_bias, gain_one, shift_one = (
        jnp.split(packed, np.cumsum([FF, D, D, D, 1024, 1024, D]), axis=1)
    )
    gain_grad, shift_grad = (
        jnp.stack(pair, axis=1) for pair in ((gain_one, gain_two), (shift_one, shift_two))
    )
    in_bias_grad, out_bias_grad = small_bias(in_bias), small_bias(out_bias)
    arrived, gain_grad, shift_grad, in_bias_grad, out_bias_grad, b_in_grad, b_out_grad = tie(
        (arrived, gain_grad, shift_grad, in_bias_grad, out_bias_grad, b_in_grad, b_out_grad)
    )
    blocks = side_by_side(blocks, arrived, 0).astype(F32)
    mix_grads = blocks.reshape(shard, 2, LAYERS, 2 * BS).transpose(1, 2, 0, 3)

    return (
        output, input_grad, gain_grad, shift_grad, mix_grads[0], in_bias_grad,
        mix_grads[1], out_bias_grad, w_in_grad, b_in_grad, w_out_grad, b_out_grad,
    )


def any_size(tokens, *others):
    wide, rep = lax.axis_size("wide"), lax.axis_size("rep")
    if tokens.shape[0] == 2 * wide and tokens.shape[1] * W == TT and rep == 4 and wide == 8:
        return whole_items(tokens, *others)
    return body(tokens, *others)


def solution(mesh):
    placed = (
        P("rep", "wide", None, None),
        P("rep", "wide", None, None),
        P(),
        P(),
        P(),
        P(),
        P(),
        P(),
        P(),
        P(),
        P(),
        P(),
    )
    return jax.shard_map(
        any_size,
        mesh=mesh,
        in_specs=placed,
        out_specs=(
            P("rep", "wide", None, None),
            P("rep", "wide", None, None),
            P(),
            P(),
            P(None, "wide", None),
            P(),
            P(None, "wide", None),
            P(),
            P(None, "wide", None),
            P(),
            P(None, None, "wide"),
            P(),
        ),
        check_vma=False,
    )
```
